256 devices in a mesh: fsdp: 32 (over y, x, core), tp: 8 (over z).
Axes of the slice: x: 4, y: 4, z: 8, core: 2. Of those that a mesh axis runs over, the one named last changes fastest.
Arguments:
- momentum: bfloat16 [8192, 26624], P('fsdp', 'tp'), may hold values from -6 to 6
- gradient: bfloat16 [8192, 26624], P('fsdp', 'tp'), may hold values from -60 to 60
- weights: bfloat16 [8192, 26624], P('fsdp', 'tp'), may hold values from -6 to 6
- subspace: float32 [26624, 128], P('tp'), may hold values from -0.0390625 to 0.0390625
Outputs:
- new_momentum: bfloat16 [8192, 26624], P('fsdp', 'tp')
- new_weights: bfloat16 [8192, 26624], P('fsdp', 'tp')
- new_subspace: float32 [26624, 128], P('tp')
The draws below stay inside these ranges and needn't reach their ends.
All inputs are finite; a program needn't handle non-finite values.
Results may differ from the reference program's by a relative error of at most 0.012.
Values may be sent and summed in bfloat16 or wider, within the bound.
No kernel may reach another device: no remote copies, remote signals or barrier semaphores. Data moves between devices by JAX's collectives and lax.ppermute only.
A program may use at most 64 MiB of HBM per device.

```python
import math
import jax
import jax.numpy as jnp
from jax import lax

ROWS = 8192
COLS = 26624
RANK = 128


def draw_gradient(key, part):
    key = jax.random.fold_in(key, 7)
    key_rows, key_cols, key_base = jax.random.split(key, 3)
    row_scale = jnp.exp(jax.random.uniform(key_rows, (ROWS, 1), jnp.float32, 0.0, math.log(10.0) / 2))
    col_scale = jnp.exp(jax.random.uniform(key_cols, (1, COLS), jnp.float32, 0.0, math.log(10.0) / 2))
    base = jnp.clip(jax.random.normal(key_base, (ROWS, COLS), jnp.float32), -6.0, 6.0)
    return (0.5 * base * row_scale * col_scale).astype(jnp.bfloat16)


def level_of(stream_key, dims, pieces, smallest, top_value):
    loudness, own = 1.0, jax.random.fold_in(stream_key, 6)
    for axis_at, parts in pieces:
        heights = jnp.exp(jax.random.uniform(jax.random.fold_in(own, axis_at), (parts,), jnp.float32, smallest / len(pieces), top_value / len(pieces)))
        loudness = loudness * jnp.repeat(heights, dims[axis_at] // parts).reshape([-1 if axis == axis_at else 1 for axis in range(len(dims))])
    return loudness


def noise(rng, extent, deviation, most, shards=(), dtype=jnp.bfloat16):
    drawn = deviation * jax.random.normal(rng, extent, jnp.float32)
    if shards:
        drawn = drawn * level_of(rng, extent, shards, -0.22, 0.18)
    return jnp.clip(drawn, -most, most).astype(dtype)


def setup_inputs(seed: int = 0) -> dict:
    key_list = jax.random.split(jax.random.key(seed), 5)
    return {
        "momentum": noise(key_list[0], (ROWS, COLS), 1.0, 6.0, ((0, 32), (1, 8))),
        "gradient": draw_gradient(jax.random.fold_in(key_list[4], 71), 0),
        "weights": noise(key_list[2], (ROWS, COLS), 1.0, 6.0, ((0, 32), (1, 8))),
        "subspace": noise(key_list[3], (COLS, RANK), COLS ** -0.5, 0.0390625, ((0, 8),), jnp.float32),
    }


inertia = 0.95
step_size = 0.5
shrinkage = 0.1
epsilon_sq = 1e-06

def reference(momentum, gradient, weights, subspace):
    blended = (momentum.astype(jnp.float32) + gradient.astype(jnp.float32)).astype(jnp.bfloat16)
    lowered = subspace.astype(jnp.bfloat16)
    projected = jnp.dot(blended.astype(jnp.float32), lowered.astype(jnp.float32), preferred_element_type=jnp.float32)
    gram_matrix = jnp.dot(projected.T.astype(jnp.float32), projected.astype(jnp.float32), precision=lax.Precision.HIGHEST, preferred_element_type=jnp.float32)
    factor = jnp.linalg.cholesky(gram_matrix)
    orthonormal = lax.linalg.triangular_solve(factor, projected, left_side=False, lower=True, transpose_a=True)
    ortho_rounded = orthonormal.astype(jnp.bfloat16)
    coefficients = lax.dot_general(blended.astype(jnp.float32), ortho_rounded.astype(jnp.float32), (((0,), (0,)), ((), ())), preferred_element_type=jnp.float32)
    coeff_rounded = coefficients.astype(jnp.bfloat16)
    feedback = jnp.dot(ortho_rounded.astype(jnp.float32), coeff_rounded.T.astype(jnp.float32), preferred_element_type=jnp.float32)
    new_momentum = (blended.astype(jnp.float32) - (1.0 - inertia) * feedback).astype(jnp.bfloat16)
    col_squares = lax.optimization_barrier(jnp.sum(coefficients * coefficients, axis=0))
    new_subspace = coefficients / jnp.sqrt(col_squares + epsilon_sq)
    update = jnp.dot(ortho_rounded.astype(jnp.float32), new_subspace.astype(jnp.bfloat16).T.astype(jnp.float32), preferred_element_type=jnp.float32)
    scaling = math.sqrt(ROWS * COLS / RANK)
    new_weights = (weights.astype(jnp.float32) * (1.0 - step_size * shrinkage) - step_size * scaling * update).astype(jnp.bfloat16)
    return (new_momentum, new_weights, new_subspace)
```

```python
import functools
import math

import jax
import jax.numpy as jnp
from jax import lax
from jax.experimental import pallas as pl
from jax.experimental.pallas import tpu as pltpu
from jax.sharding import PartitionSpec as P

ROWS = 8192
COLS = 26624
RANK = 128

inertia = 0.95
step_size = 0.5
shrinkage = 0.1
epsilon_sq = 1e-06

LOCAL_ROWS = 256
LOCAL_COLS = 3328
TP = 8
FSDP = 32
HALF = LOCAL_COLS // 2
CHUNK = HALF // 4
PIECE = HALF // 8
CUT = 40
WIDE = 256
TILES = LOCAL_COLS // WIDE
STRIPS = ((0, 512), (512, 768), (1280, 768), (2048, 768), (2816, 512))

X_ONE, Y_ONE, X_THREE, Y_THREE, CORE = 3, 9, 7, 25, 1
MASKS = ((X_ONE, X_THREE, Y_ONE, Y_THREE), (Y_ONE, Y_THREE, X_ONE, X_THREE))


def team(f):
    return (f % 2 + f // 2 + f // 8) % 2


Z_PAIRS = (
    ((0, 1), (2, 3), (4, 5), (6, 7)),
    ((1, 2), (3, 4), (5, 6), (7, 0)),
    ((2, 5), (1, 6), (4, 7), (3, 0)),
)

VMEM = pltpu.VMEM
VMEM_SPEC = pl.BlockSpec(memory_space=pltpu.VMEM)
HBM_SPEC = pl.BlockSpec(memory_space=pltpu.HBM)
PARAMS = pltpu.CompilerParams(vmem_limit_bytes=24 * 1024 * 1024)
NT = (((1,), (1,)), ((), ()))
TN = (((0,), (0,)), ((), ()))


def f32(*shape):
    return jax.ShapeDtypeStruct(shape, jnp.float32)


def bf16(*shape):
    return jax.ShapeDtypeStruct(shape, jnp.bfloat16)


def cost(flops, nbytes):
    return pl.CostEstimate(flops=flops, bytes_accessed=nbytes, transcendentals=0)


def swap_z(x, step):
    perm = []
    for f in range(FSDP):
        for a, b in Z_PAIRS[step]:
            one, two = f * TP + (a + f % 2) % TP, f * TP + (b + f % 2) % TP
            perm += [(one, two), (two, one)]
    return lax.ppermute(x, ("fsdp", "tp"), perm)


def cross_z(x, mask):
    perm = [(f * TP + z, (f ^ 1) * TP + (z ^ mask)) for f in range(FSDP) for z in range(TP)]
    return lax.ppermute(x, ("fsdp", "tp"), perm)


def xor_fsdp(x, mask):
    return lax.ppermute(x, "fsdp", [(i, i ^ mask) for i in range(FSDP)])


def xor_step(x, k):
    return lax.ppermute(x, "fsdp", [(i, i ^ MASKS[team(i)][k]) for i in range(FSDP)])


def step_bit(k):
    f = lax.axis_index("fsdp")
    place = jnp.where(team(f) == 0, (f // 2) % 4, f // 8)
    return place // 2 if k else place % 2 ^ place // 2


def project_kernel(m_hbm, g_hbm, s_hbm, b_ref, part_ref, m_buf, g_buf, s_buf, sems):
    copies = []
    for i, (start, size) in enumerate(STRIPS):
        cols = pl.ds(start, size)
        copies.append((
            pltpu.make_async_copy(m_hbm.at[:, cols], m_buf.at[:, cols], sems.at[0, i]),
            pltpu.make_async_copy(g_hbm.at[:, cols], g_buf.at[:, cols], sems.at[1, i]),
            pltpu.make_async_copy(s_hbm.at[cols, :], s_buf.at[cols, :], sems.at[2, i]),
        ))
    for trio in copies:
        for copy in trio:
            copy.start()
    for i, trio in enumerate(copies):
        for copy in trio:
            copy.wait()
        start, size = STRIPS[i]
        cols = slice(start, start + size)
        b = (m_buf[:, cols].astype(jnp.float32) + g_buf[:, cols].astype(jnp.float32)).astype(jnp.bfloat16)
        b_ref[:, cols] = b
        part = jnp.dot(b, s_buf[cols, :].astype(jnp.bfloat16), preferred_element_type=jnp.float32)
        if i == 0:
            part_ref[...] = part
        else:
            part_ref[...] += part


def project(momentum, gradient, subspace):
    momentum, gradient, subspace = [
        pltpu.with_memory_space_constraint(x, pltpu.HBM) for x in (momentum, gradient, subspace)
    ]
    return pl.pallas_call(
        project_kernel,
        in_specs=[HBM_SPEC] * 3,
        out_specs=[VMEM_SPEC] * 2,
        out_shape=[bf16(LOCAL_ROWS, LOCAL_COLS), f32(LOCAL_ROWS, RANK)],
        scratch_shapes=[
            VMEM((LOCAL_ROWS, LOCAL_COLS), jnp.bfloat16),
            VMEM((LOCAL_ROWS, LOCAL_COLS), jnp.bfloat16),
            VMEM((LOCAL_COLS, RANK), jnp.float32),
            pltpu.SemaphoreType.DMA((3, len(STRIPS))),
        ],
        compiler_params=PARAMS,
        cost_estimate=cost(2 * 256 * 3328 * 128, 7000000),
        name="project",
    )(momentum, gradient, subspace)


def local(kernel, out_shape, args, after=(), flops=0, nbytes=0, name=None, scratch=()):
    used = len(args)

    def body(*refs):
        kernel(*refs[:used], *refs[used + len(after):])

    single = not isinstance(out_shape, (list, tuple))
    return pl.pallas_call(
        body,
        in_specs=[VMEM_SPEC] * (used + len(after)),
        out_specs=VMEM_SPEC if single else [VMEM_SPEC] * len(out_shape),
        out_shape=out_shape,
        scratch_shapes=list(scratch),
        compiler_params=PARAMS,
        cost_estimate=cost(flops, nbytes),
        name=name,
    )(*args, *after)


def lift_half(p, b_ref, half, target):
    high = p.astype(jnp.bfloat16)
    low = (p - high.astype(jnp.float32)).astype(jnp.bfloat16)
    split = jnp.concatenate([high, low], axis=1)
    for k in range(HALF // 128):
        cols = pl.ds(pl.multiple_of(half * HALF + k * 128, 128), 128)
        d = lax.dot_general(b_ref[:, cols], split, TN, preferred_element_type=jnp.float32)
        target[k * 128:(k + 1) * 128, :] = d[:, :RANK] + d[:, RANK:]


def gram_kernel(p_ref, gram_ref):
    p = p_ref[...]
    gram_ref[...] = lax.dot_general(
        p, p, TN, precision=lax.Precision.HIGHEST, preferred_element_type=jnp.float32
    )


def lift_send_kernel(p_ref, b_ref, send_ref):
    c = team(lax.axis_index("fsdp"))
    lift_half(p_ref[...], b_ref, 1 - c, send_ref)


def lift_keep_kernel(p_ref, b_ref, keep_ref):
    lift_half(p_ref[...], b_ref, team(lax.axis_index("fsdp")), keep_ref)


def split_kernel(k, n, keep_ref, recv_ref, send_ref, next_ref):
    bit = step_bit(k)
    away = pl.ds(pl.multiple_of((1 - bit) * n, 8), n)
    stay = pl.ds(pl.multiple_of(bit * n, 8), n)
    send_ref[...] = keep_ref[away, :] + recv_ref[away, :]
    next_ref[...] = keep_ref[stay, :] + recv_ref[stay, :]


def split_step(k, n, keep, recv, after=()):
    return local(
        functools.partial(split_kernel, k, n), [f32(n, RANK), f32(n, RANK)], [keep, recv], after,
        flops=n * 256, nbytes=n * 2048, name=f"split{k}",
    )


def add_kernel(a_ref, b_ref, out_ref):
    out_ref[...] = a_ref[...] + b_ref[...]


def hold_kernel(a_ref, out_ref):
    out_ref[...] = a_ref[...]


def add(a, b, after, name):
    return local(add_kernel, f32(*a.shape), [a, b], after, nbytes=3 * 4 * a.size, name=name)


def reciprocal(x):
    r = pl.reciprocal(x, approx=True)
    r = r * (2.0 - x * r)
    return r * (2.0 - x * r)


def unit_scale(rows, lane, sub):
    diagonal = jnp.zeros((8, RANK), jnp.float32)
    for k, row in enumerate(rows):
        diagonal = diagonal + jnp.where(lane == sub + 8 * k, row, 0.0)
    return lax.rsqrt(jnp.sum(diagonal, axis=0, keepdims=True))


def eliminate_kernel(start, stop, in_ref, gram_ref, out_ref):
    groups = RANK // 8
    lane = lax.broadcasted_iota(jnp.int32, (8, RANK), 1)
    sub = lax.broadcasted_iota(jnp.int32, (8, RANK), 0)

    def across(x):
        return jnp.broadcast_to(x, (8, RANK))

    t = [in_ref[8 * r:8 * r + 8, :] for r in range(groups)]
    if start == 0 or stop == RANK:
        gram = [gram_ref[8 * r:8 * r + 8, :] for r in range(groups)]
        scale = unit_scale(gram, lane, sub)
    if start == 0:
        for r in range(groups):
            own = jnp.sum(jnp.where(lane == sub + 8 * r, t[r], 0.0), axis=1, keepdims=True)
            t[r] = t[r] * lax.rsqrt(own) * scale
    for r in range(start // 8, stop // 8):
        cols = {
            k: [across(t[k][:, 8 * r + i:8 * r + i + 1]) for i in range(8)]
            for k in range(r, groups)
        }
        for i in range(0, 8, 2):
            j = 8 * r + i
            p, q = across(cols[r][i][i:i + 1, :]), across(cols[r][i][i + 1:i + 2, :])
            d = across(cols[r][i + 1][i + 1:i + 2, :])
            inv_p = reciprocal(p)
            inv_d = p * reciprocal(p * d - q * q)
            ratio = q * inv_p
            above = {n: across(cols[r][n][i:i + 1, :]) for n in range(i + 2, 8)}
            below = {n: across(cols[r][n][i + 1:i + 2, :]) - ratio * above[n] for n in above}
            at_j, at_next = lane == j, lane == j + 1
            unit_a = jnp.where(at_j, 1.0, across(t[r][i:i + 1, :]))
            new_b = jnp.where(at_j, 0.0, across(t[r][i + 1:i + 2, :])) - ratio * unit_a
            row_a = jnp.where(at_next, 0.0, unit_a)
            row_b = jnp.where(at_next, 1.0, new_b)
            either = at_j | at_next
            for k in range(r, groups):
                first = cols[k][i] * inv_p
                second = (cols[k][i + 1] - first * q) * inv_d
                if k == r:
                    first = jnp.where(sub > i, first, 0.0)
                    second = jnp.where(sub > i + 1, second, 0.0)
                for n in above:
                    cols[k][n] = cols[k][n] - first * above[n] - second * below[n]
                new = jnp.where(either, 0.0, t[k]) - first * row_a - second * row_b
                if k == r:
                    new = jnp.where(sub > i + 1, new, jnp.where(sub == i + 1, new_b, t[k]))
                t[k] = new
    for k in range(groups):
        if stop == RANK:
            row_of = sub + 8 * k
            pivot = jnp.sum(jnp.where(lane == row_of, t[k], 0.0), axis=1, keepdims=True)
            unit = jnp.where(lane < row_of, t[k], jnp.where(lane == row_of, 1.0, 0.0))
            out_ref[8 * k:8 * k + 8, :] = unit * lax.rsqrt(pivot) * scale
        else:
            out_ref[8 * k:8 * k + 8, :] = t[k]


def eliminate(start, stop, state, gram, after=()):
    return local(
        functools.partial(eliminate_kernel, start, stop), f32(RANK, RANK), [state, gram], after,
        flops=4000000, nbytes=(stop - start) * 150000, name=f"eliminate{start}",
    )


def block_kernel(keep_ref, recv_ref, w_ref, out_ref):
    w = w_ref[...].T
    w_high = w.astype(jnp.bfloat16)
    w_low = (w - w_high.astype(jnp.float32)).astype(jnp.bfloat16)
    both = jnp.concatenate([
        jnp.concatenate([w_high, w_low], axis=1),
        jnp.concatenate([w_high, jnp.zeros_like(w_low)], axis=1),
    ], axis=0)
    d = keep_ref[...] + recv_ref[...]
    high = d.astype(jnp.bfloat16)
    low = (d - high.astype(jnp.float32)).astype(jnp.bfloat16)
    out = jnp.dot(jnp.concatenate([high, low], axis=1), both, preferred_element_type=jnp.float32)
    out_ref[...] = (out[:, :RANK] + out[:, RANK:]).astype(jnp.bfloat16)


def ortho_kernel(p_ref, w_ref, out_ref):
    out_ref[...] = lax.dot_general(
        p_ref[...], w_ref[...], NT, precision=lax.Precision.HIGHEST, preferred_element_type=jnp.float32
    ).astype(jnp.bfloat16)


def join_kernel(k, n, mine_ref, recv_ref, out_ref):
    bit = step_bit(k)
    out_ref[pl.ds(pl.multiple_of(bit * n, 16), n), :] = mine_ref[...]
    out_ref[pl.ds(pl.multiple_of((1 - bit) * n, 16), n), :] = recv_ref[...]


def unpack_kernel(own_ref, other_ref, coef_ref, sq_ref):
    c = team(lax.axis_index("fsdp"))
    squares = jnp.zeros((8, RANK), jnp.float32)
    for source, half in ((own_ref, c), (other_ref, 1 - c)):
        for i in range(0, HALF, PIECE):
            rows = source[i:i + PIECE, :].astype(jnp.float32)
            squares = squares + jnp.sum((rows * rows).reshape(PIECE // 8, 8, RANK), axis=0)
            coef_ref[pl.ds(pl.multiple_of(half * HALF + i, 8), PIECE), :] = rows
    sq_ref[...] = jnp.broadcast_to(jnp.sum(squares, axis=0, keepdims=True), (8, RANK))


def momentum_kernel(coef_ref, ortho_ref, b_ref, mom_hbm, buf, sems):
    ortho = ortho_ref[...]
    copies = []
    for i in range(TILES):
        cols = slice(i * WIDE, (i + 1) * WIDE)
        feedback = lax.dot_general(
            ortho, coef_ref[cols, :].astype(jnp.bfloat16), NT, preferred_element_type=jnp.float32
        )
        buf[:, cols] = (
            b_ref[:, cols].astype(jnp.float32) - (1.0 - inertia) * feedback
        ).astype(jnp.bfloat16)
        at = pl.ds(i * WIDE, WIDE)
        copies.append(pltpu.make_async_copy(buf.at[:, at], mom_hbm.at[:, at], sems.at[i]))
        copies[-1].start()
    for copy in copies:
        copy.wait()


def finish_momentum(coef, ortho, blended):
    return pl.pallas_call(
        momentum_kernel,
        in_specs=[VMEM_SPEC] * 3,
        out_specs=HBM_SPEC,
        out_shape=bf16(LOCAL_ROWS, LOCAL_COLS),
        scratch_shapes=[
            VMEM((LOCAL_ROWS, LOCAL_COLS), jnp.bfloat16),
            pltpu.SemaphoreType.DMA((TILES,)),
        ],
        compiler_params=PARAMS,
        cost_estimate=cost(2 * 256 * 3328 * 128, 5000000),
        name="finish_momentum",
    )(coef, ortho, blended)


def weights_kernel(sq_ref, coef_ref, ortho_ref, weights_ref, new_hbm, sub_hbm, buf, sub_buf, sems):
    scaling = math.sqrt(ROWS * COLS / RANK)
    norm = 1.0 / jnp.sqrt(sq_ref[0:1, :] + epsilon_sq)
    ortho = ortho_ref[...]
    copies = []
    for i in range(TILES):
        cols = slice(i * WIDE, (i + 1) * WIDE)
        at = pl.ds(i * WIDE, WIDE)
        subspace = coef_ref[cols, :] * norm
        sub_buf[cols, :] = subspace
        copies.append(pltpu.make_async_copy(sub_buf.at[at, :], sub_hbm.at[at, :], sems.at[0, i]))
        copies[-1].start()
        update = lax.dot_general(
            ortho, subspace.astype(jnp.bfloat16), NT, preferred_element_type=jnp.float32
        )
        buf[:, cols] = (
            weights_ref[:, cols].astype(jnp.float32) * (1.0 - step_size * shrinkage)
            - step_size * scaling * update
        ).astype(jnp.bfloat16)
        copies.append(pltpu.make_async_copy(buf.at[:, at], new_hbm.at[:, at], sems.at[1, i]))
        copies[-1].start()
    for copy in copies:
        copy.wait()


def finish_weights(squares, coef, ortho, weights):
    return pl.pallas_call(
        weights_kernel,
        in_specs=[VMEM_SPEC] * 4,
        out_specs=[HBM_SPEC] * 2,
        out_shape=[bf16(LOCAL_ROWS, LOCAL_COLS), f32(LOCAL_COLS, RANK)],
        scratch_shapes=[
            VMEM((LOCAL_ROWS, LOCAL_COLS), jnp.bfloat16),
            VMEM((LOCAL_COLS, RANK), jnp.float32),
            pltpu.SemaphoreType.DMA((2, TILES)),
        ],
        compiler_params=PARAMS,
        cost_estimate=cost(2 * 256 * 3328 * 128, 7000000),
        name="finish_weights",
    )(squares, coef, ortho, weights)


def on_device(momentum, gradient, weights, subspace):
    blended, projected = project(momentum, gradient, subspace)
    for step in range(3):
        projected = projected + swap_z(projected, step)

    gram = local(gram_kernel, f32(RANK, RANK), [projected], flops=6 * 256 * 128 * 256, nbytes=200000, name="gram")
    more = xor_fsdp(gram, X_ONE)
    send = local(
        lift_send_kernel, f32(HALF, RANK), [projected, blended], [gram],
        flops=2 * 256 * 3328 * 128, nbytes=2000000, name="lift_send",
    )
    recv = xor_fsdp(send, CORE)
    keep = local(
        lift_keep_kernel, f32(HALF, RANK), [projected, blended], [send],
        flops=2 * 256 * 3328 * 128, nbytes=2000000, name="lift_keep",
    )
    gram = add(gram, more, [keep], "add_x1")
    more = xor_fsdp(gram, X_THREE)
    n = HALF // 2
    moving, keep = split_step(0, n, keep, recv, [gram])
    recv = xor_step(moving, 0)
    gram = add(gram, more, [moving], "add_x3")
    gram = add(gram, xor_fsdp(gram, Y_ONE), [], "add_y1")
    n //= 2
    moving, keep = split_step(1, n, keep, recv, [gram])
    recv = xor_step(moving, 1)
    gram = local(hold_kernel, f32(RANK, RANK), [gram], [moving], nbytes=130000, name="hold")
    more = xor_fsdp(gram, Y_THREE)
    d = add(keep, recv, [more], "first_sum")
    recv = xor_step(d, 2)
    gram = add(gram, more, [d], "add_y3")
    gram = add(gram, xor_fsdp(gram, CORE), [], "add_core")
    state = eliminate(0, CUT, gram, gram)
    d = add(d, recv, [state], "second_sum")
    recv = xor_step(d, 3)
    inverse = eliminate(CUT, RANK, state, gram, [d])

    coef = local(
        block_kernel, bf16(CHUNK, RANK), [d, recv, inverse],
        flops=2 * CHUNK * 256 * 256, nbytes=700000, name="block",
    )
    ortho = local(
        ortho_kernel, bf16(LOCAL_ROWS, RANK), [projected, inverse], [coef],
        flops=6 * 256 * 256 * 128, nbytes=300000, name="ortho",
    )
    for k, n in ((1, CHUNK), (0, 2 * CHUNK)):
        coef = local(
            functools.partial(join_kernel, k, n), bf16(2 * n, RANK), [coef, xor_step(coef, k)],
            [ortho] if k else [], nbytes=n * 1024, name=f"join{k}",
        )
    coef, squares = local(
        unpack_kernel, [f32(LOCAL_COLS, RANK), f32(8, RANK)], [coef, xor_fsdp(coef, CORE)],
        flops=3328 * 256, nbytes=2600000, name="unpack",
    )
    squares = (squares + cross_z(squares, 1)) + (cross_z(squares, 2) + cross_z(squares, 3))
    squares = squares + cross_z(squares, 7)
    new_momentum = finish_momentum(coef, ortho, blended)
    new_weights, new_subspace = finish_weights(squares, coef, ortho, weights)
    return (new_momentum, new_weights, new_subspace)


def solution(mesh):
    placed = (P("fsdp", "tp"), P("fsdp", "tp"), P("fsdp", "tp"), P("tp", None))
    return jax.shard_map(
        on_device,
        mesh=mesh,
        in_specs=placed,
        out_specs=(P("fsdp", "tp"), P("fsdp", "tp"), P("tp", None)),
        check_vma=False,
    )
```

```python
import functools
import math

import jax
import jax.numpy as jnp
from jax import lax
from jax.experimental import pallas as pl
from jax.experimental.pallas import tpu as pltpu
from jax.sharding import PartitionSpec as P

ROWS = 8192
COLS = 26624
RANK = 128

inertia = 0.95
step_size = 0.5
shrinkage = 0.1
epsilon_sq = 1e-06

LOCAL_ROWS = 256
LOCAL_COLS = 3328
TP = 8
FSDP = 32
HALF = LOCAL_COLS // 2
CHUNK = HALF // 4
PIECE = HALF // 8
WIDE = 256
TILES = LOCAL_COLS // WIDE
STRIPS = ((0, 512), (512, 768), (1280, 768), (2048, 768), (2816, 512))

X_ONE, Y_ONE, X_THREE, Y_THREE, CORE = 3, 9, 7, 25, 1
MASKS = ((X_ONE, X_THREE, Y_ONE, Y_THREE), (Y_ONE, Y_THREE, X_ONE, X_THREE))


def team(f):
    return (f % 2 + f // 2 + f // 8) % 2


Z_PAIRS = (
    ((0, 1), (2, 3), (4, 5), (6, 7)),
    ((1, 2), (3, 4), (5, 6), (7, 0)),
    ((2, 5), (1, 6), (4, 7), (3, 0)),
)

VMEM = pltpu.VMEM
VMEM_SPEC = pl.BlockSpec(memory_space=pltpu.VMEM)
HBM_SPEC = pl.BlockSpec(memory_space=pltpu.HBM)
PARAMS = pltpu.CompilerParams(vmem_limit_bytes=24 * 1024 * 1024)
NT = (((1,), (1,)), ((), ()))
TN = (((0,), (0,)), ((), ()))


def f32(*shape):
    return jax.ShapeDtypeStruct(shape, jnp.float32)


def bf16(*shape):
    return jax.ShapeDtypeStruct(shape, jnp.bfloat16)


def cost(flops, nbytes):
    return pl.CostEstimate(flops=flops, bytes_accessed=nbytes, transcendentals=0)


def swap_z(x, step):
    perm = []
    for f in range(FSDP):
        for a, b in Z_PAIRS[step]:
            one, two = f * TP + (a + f % 2) % TP, f * TP + (b + f % 2) % TP
            perm += [(one, two), (two, one)]
    return lax.ppermute(x, ("fsdp", "tp"), perm)


def cross_z(x, mask):
    perm = [(f * TP + z, (f ^ 1) * TP + (z ^ mask)) for f in range(FSDP) for z in range(TP)]
    return lax.ppermute(x, ("fsdp", "tp"), perm)


def xor_fsdp(x, mask):
    return lax.ppermute(x, "fsdp", [(i, i ^ mask) for i in range(FSDP)])


def xor_step(x, k):
    return lax.ppermute(x, "fsdp", [(i, i ^ MASKS[team(i)][k]) for i in range(FSDP)])


def step_bit(k):
    f = lax.axis_index("fsdp")
    place = jnp.where(team(f) == 0, (f // 2) % 4, f // 8)
    return place // 2 if k else place % 2 ^ place // 2


def project_kernel(m_hbm, g_hbm, s_hbm, b_ref, part_ref, m_buf, g_buf, s_buf, sems):
    copies = []
    for i, (start, size) in enumerate(STRIPS):
        cols = pl.ds(start, size)
        copies.append((
            pltpu.make_async_copy(m_hbm.at[:, cols], m_buf.at[:, cols], sems.at[0, i]),
            pltpu.make_async_copy(g_hbm.at[:, cols], g_buf.at[:, cols], sems.at[1, i]),
            pltpu.make_async_copy(s_hbm.at[cols, :], s_buf.at[cols, :], sems.at[2, i]),
        ))
    for trio in copies:
        for copy in trio:
            copy.start()
    for i, trio in enumerate(copies):
        for copy in trio:
            copy.wait()
        start, size = STRIPS[i]
        cols = slice(start, start + size)
        b = (m_buf[:, cols].astype(jnp.float32) + g_buf[:, cols].astype(jnp.float32)).astype(jnp.bfloat16)
        b_ref[:, cols] = b
        part = jnp.dot(b, s_buf[cols, :].astype(jnp.bfloat16), preferred_element_type=jnp.float32)
        if i == 0:
            part_ref[...] = part
        else:
            part_ref[...] += part


def project(momentum, gradient, subspace):
    momentum, gradient, subspace = [
        pltpu.with_memory_space_constraint(x, pltpu.HBM) for x in (momentum, gradient, subspace)
    ]
    return pl.pallas_call(
        project_kernel,
        in_specs=[HBM_SPEC] * 3,
        out_specs=[VMEM_SPEC] * 2,
        out_shape=[bf16(LOCAL_ROWS, LOCAL_COLS), f32(LOCAL_ROWS, RANK)],
        scratch_shapes=[
            VMEM((LOCAL_ROWS, LOCAL_COLS), jnp.bfloat16),
            VMEM((LOCAL_ROWS, LOCAL_COLS), jnp.bfloat16),
            VMEM((LOCAL_COLS, RANK), jnp.float32),
            pltpu.SemaphoreType.DMA((3, len(STRIPS))),
        ],
        compiler_params=PARAMS,
        cost_estimate=cost(2 * 256 * 3328 * 128, 7000000),
        name="project",
    )(momentum, gradient, subspace)


def local(kernel, out_shape, args, after=(), flops=0, nbytes=0, name=None, scratch=()):
    used = len(args)

    def body(*refs):
        kernel(*refs[:used], *refs[used + len(after):])

    single = not isinstance(out_shape, (list, tuple))
    return pl.pallas_call(
        body,
        in_specs=[VMEM_SPEC] * (used + len(after)),
        out_specs=VMEM_SPEC if single else [VMEM_SPEC] * len(out_shape),
        out_shape=out_shape,
        scratch_shapes=list(scratch),
        compiler_params=PARAMS,
        cost_estimate=cost(flops, nbytes),
        name=name,
    )(*args, *after)


def lift_half(p, b_ref, half, target):
    high = p.astype(jnp.bfloat16)
    low = (p - high.astype(jnp.float32)).astype(jnp.bfloat16)
    split = jnp.concatenate([high, low], axis=1)
    for k in range(HALF // 128):
        cols = pl.ds(pl.multiple_of(half * HALF + k * 128, 128), 128)
        d = lax.dot_general(b_ref[:, cols], split, TN, preferred_element_type=jnp.float32)
        target[k * 128:(k + 1) * 128, :] = d[:, :RANK] + d[:, RANK:]


def lift_send_kernel(p_ref, b_ref, send_ref):
    c = team(lax.axis_index("fsdp"))
    p = p_ref[...]
    lift_half(p, b_ref, 1 - c, send_ref)
    send_ref[HALF:, :] = lax.dot_general(
        p, p, TN, precision=lax.Precision.HIGHEST, preferred_element_type=jnp.float32
    )


def lift_keep_kernel(p_ref, b_ref, keep_ref):
    lift_half(p_ref[...], b_ref, team(lax.axis_index("fsdp")), keep_ref)


def split_kernel(k, n, keep_ref, recv_ref, send_ref, next_ref):
    bit = step_bit(k)
    away = pl.ds(pl.multiple_of((1 - bit) * n, 8), n)
    stay = pl.ds(pl.multiple_of(bit * n, 8), n)
    send_ref[...] = keep_ref[away, :] + recv_ref[away, :]
    next_ref[...] = keep_ref[stay, :] + recv_ref[stay, :]


def split_step(k, n, keep, recv, after=()):
    return local(
        functools.partial(split_kernel, k, n), [f32(n, RANK), f32(n, RANK)], [keep, recv], after,
        flops=n * 256, nbytes=n * 2048, name=f"split{k}",
    )


def add_kernel(a_ref, b_ref, out_ref):
    out_ref[...] = a_ref[...] + b_ref[...]


def gram_pair_kernel(sent_ref, recv_ref, out_ref):
    out_ref[...] = sent_ref[HALF:, :] + recv_ref[HALF:, :]


def hold_kernel(a_ref, out_ref):
    out_ref[...] = a_ref[...]


def add(a, b, after, name):
    return local(add_kernel, f32(*a.shape), [a, b], after, nbytes=3 * 4 * a.size, name=name)


def reciprocal(x):
    r = pl.reciprocal(x, approx=True)
    r = r * (2.0 - x * r)
    return r * (2.0 - x * r)


def unit_scale(rows, lane, sub):
    diagonal = jnp.zeros((8, RANK), jnp.float32)
    for k, row in enumerate(rows):
        diagonal = diagonal + jnp.where(lane == sub + 8 * k, row, 0.0)
    return lax.rsqrt(jnp.sum(diagonal, axis=0, keepdims=True))


def eliminate_kernel(start, stop, in_ref, gram_ref, out_ref):
    groups = RANK // 8
    lane = lax.broadcasted_iota(jnp.int32, (8, RANK), 1)
    sub = lax.broadcasted_iota(jnp.int32, (8, RANK), 0)

    def across(x):
        return jnp.broadcast_to(x, (8, RANK))

    t = [in_ref[8 * r:8 * r + 8, :] for r in range(groups)]
    if start == 0 or stop == RANK:
        gram = [gram_ref[8 * r:8 * r + 8, :] for r in range(groups)]
        scale = unit_scale(gram, lane, sub)
    if start == 0:
        for r in range(groups):
            own = jnp.sum(jnp.where(lane == sub + 8 * r, t[r], 0.0), axis=1, keepdims=True)
            t[r] = t[r] * lax.rsqrt(own) * scale
    for r in range(start // 8, stop // 8):
        cols = {
            k: [across(t[k][:, 8 * r + i:8 * r + i + 1]) for i in range(8)]
            for k in range(r, groups)
        }
        for i in range(0, 8, 2):
            j = 8 * r + i
            p, q = across(cols[r][i][i:i + 1, :]), across(cols[r][i][i + 1:i + 2, :])
            d = across(cols[r][i + 1][i + 1:i + 2, :])
            inv_p = reciprocal(p)
            inv_d = p * reciprocal(p * d - q * q)
            ratio = q * inv_p
            above = {n: across(cols[r][n][i:i + 1, :]) for n in range(i + 2, 8)}
            below = {n: across(cols[r][n][i + 1:i + 2, :]) - ratio * above[n] for n in above}
            at_j, at_next = lane == j, lane == j + 1
            unit_a = jnp.where(at_j, 1.0, across(t[r][i:i + 1, :]))
            new_b = jnp.where(at_j, 0.0, across(t[r][i + 1:i + 2, :])) - ratio * unit_a
            row_a = jnp.where(at_next, 0.0, unit_a)
            row_b = jnp.where(at_next, 1.0, new_b)
            either = at_j | at_next
            for k in range(r, groups):
                first = cols[k][i] * inv_p
                second = (cols[k][i + 1] - first * q) * inv_d
                if k == r:
                    first = jnp.where(sub > i, first, 0.0)
                    second = jnp.where(sub > i + 1, second, 0.0)
                for n in above:
                    cols[k][n] = cols[k][n] - first * above[n] - second * below[n]
                new = jnp.where(either, 0.0, t[k]) - first * row_a - second * row_b
                if k == r:
                    new = jnp.where(sub > i + 1, new, jnp.where(sub == i + 1, new_b, t[k]))
                t[k] = new
    for k in range(groups):
        if stop == RANK:
            row_of = sub + 8 * k
            pivot = jnp.sum(jnp.where(lane == row_of, t[k], 0.0), axis=1, keepdims=True)
            unit = jnp.where(lane < row_of, t[k], jnp.where(lane == row_of, 1.0, 0.0))
            out_ref[8 * k:8 * k + 8, :] = unit * lax.rsqrt(pivot) * scale
        else:
            out_ref[8 * k:8 * k + 8, :] = t[k]


def eliminate(start, stop, state, gram, after=()):
    return local(
        functools.partial(eliminate_kernel, start, stop), f32(RANK, RANK), [state, gram], after,
        flops=4000000, nbytes=(stop - start) * 150000, name=f"eliminate{start}",
    )


def block_kernel(keep_ref, recv_ref, w_ref, out_ref):
    w = w_ref[...].T
    w_high = w.astype(jnp.bfloat16)
    w_low = (w - w_high.astype(jnp.float32)).astype(jnp.bfloat16)
    both = jnp.concatenate([
        jnp.concatenate([w_high, w_low], axis=1),
        jnp.concatenate([w_high, jnp.zeros_like(w_low)], axis=1),
    ], axis=0)
    d = keep_ref[...] + recv_ref[...]
    high = d.astype(jnp.bfloat16)
    low = (d - high.astype(jnp.float32)).astype(jnp.bfloat16)
    out = jnp.dot(jnp.concatenate([high, low], axis=1), both, preferred_element_type=jnp.float32)
    out_ref[...] = (out[:, :RANK] + out[:, RANK:]).astype(jnp.bfloat16)


def ortho_kernel(p_ref, w_ref, out_ref):
    out_ref[...] = lax.dot_general(
        p_ref[...], w_ref[...], NT, precision=lax.Precision.HIGHEST, preferred_element_type=jnp.float32
    ).astype(jnp.bfloat16)


def join_kernel(k, n, mine_ref, recv_ref, out_ref):
    bit = step_bit(k)
    out_ref[pl.ds(pl.multiple_of(bit * n, 16), n), :] = mine_ref[...]
    out_ref[pl.ds(pl.multiple_of((1 - bit) * n, 16), n), :] = recv_ref[...]


def unpack_kernel(own_ref, other_ref, coef_ref, sq_ref):
    c = team(lax.axis_index("fsdp"))
    squares = jnp.zeros((8, RANK), jnp.float32)
    for source, half in ((own_ref, c), (other_ref, 1 - c)):
        for i in range(0, HALF, PIECE):
            rows = source[i:i + PIECE, :].astype(jnp.float32)
            squares = squares + jnp.sum((rows * rows).reshape(PIECE // 8, 8, RANK), axis=0)
            coef_ref[pl.ds(pl.multiple_of(half * HALF + i, 8), PIECE), :] = rows
    sq_ref[...] = jnp.broadcast_to(jnp.sum(squares, axis=0, keepdims=True), (8, RANK))


def momentum_kernel(coef_ref, ortho_ref, b_ref, mom_hbm, buf, sems):
    ortho = ortho_ref[...]
    copies = []
    for i in range(TILES):
        cols = slice(i * WIDE, (i + 1) * WIDE)
        feedback = lax.dot_general(
            ortho, coef_ref[cols, :].astype(jnp.bfloat16), NT, preferred_element_type=jnp.float32
        )
        buf[:, cols] = (
            b_ref[:, cols].astype(jnp.float32) - (1.0 - inertia) * feedback
        ).astype(jnp.bfloat16)
        at = pl.ds(i * WIDE, WIDE)
        copies.append(pltpu.make_async_copy(buf.at[:, at], mom_hbm.at[:, at], sems.at[i]))
        copies[-1].start()
    for copy in copies:
        copy.wait()


def finish_momentum(coef, ortho, blended):
    return pl.pallas_call(
        momentum_kernel,
        in_specs=[VMEM_SPEC] * 3,
        out_specs=HBM_SPEC,
        out_shape=bf16(LOCAL_ROWS, LOCAL_COLS),
        scratch_shapes=[
            VMEM((LOCAL_ROWS, LOCAL_COLS), jnp.bfloat16),
            pltpu.SemaphoreType.DMA((TILES,)),
        ],
        compiler_params=PARAMS,
        cost_estimate=cost(2 * 256 * 3328 * 128, 5000000),
        name="finish_momentum",
    )(coef, ortho, blended)


def weights_kernel(sq_ref, coef_ref, ortho_ref, weights_ref, new_hbm, sub_hbm, buf, sub_buf, sems):
    scaling = math.sqrt(ROWS * COLS / RANK)
    norm = 1.0 / jnp.sqrt(sq_ref[0:1, :] + epsilon_sq)
    ortho = ortho_ref[...]
    copies = []
    for i in range(4):
        at = pl.ds(i * 2 * CHUNK, 2 * CHUNK)
        sub_buf[at, :] = coef_ref[at, :] * norm
        copies.append(pltpu.make_async_copy(sub_buf.at[at, :], sub_hbm.at[at, :], sems.at[0, i]))
        copies[-1].start()
    for i, (start, size) in enumerate(STRIPS):
        for first in range(start, start + size, WIDE):
            cols = slice(first, first + WIDE)
            update = lax.dot_general(
                ortho, sub_buf[cols, :].astype(jnp.bfloat16), NT, preferred_element_type=jnp.float32
            )
            buf[:, cols] = (
                weights_ref[:, cols].astype(jnp.float32) * (1.0 - step_size * shrinkage)
                - step_size * scaling * update
            ).astype(jnp.bfloat16)
        at = pl.ds(start, size)
        copies.append(pltpu.make_async_copy(buf.at[:, at], new_hbm.at[:, at], sems.at[1, i]))
        copies[-1].start()
    for copy in copies:
        copy.wait()


def finish_weights(squares, coef, ortho, weights):
    return pl.pallas_call(
        weights_kernel,
        in_specs=[VMEM_SPEC] * 4,
        out_specs=[HBM_SPEC] * 2,
        out_shape=[bf16(LOCAL_ROWS, LOCAL_COLS), f32(LOCAL_COLS, RANK)],
        scratch_shapes=[
            VMEM((LOCAL_ROWS, LOCAL_COLS), jnp.bfloat16),
            VMEM((LOCAL_COLS, RANK), jnp.float32),
            pltpu.SemaphoreType.DMA((2, len(STRIPS))),
        ],
        compiler_params=PARAMS,
        cost_estimate=cost(2 * 256 * 3328 * 128, 7000000),
        name="finish_weights",
    )(squares, coef, ortho, weights)


def on_device(momentum, gradient, weights, subspace):
    blended, projected = project(momentum, gradient, subspace)
    for step in range(3):
        projected = projected + swap_z(projected, step)

    send = local(
        lift_send_kernel, f32(HALF + RANK, RANK), [projected, blended],
        flops=2 * 256 * 3328 * 128, nbytes=2000000, name="lift_send",
    )
    recv = xor_fsdp(send, CORE)
    keep = local(
        lift_keep_kernel, f32(HALF, RANK), [projected, blended], [send],
        flops=2 * 256 * 3328 * 128, nbytes=2000000, name="lift_keep",
    )
    n = HALF // 2
    moving, keep = split_step(0, n, keep, recv)
    gram = local(gram_pair_kernel, f32(RANK, RANK), [send, recv], [moving], nbytes=200000, name="gram_pair")
    recv = xor_step(moving, 0)
    gram = add(gram, xor_fsdp(gram, X_THREE), [], "add_x3")
    gram = add(gram, xor_fsdp(gram, Y_THREE), [], "add_y3")
    n //= 2
    moving, keep = split_step(1, n, keep, recv, [gram])
    recv = xor_step(moving, 1)
    gram = local(hold_kernel, f32(RANK, RANK), [gram], [moving], nbytes=130000, name="hold")
    more = xor_fsdp(gram, X_ONE)
    d = add(keep, recv, [more], "first_sum")
    recv = xor_step(d, 2)
    gram = add(gram, more, [d], "add_x1")
    more = xor_fsdp(gram, Y_ONE)
    d = add(d, recv, [more], "second_sum")
    recv = xor_step(d, 3)
    gram = add(gram, more, [d], "add_y1")
    inverse = eliminate(0, RANK, gram, gram)

    coef = local(
        block_kernel, bf16(CHUNK, RANK), [d, recv, inverse],
        flops=2 * CHUNK * 256 * 256, nbytes=700000, name="block",
    )
    ortho = local(
        ortho_kernel, bf16(LOCAL_ROWS, RANK), [projected, inverse], [coef],
        flops=6 * 256 * 256 * 128, nbytes=300000, name="ortho",
    )
    for k, n in ((1, CHUNK), (0, 2 * CHUNK)):
        coef = local(
            functools.partial(join_kernel, k, n), bf16(2 * n, RANK), [coef, xor_step(coef, k)],
            [ortho] if k else [], nbytes=n * 1024, name=f"join{k}",
        )
    coef, squares = local(
        unpack_kernel, [f32(LOCAL_COLS, RANK), f32(8, RANK)], [coef, xor_fsdp(coef, CORE)],
        flops=3328 * 256, nbytes=2600000, name="unpack",
    )
    squares = (squares + cross_z(squares, 1)) + (cross_z(squares, 2) + cross_z(squares, 3))
    squares = squares + cross_z(squares, 7)
    new_momentum = finish_momentum(coef, ortho, blended)
    new_weights, new_subspace = finish_weights(squares, coef, ortho, weights)
    return (new_momentum, new_weights, new_subspace)


def solution(mesh):
    placed = (P("fsdp", "tp"), P("fsdp", "tp"), P("fsdp", "tp"), P("tp", None))
    return jax.shard_map(
        on_device,
        mesh=mesh,
        in_specs=placed,
        out_specs=(P("fsdp", "tp"), P("fsdp", "tp"), P("tp", None)),
        check_vma=False,
    )
```

```python
import functools
import math

import jax
import jax.numpy as jnp
from jax import lax
from jax.experimental import pallas as pl
from jax.experimental.pallas import tpu as pltpu
from jax.sharding import PartitionSpec as P

ROWS = 8192
COLS = 26624
RANK = 128

inertia = 0.95
step_size = 0.5
shrinkage = 0.1
epsilon_sq = 1e-06

LOCAL_ROWS = 256
LOCAL_COLS = 3328
TP = 8
FSDP = 32
HALF = LOCAL_COLS // 2
CHUNK = HALF // 4
PIECE = HALF // 8
WIDE = 256
TILES = LOCAL_COLS // WIDE
STRIPS = ((0, 512), (512, 768), (1280, 768), (2048, 768), (2816, 512))

X_ONE, Y_ONE, X_THREE, Y_THREE, CORE = 3, 9, 7, 25, 1
MASKS = ((X_ONE, X_THREE, Y_ONE, Y_THREE), (Y_ONE, Y_THREE, X_ONE, X_THREE))


def team(f):
    return (f % 2 + f // 2 + f // 8) % 2


Z_PAIRS = (
    ((0, 1), (2, 3), (4, 5), (6, 7)),
    ((1, 2), (3, 4), (5, 6), (7, 0)),
    ((2, 5), (1, 6), (4, 7), (3, 0)),
)

VMEM = pltpu.VMEM
VMEM_SPEC = pl.BlockSpec(memory_space=pltpu.VMEM)
HBM_SPEC = pl.BlockSpec(memory_space=pltpu.HBM)
PARAMS = pltpu.CompilerParams(vmem_limit_bytes=24 * 1024 * 1024)
NT = (((1,), (1,)), ((), ()))
TN = (((0,), (0,)), ((), ()))


def f32(*shape):
    return jax.ShapeDtypeStruct(shape, jnp.float32)


def bf16(*shape):
    return jax.ShapeDtypeStruct(shape, jnp.bfloat16)


def cost(flops, nbytes):
    return pl.CostEstimate(flops=flops, bytes_accessed=nbytes, transcendentals=0)

Z_TURNS = ((3, -3), (1, -1), (-2, 2))


def swap_z(x, step):
    perm = []
    for f in range(FSDP):
        for a, b in Z_PAIRS[step]:
            one, two = f * TP + (a + f % 2) % TP, f * TP + (b + f % 2) % TP
            perm += [(one, two), (two, one)]
    return lax.ppermute(x, ("fsdp", "tp"), perm)


def pair_z(x, cross):
    perm = [
        (f * TP + z, (f ^ (MASKS[team(f)][0] if cross else 0)) * TP + (z ^ 1))
        for f in range(FSDP) for z in range(TP)
    ]
    return lax.ppermute(x, ("fsdp", "tp"), perm)


def turn_z(x, to_odd, to_even):
    perm = [
        ((f ^ 1) * TP + (z + (to_odd if z % 2 else to_even)) % TP, f * TP + z)
        for f in range(FSDP) for z in range(TP)
    ]
    return lax.ppermute(x, ("fsdp", "tp"), perm)


def xor_fsdp(x, mask):
    return lax.ppermute(x, "fsdp", [(i, i ^ mask) for i in range(FSDP)])


def xor_step(x, k):
    return lax.ppermute(x, "fsdp", [(i, i ^ MASKS[team(i)][k]) for i in range(FSDP)])


def step_bit(k):
    f = lax.axis_index("fsdp")
    place = jnp.where(team(f) == 0, (f // 2) % 4, f // 8)
    return place // 2 if k else place % 2 ^ place // 2


def project_kernel(m_hbm, g_hbm, s_hbm, b_ref, part_ref, m_buf, g_buf, s_buf, sems):
    copies = []
    for i, (start, size) in enumerate(STRIPS):
        cols = pl.ds(start, size)
        copies.append((
            pltpu.make_async_copy(m_hbm.at[:, cols], m_buf.at[:, cols], sems.at[0, i]),
            pltpu.make_async_copy(g_hbm.at[:, cols], g_buf.at[:, cols], sems.at[1, i]),
            pltpu.make_async_copy(s_hbm.at[cols, :], s_buf.at[cols, :], sems.at[2, i]),
        ))
    for trio in copies:
        for copy in trio:
            copy.start()
    for i, trio in enumerate(copies):
        for copy in trio:
            copy.wait()
        start, size = STRIPS[i]
        cols = slice(start, start + size)
        b = (m_buf[:, cols].astype(jnp.float32) + g_buf[:, cols].astype(jnp.float32)).astype(jnp.bfloat16)
        b_ref[:, cols] = b
        part = jnp.dot(b, s_buf[cols, :].astype(jnp.bfloat16), preferred_element_type=jnp.float32)
        if i == 0:
            part_ref[...] = part
        else:
            part_ref[...] += part


def project(momentum, gradient, subspace):
    momentum, gradient, subspace = [
        pltpu.with_memory_space_constraint(x, pltpu.HBM) for x in (momentum, gradient, subspace)
    ]
    return pl.pallas_call(
        project_kernel,
        in_specs=[HBM_SPEC] * 3,
        out_specs=[VMEM_SPEC] * 2,
        out_shape=[bf16(LOCAL_ROWS, LOCAL_COLS), f32(LOCAL_ROWS, RANK)],
        scratch_shapes=[
            VMEM((LOCAL_ROWS, LOCAL_COLS), jnp.bfloat16),
            VMEM((LOCAL_ROWS, LOCAL_COLS), jnp.bfloat16),
            VMEM((LOCAL_COLS, RANK), jnp.float32),
            pltpu.SemaphoreType.DMA((3, len(STRIPS))),
        ],
        compiler_params=PARAMS,
        cost_estimate=cost(2 * 256 * 3328 * 128, 7000000),
        name="project",
    )(momentum, gradient, subspace)


def local(kernel, out_shape, args, after=(), flops=0, nbytes=0, name=None, scratch=()):
    used = len(args)

    def body(*refs):
        kernel(*refs[:used], *refs[used + len(after):])

    single = not isinstance(out_shape, (list, tuple))
    return pl.pallas_call(
        body,
        in_specs=[VMEM_SPEC] * (used + len(after)),
        out_specs=VMEM_SPEC if single else [VMEM_SPEC] * len(out_shape),
        out_shape=out_shape,
        scratch_shapes=list(scratch),
        compiler_params=PARAMS,
        cost_estimate=cost(flops, nbytes),
        name=name,
    )(*args, *after)


def lift_half(p, b_ref, half, target):
    high = p.astype(jnp.bfloat16)
    low = (p - high.astype(jnp.float32)).astype(jnp.bfloat16)
    split = jnp.concatenate([high, low], axis=1)
    for k in range(HALF // 128):
        cols = pl.ds(pl.multiple_of(half * HALF + k * 128, 128), 128)
        d = lax.dot_general(b_ref[:, cols], split, TN, preferred_element_type=jnp.float32)
        target[k * 128:(k + 1) * 128, :] = d[:, :RANK] + d[:, RANK:]


def lift_send_kernel(p_ref, b_ref, send_ref):
    c = team(lax.axis_index("fsdp"))
    p = p_ref[...]
    lift_half(p, b_ref, 1 - c, send_ref)
    send_ref[HALF:, :] = lax.dot_general(
        p, p, TN, precision=lax.Precision.HIGHEST, preferred_element_type=jnp.float32
    )


def lift_keep_kernel(p_ref, b_ref, keep_ref):
    lift_half(p_ref[...], b_ref, team(lax.axis_index("fsdp")), keep_ref)


def split_kernel(k, n, keep_ref, recv_ref, send_ref, next_ref):
    bit = step_bit(k)
    away = pl.ds(pl.multiple_of((1 - bit) * n, 8), n)
    stay = pl.ds(pl.multiple_of(bit * n, 8), n)
    send_ref[...] = keep_ref[away, :] + recv_ref[away, :]
    next_ref[...] = keep_ref[stay, :] + recv_ref[stay, :]


def split_step(k, n, keep, recv, after=()):
    return local(
        functools.partial(split_kernel, k, n), [f32(n, RANK), f32(n, RANK)], [keep, recv], after,
        flops=n * 256, nbytes=n * 2048, name=f"split{k}",
    )


def add_kernel(a_ref, b_ref, out_ref):
    out_ref[...] = a_ref[...] + b_ref[...]


def gram_pair_kernel(sent_ref, recv_ref, out_ref):
    out_ref[...] = sent_ref[HALF:, :] + recv_ref[HALF:, :]


def gram_four_kernel(a_ref, b_ref, c_ref, d_ref, out_ref):
    out_ref[...] = (a_ref[...] + b_ref[...]) + (c_ref[...] + d_ref[...])


def hold_kernel(a_ref, out_ref):
    out_ref[...] = a_ref[...]


def add(a, b, after, name):
    return local(add_kernel, f32(*a.shape), [a, b], after, nbytes=3 * 4 * a.size, name=name)


def reciprocal(x):
    r = pl.reciprocal(x, approx=True)
    r = r * (2.0 - x * r)
    return r * (2.0 - x * r)


def unit_scale(rows, lane, sub):
    diagonal = jnp.zeros((8, RANK), jnp.float32)
    for k, row in enumerate(rows):
        diagonal = diagonal + jnp.where(lane == sub + 8 * k, row, 0.0)
    return lax.rsqrt(jnp.sum(diagonal, axis=0, keepdims=True))


def eliminate_kernel(start, stop, in_ref, gram_ref, out_ref):
    groups = RANK // 8
    lane = lax.broadcasted_iota(jnp.int32, (8, RANK), 1)
    sub = lax.broadcasted_iota(jnp.int32, (8, RANK), 0)

    def across(x):
        return jnp.broadcast_to(x, (8, RANK))

    t = [in_ref[8 * r:8 * r + 8, :] for r in range(groups)]
    if start == 0 or stop == RANK:
        gram = [gram_ref[8 * r:8 * r + 8, :] for r in range(groups)]
        scale = unit_scale(gram, lane, sub)
    if start == 0:
        for r in range(groups):
            own = jnp.sum(jnp.where(lane == sub + 8 * r, t[r], 0.0), axis=1, keepdims=True)
            t[r] = t[r] * lax.rsqrt(own) * scale
    for r in range(start // 8, stop // 8):
        cols = {
            k: [across(t[k][:, 8 * r + i:8 * r + i + 1]) for i in range(8)]
            for k in range(r, groups)
        }
        for i in range(0, 8, 2):
            j = 8 * r + i
            p, q = across(cols[r][i][i:i + 1, :]), across(cols[r][i][i + 1:i + 2, :])
            d = across(cols[r][i + 1][i + 1:i + 2, :])
            inv_p = reciprocal(p)
            inv_d = p * reciprocal(p * d - q * q)
            ratio = q * inv_p
            above = {n: across(cols[r][n][i:i + 1, :]) for n in range(i + 2, 8)}
            below = {n: across(cols[r][n][i + 1:i + 2, :]) - ratio * above[n] for n in above}
            at_j, at_next = lane == j, lane == j + 1
            unit_a = jnp.where(at_j, 1.0, across(t[r][i:i + 1, :]))
            new_b = jnp.where(at_j, 0.0, across(t[r][i + 1:i + 2, :])) - ratio * unit_a
            row_a = jnp.where(at_next, 0.0, unit_a)
            row_b = jnp.where(at_next, 1.0, new_b)
            either = at_j | at_next
            for k in range(r, groups):
                first = cols[k][i] * inv_p
                second = (cols[k][i + 1] - first * q) * inv_d
                if k == r:
                    first = jnp.where(sub > i, first, 0.0)
                    second = jnp.where(sub > i + 1, second, 0.0)
                for n in above:
                    cols[k][n] = cols[k][n] - first * above[n] - second * below[n]
                new = jnp.where(either, 0.0, t[k]) - first * row_a - second * row_b
                if k == r:
                    new = jnp.where(sub > i + 1, new, jnp.where(sub == i + 1, new_b, t[k]))
                t[k] = new
    for k in range(groups):
        if stop == RANK:
            row_of = sub + 8 * k
            pivot = jnp.sum(jnp.where(lane == row_of, t[k], 0.0), axis=1, keepdims=True)
            unit = jnp.where(lane < row_of, t[k], jnp.where(lane == row_of, 1.0, 0.0))
            out_ref[8 * k:8 * k + 8, :] = unit * lax.rsqrt(pivot) * scale
        else:
            out_ref[8 * k:8 * k + 8, :] = t[k]


def eliminate(start, stop, state, gram, after=()):
    return local(
        functools.partial(eliminate_kernel, start, stop), f32(RANK, RANK), [state, gram], after,
        flops=4000000, nbytes=(stop - start) * 150000, name=f"eliminate{start}",
    )


def block_kernel(keep_ref, recv_ref, w_ref, out_ref):
    w = w_ref[...].T
    w_high = w.astype(jnp.bfloat16)
    w_low = (w - w_high.astype(jnp.float32)).astype(jnp.bfloat16)
    both = jnp.concatenate([
        jnp.concatenate([w_high, w_low], axis=1),
        jnp.concatenate([w_high, jnp.zeros_like(w_low)], axis=1),
    ], axis=0)
    d = keep_ref[...] + recv_ref[...]
    high = d.astype(jnp.bfloat16)
    low = (d - high.astype(jnp.float32)).astype(jnp.bfloat16)
    out = jnp.dot(jnp.concatenate([high, low], axis=1), both, preferred_element_type=jnp.float32)
    out_ref[...] = (out[:, :RANK] + out[:, RANK:]).astype(jnp.bfloat16)


def ortho_kernel(p_ref, w_ref, out_ref):
    out_ref[...] = lax.dot_general(
        p_ref[...], w_ref[...], NT, precision=lax.Precision.HIGHEST, preferred_element_type=jnp.float32
    ).astype(jnp.bfloat16)


def join_kernel(k, n, mine_ref, recv_ref, out_ref):
    bit = step_bit(k)
    out_ref[pl.ds(pl.multiple_of(bit * n, 16), n), :] = mine_ref[...]
    out_ref[pl.ds(pl.multiple_of((1 - bit) * n, 16), n), :] = recv_ref[...]


def chunk_squares(ref, start):
    rows = ref[start:start + CHUNK, :].astype(jnp.float32)
    return jnp.sum((rows * rows).reshape(CHUNK // 8, 8, RANK), axis=0)


def squares_kernel(ref, out_ref):
    out_ref[...] = chunk_squares(ref, 0) + chunk_squares(ref, CHUNK)


def last_join_kernel(mine_ref, recv_ref, sq_ref, pair_ref, cross_ref, out_ref, sum_ref):
    join_kernel(0, 2 * CHUNK, mine_ref, recv_ref, out_ref)
    other = chunk_squares(recv_ref, 0) + chunk_squares(recv_ref, CHUNK)
    sum_ref[...] = (sq_ref[...] + other) + (pair_ref[...] + cross_ref[...])


def unpack_kernel(own_ref, other_ref, sq_ref, other_sq_ref, coef_ref, sum_ref):
    c = team(lax.axis_index("fsdp"))
    for source, half in ((own_ref, c), (other_ref, 1 - c)):
        for i in range(0, HALF, PIECE):
            rows = source[i:i + PIECE, :].astype(jnp.float32)
            coef_ref[pl.ds(pl.multiple_of(half * HALF + i, 8), PIECE), :] = rows
    sum_ref[...] = sq_ref[...] + other_sq_ref[...]


def momentum_kernel(coef_ref, ortho_ref, b_ref, mom_hbm, buf, sems):
    ortho = ortho_ref[...]
    copies = []
    for i in range(TILES):
        cols = slice(i * WIDE, (i + 1) * WIDE)
        feedback = lax.dot_general(
            ortho, coef_ref[cols, :].astype(jnp.bfloat16), NT, preferred_element_type=jnp.float32
        )
        buf[:, cols] = (
            b_ref[:, cols].astype(jnp.float32) - (1.0 - inertia) * feedback
        ).astype(jnp.bfloat16)
        at = pl.ds(i * WIDE, WIDE)
        copies.append(pltpu.make_async_copy(buf.at[:, at], mom_hbm.at[:, at], sems.at[i]))
        copies[-1].start()
    for copy in copies:
        copy.wait()


def finish_momentum(coef, ortho, blended):
    return pl.pallas_call(
        momentum_kernel,
        in_specs=[VMEM_SPEC] * 3,
        out_specs=HBM_SPEC,
        out_shape=bf16(LOCAL_ROWS, LOCAL_COLS),
        scratch_shapes=[
            VMEM((LOCAL_ROWS, LOCAL_COLS), jnp.bfloat16),
            pltpu.SemaphoreType.DMA((TILES,)),
        ],
        compiler_params=PARAMS,
        cost_estimate=cost(2 * 256 * 3328 * 128, 5000000),
        name="finish_momentum",
    )(coef, ortho, blended)


def weights_kernel(sq_ref, opposite_ref, next_ref, previous_ref, coef_ref, ortho_ref, weights_ref, new_hbm, sub_hbm, buf, sub_buf, sems):
    scaling = math.sqrt(ROWS * COLS / RANK)
    squares = (sq_ref[...] + opposite_ref[...]) + (next_ref[...] + previous_ref[...])
    norm = 1.0 / jnp.sqrt(jnp.sum(squares, axis=0, keepdims=True) + epsilon_sq)
    ortho = ortho_ref[...]
    copies = []
    for i in range(4):
        at = pl.ds(i * 2 * CHUNK, 2 * CHUNK)
        sub_buf[at, :] = coef_ref[at, :] * norm
        copies.append(pltpu.make_async_copy(sub_buf.at[at, :], sub_hbm.at[at, :], sems.at[0, i]))
        copies[-1].start()
    for i, (start, size) in enumerate(STRIPS):
        for first in range(start, start + size, WIDE):
            cols = slice(first, first + WIDE)
            update = lax.dot_general(
                ortho, sub_buf[cols, :].astype(jnp.bfloat16), NT, preferred_element_type=jnp.float32
            )
            buf[:, cols] = (
                weights_ref[:, cols].astype(jnp.float32) * (1.0 - step_size * shrinkage)
                - step_size * scaling * update
            ).astype(jnp.bfloat16)
        at = pl.ds(start, size)
        copies.append(pltpu.make_async_copy(buf.at[:, at], new_hbm.at[:, at], sems.at[1, i]))
        copies[-1].start()
    for copy in copies:
        copy.wait()


def finish_weights(squares, coef, ortho, weights):
    return pl.pallas_call(
        weights_kernel,
        in_specs=[VMEM_SPEC] * 7,
        out_specs=[HBM_SPEC] * 2,
        out_shape=[bf16(LOCAL_ROWS, LOCAL_COLS), f32(LOCAL_COLS, RANK)],
        scratch_shapes=[
            VMEM((LOCAL_ROWS, LOCAL_COLS), jnp.bfloat16),
            VMEM((LOCAL_COLS, RANK), jnp.float32),
            pltpu.SemaphoreType.DMA((2, len(STRIPS))),
        ],
        compiler_params=PARAMS,
        cost_estimate=cost(2 * 256 * 3328 * 128, 7000000),
        name="finish_weights",
    )(*squares, coef, ortho, weights)


def on_device(momentum, gradient, weights, subspace):
    blended, projected = project(momentum, gradient, subspace)
    for step in range(3):
        projected = projected + swap_z(projected, step)

    send = local(
        lift_send_kernel, f32(HALF + RANK, RANK), [projected, blended],
        flops=2 * 256 * 3328 * 128, nbytes=2000000, name="lift_send",
    )
    recv = xor_fsdp(send, CORE)
    keep = local(
        lift_keep_kernel, f32(HALF, RANK), [projected, blended], [send],
        flops=2 * 256 * 3328 * 128, nbytes=2000000, name="lift_keep",
    )
    n = HALF // 2
    moving, keep = split_step(0, n, keep, recv)
    gram = local(gram_pair_kernel, f32(RANK, RANK), [send, recv], [moving], nbytes=200000, name="gram_pair")
    recv = xor_step(moving, 0)
    gram = local(
        gram_four_kernel, f32(RANK, RANK),
        [gram] + [xor_fsdp(gram, mask) for mask in (X_THREE, Y_THREE, X_THREE ^ Y_THREE)],
        nbytes=400000, name="gram_four",
    )
    n //= 2
    moving, keep = split_step(1, n, keep, recv, [gram])
    recv = xor_step(moving, 1)
    gram = local(hold_kernel, f32(RANK, RANK), [gram], [moving], nbytes=130000, name="hold")
    more = xor_fsdp(gram, X_ONE)
    d = add(keep, recv, [more], "first_sum")
    recv = xor_step(d, 2)
    gram = add(gram, more, [d], "add_x1")
    more = xor_fsdp(gram, Y_ONE)
    d = add(d, recv, [more], "second_sum")
    recv = xor_step(d, 3)
    gram = add(gram, more, [d], "add_y1")
    inverse = eliminate(0, RANK, gram, gram)

    coef = local(
        block_kernel, bf16(CHUNK, RANK), [d, recv, inverse],
        flops=2 * CHUNK * 256 * 256, nbytes=700000, name="block",
    )
    ortho = local(
        ortho_kernel, bf16(LOCAL_ROWS, RANK), [projected, inverse], [coef],
        flops=6 * 256 * 256 * 128, nbytes=300000, name="ortho",
    )
    coef = local(
        functools.partial(join_kernel, 1, CHUNK), bf16(2 * CHUNK, RANK), [coef, xor_step(coef, 1)],
        [ortho], nbytes=CHUNK * 1024, name="join1",
    )

    recv = xor_step(coef, 0)
    squares = local(squares_kernel, f32(8, RANK), [coef], flops=CHUNK * 512, nbytes=400000, name="squares")
    coef, squares = local(
        last_join_kernel, [bf16(HALF, RANK), f32(8, RANK)],
        [coef, recv, squares, pair_z(squares, False), pair_z(squares, True)],
        nbytes=CHUNK * 4096, name="join0",
    )
    coef, squares = local(
        unpack_kernel, [f32(LOCAL_COLS, RANK), f32(8, RANK)],
        [coef, xor_fsdp(coef, CORE), squares, xor_fsdp(squares, CORE)],
        flops=3328 * 128, nbytes=2600000, name="unpack",
    )
    squares = [squares] + [turn_z(squares, to_odd, to_even) for to_odd, to_even in Z_TURNS]
    new_momentum = finish_momentum(coef, ortho, blended)
    new_weights, new_subspace = finish_weights(squares, coef, ortho, weights)
    return (new_momentum, new_weights, new_subspace)


def solution(mesh):
    placed = (P("fsdp", "tp"), P("fsdp", "tp"), P("fsdp", "tp"), P("tp", None))
    return jax.shard_map(
        on_device,
        mesh=mesh,
        in_specs=placed,
        out_specs=(P("fsdp", "tp"), P("fsdp", "tp"), P("tp", None)),
        check_vma=False,
    )
```

```python
import functools
import math

import jax
import jax.numpy as jnp
from jax import lax
from jax.experimental import pallas as pl
from jax.experimental.pallas import tpu as pltpu
from jax.sharding import PartitionSpec as P

ROWS = 8192
COLS = 26624
RANK = 128

inertia = 0.95
step_size = 0.5
shrinkage = 0.1
epsilon_sq = 1e-06

LOCAL_ROWS = 256
LOCAL_COLS = 3328
TP = 8
FSDP = 32
HALF = LOCAL_COLS // 2
CHUNK = HALF // 4
PIECE = HALF // 8
CUT = 40
WIDE = 256
TILES = LOCAL_COLS // WIDE
STRIPS = ((0, 512), (512, 768), (1280, 768), (2048, 768), (2816, 512))

X_ONE, Y_ONE, X_THREE, Y_THREE, CORE = 3, 9, 7, 25, 1
MASKS = ((X_ONE, X_THREE, Y_THREE, Y_ONE), (Y_ONE, Y_THREE, X_THREE, X_ONE))


def team(f):
    return (f % 2 + f // 2 + f // 8) % 2


Z_PAIRS = (
    ((0, 1), (2, 3), (4, 5), (6, 7)),
    ((1, 2), (3, 4), (5, 6), (7, 0)),
    ((2, 5), (1, 6), (4, 7), (3, 0)),
)

VMEM = pltpu.VMEM
VMEM_SPEC = pl.BlockSpec(memory_space=pltpu.VMEM)
HBM_SPEC = pl.BlockSpec(memory_space=pltpu.HBM)
PARAMS = pltpu.CompilerParams(vmem_limit_bytes=24 * 1024 * 1024)
NT = (((1,), (1,)), ((), ()))
TN = (((0,), (0,)), ((), ()))


def f32(*shape):
    return jax.ShapeDtypeStruct(shape, jnp.float32)


def bf16(*shape):
    return jax.ShapeDtypeStruct(shape, jnp.bfloat16)


def cost(flops, nbytes):
    return pl.CostEstimate(flops=flops, bytes_accessed=nbytes, transcendentals=0)

def swap_z(x, step):
    perm = []
    for f in range(FSDP):
        for a, b in Z_PAIRS[step]:
            one, two = f * TP + (a + f % 2) % TP, f * TP + (b + f % 2) % TP
            perm += [(one, two), (two, one)]
    return lax.ppermute(x, ("fsdp", "tp"), perm)


def pair_z(x, cross):
    perm = [
        (f * TP + z, (f ^ (MASKS[team(f)][0] if cross else 0)) * TP + (z ^ 1))
        for f in range(FSDP) for z in range(TP)
    ]
    return lax.ppermute(x, ("fsdp", "tp"), perm)


def turn_z(x, turns):
    perm = [
        ((f ^ 1) * TP + (z + turns[f % 2] * (1 if z % 2 else -1)) % TP, f * TP + z)
        for f in range(FSDP) for z in range(TP)
    ]
    return lax.ppermute(x, ("fsdp", "tp"), perm)


def xor_fsdp(x, mask):
    return lax.ppermute(x, "fsdp", [(i, i ^ mask) for i in range(FSDP)])


def split_xy(x, x_mask, y_mask):
    split = [(f ^ (y_mask if f % 2 else x_mask), f) for f in range(FSDP)]
    return lax.ppermute(x, "fsdp", split), xor_fsdp(x, x_mask ^ y_mask)


def xor_step(x, k):
    return lax.ppermute(x, "fsdp", [(i, i ^ MASKS[team(i)][k]) for i in range(FSDP)])


def step_bit(k):
    f = lax.axis_index("fsdp")
    place = jnp.where(team(f) == 0, (f // 2) % 4, f // 8)
    return place // 2 if k else place % 2 ^ place // 2


def project_kernel(m_hbm, g_hbm, s_hbm, b_ref, part_ref, m_buf, g_buf, s_buf, sems):
    copies = []
    for i, (start, size) in enumerate(STRIPS):
        cols = pl.ds(start, size)
        copies.append((
            pltpu.make_async_copy(m_hbm.at[:, cols], m_buf.at[:, cols], sems.at[0, i]),
            pltpu.make_async_copy(g_hbm.at[:, cols], g_buf.at[:, cols], sems.at[1, i]),
            pltpu.make_async_copy(s_hbm.at[cols, :], s_buf.at[cols, :], sems.at[2, i]),
        ))
    for trio in copies:
        for copy in trio:
            copy.start()
    for i, trio in enumerate(copies):
        for copy in trio:
            copy.wait()
        start, size = STRIPS[i]
        cols = slice(start, start + size)
        b = (m_buf[:, cols].astype(jnp.float32) + g_buf[:, cols].astype(jnp.float32)).astype(jnp.bfloat16)
        b_ref[:, cols] = b
        part = jnp.dot(b, s_buf[cols, :].astype(jnp.bfloat16), preferred_element_type=jnp.float32)
        if i == 0:
            part_ref[...] = part
        else:
            part_ref[...] += part


def project(momentum, gradient, subspace):
    momentum, gradient, subspace = [
        pltpu.with_memory_space_constraint(x, pltpu.HBM) for x in (momentum, gradient, subspace)
    ]
    return pl.pallas_call(
        project_kernel,
        in_specs=[HBM_SPEC] * 3,
        out_specs=[VMEM_SPEC] * 2,
        out_shape=[bf16(LOCAL_ROWS, LOCAL_COLS), f32(LOCAL_ROWS, RANK)],
        scratch_shapes=[
            VMEM((LOCAL_ROWS, LOCAL_COLS), jnp.bfloat16),
            VMEM((LOCAL_ROWS, LOCAL_COLS), jnp.bfloat16),
            VMEM((LOCAL_COLS, RANK), jnp.float32),
            pltpu.SemaphoreType.DMA((3, len(STRIPS))),
        ],
        compiler_params=PARAMS,
        cost_estimate=cost(2 * 256 * 3328 * 128, 7000000),
        name="project",
    )(momentum, gradient, subspace)


def local(kernel, out_shape, args, after=(), flops=0, nbytes=0, name=None, scratch=()):
    used = len(args)

    def body(*refs):
        kernel(*refs[:used], *refs[used + len(after):])

    single = not isinstance(out_shape, (list, tuple))
    return pl.pallas_call(
        body,
        in_specs=[VMEM_SPEC] * (used + len(after)),
        out_specs=VMEM_SPEC if single else [VMEM_SPEC] * len(out_shape),
        out_shape=out_shape,
        scratch_shapes=list(scratch),
        compiler_params=PARAMS,
        cost_estimate=cost(flops, nbytes),
        name=name,
    )(*args, *after)


def lift_half(p, b_ref, half, target):
    high = p.astype(jnp.bfloat16)
    low = (p - high.astype(jnp.float32)).astype(jnp.bfloat16)
    split = jnp.concatenate([high, low], axis=1)
    for k in range(HALF // 128):
        cols = pl.ds(pl.multiple_of(half * HALF + k * 128, 128), 128)
        d = lax.dot_general(b_ref[:, cols], split, TN, preferred_element_type=jnp.float32)
        target[k * 128:(k + 1) * 128, :] = d[:, :RANK] + d[:, RANK:]


def lift_send_kernel(p_ref, b_ref, send_ref):
    c = team(lax.axis_index("fsdp"))
    p = p_ref[...]
    lift_half(p, b_ref, 1 - c, send_ref)
    send_ref[HALF:, :] = lax.dot_general(
        p, p, TN, precision=lax.Precision.HIGHEST, preferred_element_type=jnp.float32
    )


def lift_keep_kernel(p_ref, b_ref, keep_ref):
    lift_half(p_ref[...], b_ref, team(lax.axis_index("fsdp")), keep_ref)


def split_kernel(k, n, keep_ref, recv_ref, send_ref, next_ref):
    bit = step_bit(k)
    away = pl.ds(pl.multiple_of((1 - bit) * n, 8), n)
    stay = pl.ds(pl.multiple_of(bit * n, 8), n)
    send_ref[...] = keep_ref[away, :] + recv_ref[away, :]
    next_ref[...] = keep_ref[stay, :] + recv_ref[stay, :]


def split_step(k, n, keep, recv, after=()):
    return local(
        functools.partial(split_kernel, k, n), [f32(n, RANK), f32(n, RANK)], [keep, recv], after,
        flops=n * 256, nbytes=n * 2048, name=f"split{k}",
    )


def add_kernel(a_ref, b_ref, out_ref):
    out_ref[...] = a_ref[...] + b_ref[...]


def gram_pair_kernel(sent_ref, recv_ref, out_ref):
    out_ref[...] = sent_ref[HALF:, :] + recv_ref[HALF:, :]


def gram_four_kernel(a_ref, b_ref, c_ref, d_ref, out_ref):
    out_ref[...] = (a_ref[...] + b_ref[...]) + (c_ref[...] + d_ref[...])


def gram_four(a, b, c, d, after):
    return local(gram_four_kernel, f32(RANK, RANK), [a, b, c, d], after, nbytes=400000, name="gram_four")


def hold_kernel(a_ref, out_ref):
    out_ref[...] = a_ref[...]


def add(a, b, after, name):
    return local(add_kernel, f32(*a.shape), [a, b], after, nbytes=3 * 4 * a.size, name=name)


def reciprocal(x):
    r = pl.reciprocal(x, approx=True)
    r = r * (2.0 - x * r)
    return r * (2.0 - x * r)


def unit_scale(rows, lane, sub):
    diagonal = jnp.zeros((8, RANK), jnp.float32)
    for k, row in enumerate(rows):
        diagonal = diagonal + jnp.where(lane == sub + 8 * k, row, 0.0)
    return lax.rsqrt(jnp.sum(diagonal, axis=0, keepdims=True))


def eliminate_kernel(start, stop, in_ref, gram_ref, out_ref):
    groups = RANK // 8
    lane = lax.broadcasted_iota(jnp.int32, (8, RANK), 1)
    sub = lax.broadcasted_iota(jnp.int32, (8, RANK), 0)

    def across(x):
        return jnp.broadcast_to(x, (8, RANK))

    t = [in_ref[8 * r:8 * r + 8, :] for r in range(groups)]
    if start == 0 or stop == RANK:
        gram = [gram_ref[8 * r:8 * r + 8, :] for r in range(groups)]
        scale = unit_scale(gram, lane, sub)
    if start == 0:
        for r in range(groups):
            own = jnp.sum(jnp.where(lane == sub + 8 * r, t[r], 0.0), axis=1, keepdims=True)
            t[r] = t[r] * lax.rsqrt(own) * scale
    for r in range(start // 8, stop // 8):
        cols = {
            k: [across(t[k][:, 8 * r + i:8 * r + i + 1]) for i in range(8)]
            for k in range(r, groups)
        }
        for i in range(0, 8, 2):
            j = 8 * r + i
            p, q = across(cols[r][i][i:i + 1, :]), across(cols[r][i][i + 1:i + 2, :])
            d = across(cols[r][i + 1][i + 1:i + 2, :])
            inv_p = reciprocal(p)
            inv_d = p * reciprocal(p * d - q * q)
            ratio = q * inv_p
            above = {n: across(cols[r][n][i:i + 1, :]) for n in range(i + 2, 8)}
            below = {n: across(cols[r][n][i + 1:i + 2, :]) - ratio * above[n] for n in above}
            at_j, at_next = lane == j, lane == j + 1
            unit_a = jnp.where(at_j, 1.0, across(t[r][i:i + 1, :]))
            new_b = jnp.where(at_j, 0.0, across(t[r][i + 1:i + 2, :])) - ratio * unit_a
            row_a = jnp.where(at_next, 0.0, unit_a)
            row_b = jnp.where(at_next, 1.0, new_b)
            either = at_j | at_next
            for k in range(r, groups):
                first = cols[k][i] * inv_p
                second = (cols[k][i + 1] - first * q) * inv_d
                if k == r:
                    first = jnp.where(sub > i, first, 0.0)
                    second = jnp.where(sub > i + 1, second, 0.0)
                for n in above:
                    cols[k][n] = cols[k][n] - first * above[n] - second * below[n]
                new = jnp.where(either, 0.0, t[k]) - first * row_a - second * row_b
                if k == r:
                    new = jnp.where(sub > i + 1, new, jnp.where(sub == i + 1, new_b, t[k]))
                t[k] = new
    for k in range(groups):
        if stop == RANK:
            row_of = sub + 8 * k
            pivot = jnp.sum(jnp.where(lane == row_of, t[k], 0.0), axis=1, keepdims=True)
            unit = jnp.where(lane < row_of, t[k], jnp.where(lane == row_of, 1.0, 0.0))
            out_ref[8 * k:8 * k + 8, :] = unit * lax.rsqrt(pivot) * scale
        else:
            out_ref[8 * k:8 * k + 8, :] = t[k]


def eliminate(start, stop, state, gram, after=()):
    return local(
        functools.partial(eliminate_kernel, start, stop), f32(RANK, RANK), [state, gram], after,
        flops=4000000, nbytes=(stop - start) * 150000, name=f"eliminate{start}",
    )


def block_kernel(keep_ref, recv_ref, w_ref, out_ref):
    w = w_ref[...].T
    w_high = w.astype(jnp.bfloat16)
    w_low = (w - w_high.astype(jnp.float32)).astype(jnp.bfloat16)
    both = jnp.concatenate([
        jnp.concatenate([w_high, w_low], axis=1),
        jnp.concatenate([w_high, jnp.zeros_like(w_low)], axis=1),
    ], axis=0)
    d = keep_ref[...] + recv_ref[...]
    high = d.astype(jnp.bfloat16)
    low = (d - high.astype(jnp.float32)).astype(jnp.bfloat16)
    out = jnp.dot(jnp.concatenate([high, low], axis=1), both, preferred_element_type=jnp.float32)
    out_ref[...] = (out[:, :RANK] + out[:, RANK:]).astype(jnp.bfloat16)


def ortho_kernel(p_ref, w_ref, out_ref):
    out_ref[...] = lax.dot_general(
        p_ref[...], w_ref[...], NT, precision=lax.Precision.HIGHEST, preferred_element_type=jnp.float32
    ).astype(jnp.bfloat16)


def join_kernel(k, n, mine_ref, recv_ref, out_ref):
    bit = step_bit(k)
    out_ref[pl.ds(pl.multiple_of(bit * n, 16), n), :] = mine_ref[...]
    out_ref[pl.ds(pl.multiple_of((1 - bit) * n, 16), n), :] = recv_ref[...]


def chunk_squares(ref, start):
    rows = ref[start:start + CHUNK, :].astype(jnp.float32)
    return jnp.sum((rows * rows).reshape(CHUNK // 8, 8, RANK), axis=0)


def squares_kernel(ref, out_ref):
    out_ref[...] = chunk_squares(ref, 0) + chunk_squares(ref, CHUNK)


def last_join_kernel(mine_ref, recv_ref, sq_ref, pair_ref, cross_ref, out_ref, sum_ref):
    join_kernel(0, 2 * CHUNK, mine_ref, recv_ref, out_ref)
    other = chunk_squares(recv_ref, 0) + chunk_squares(recv_ref, CHUNK)
    sum_ref[...] = (sq_ref[...] + other) + (pair_ref[...] + cross_ref[...])


def unpack_kernel(own_ref, other_ref, sq_ref, other_sq_ref, coef_ref, sum_ref):
    c = team(lax.axis_index("fsdp"))
    for source, half in ((own_ref, c), (other_ref, 1 - c)):
        for i in range(0, HALF, PIECE):
            rows = source[i:i + PIECE, :].astype(jnp.float32)
            coef_ref[pl.ds(pl.multiple_of(half * HALF + i, 8), PIECE), :] = rows
    sum_ref[...] = sq_ref[...] + other_sq_ref[...]


def momentum_kernel(coef_ref, ortho_ref, b_ref, mom_hbm, buf, sems):
    ortho = ortho_ref[...]
    copies = []
    for i in range(TILES):
        cols = slice(i * WIDE, (i + 1) * WIDE)
        feedback = lax.dot_general(
            ortho, coef_ref[cols, :].astype(jnp.bfloat16), NT, preferred_element_type=jnp.float32
        )
        buf[:, cols] = (
            b_ref[:, cols].astype(jnp.float32) - (1.0 - inertia) * feedback
        ).astype(jnp.bfloat16)
        at = pl.ds(i * WIDE, WIDE)
        copies.append(pltpu.make_async_copy(buf.at[:, at], mom_hbm.at[:, at], sems.at[i]))
        copies[-1].start()
    for copy in copies:
        copy.wait()


def finish_momentum(coef, ortho, blended):
    return pl.pallas_call(
        momentum_kernel,
        in_specs=[VMEM_SPEC] * 3,
        out_specs=HBM_SPEC,
        out_shape=bf16(LOCAL_ROWS, LOCAL_COLS),
        scratch_shapes=[
            VMEM((LOCAL_ROWS, LOCAL_COLS), jnp.bfloat16),
            pltpu.SemaphoreType.DMA((TILES,)),
        ],
        compiler_params=PARAMS,
        cost_estimate=cost(2 * 256 * 3328 * 128, 5000000),
        name="finish_momentum",
    )(coef, ortho, blended)


def weights_kernel(sq_ref, opposite_ref, next_ref, previous_ref, coef_ref, ortho_ref, weights_ref, new_hbm, sub_hbm, buf, sub_buf, sems):
    scaling = math.sqrt(ROWS * COLS / RANK)
    squares = (sq_ref[...] + opposite_ref[...]) + (next_ref[...] + previous_ref[...])
    norm = 1.0 / jnp.sqrt(jnp.sum(squares, axis=0, keepdims=True) + epsilon_sq)
    ortho = ortho_ref[...]
    copies = []
    for i in range(4):
        at = pl.ds(i * 2 * CHUNK, 2 * CHUNK)
        sub_buf[at, :] = coef_ref[at, :] * norm
        copies.append(pltpu.make_async_copy(sub_buf.at[at, :], sub_hbm.at[at, :], sems.at[0, i]))
        copies[-1].start()
    for i, (start, size) in enumerate(STRIPS):
        for first in range(start, start + size, WIDE):
            cols = slice(first, first + WIDE)
            update = lax.dot_general(
                ortho, sub_buf[cols, :].astype(jnp.bfloat16), NT, preferred_element_type=jnp.float32
            )
            buf[:, cols] = (
                weights_ref[:, cols].astype(jnp.float32) * (1.0 - step_size * shrinkage)
                - step_size * scaling * update
            ).astype(jnp.bfloat16)
        at = pl.ds(start, size)
        copies.append(pltpu.make_async_copy(buf.at[:, at], new_hbm.at[:, at], sems.at[1, i]))
        copies[-1].start()
    for copy in copies:
        copy.wait()


def finish_weights(squares, coef, ortho, weights):
    return pl.pallas_call(
        weights_kernel,
        in_specs=[VMEM_SPEC] * 7,
        out_specs=[HBM_SPEC] * 2,
        out_shape=[bf16(LOCAL_ROWS, LOCAL_COLS), f32(LOCAL_COLS, RANK)],
        scratch_shapes=[
            VMEM((LOCAL_ROWS, LOCAL_COLS), jnp.bfloat16),
            VMEM((LOCAL_COLS, RANK), jnp.float32),
            pltpu.SemaphoreType.DMA((2, len(STRIPS))),
        ],
        compiler_params=PARAMS,
        cost_estimate=cost(2 * 256 * 3328 * 128, 7000000),
        name="finish_weights",
    )(*squares, coef, ortho, weights)


def on_device(momentum, gradient, weights, subspace):
    blended, projected = project(momentum, gradient, subspace)
    for step in range(3):
        projected = projected + swap_z(projected, step)

    send = local(
        lift_send_kernel, f32(HALF + RANK, RANK), [projected, blended],
        flops=2 * 256 * 3328 * 128, nbytes=2000000, name="lift_send",
    )
    recv = xor_fsdp(send, CORE)
    keep = local(
        lift_keep_kernel, f32(HALF, RANK), [projected, blended], [send],
        flops=2 * 256 * 3328 * 128, nbytes=2000000, name="lift_keep",
    )
    n = HALF // 2
    moving, keep = split_step(0, n, keep, recv)
    gram = local(gram_pair_kernel, f32(RANK, RANK), [send, recv], [moving], nbytes=200000, name="gram_pair")
    recv = xor_step(moving, 0)
    split, both = split_xy(gram, X_THREE, Y_THREE)
    gram = gram_four(gram, both, split, xor_fsdp(split, CORE), [])
    n //= 2
    moving, keep = split_step(1, n, keep, recv, [gram])
    recv = xor_step(moving, 1)
    gram = local(hold_kernel, f32(RANK, RANK), [gram], [moving], nbytes=130000, name="hold")
    split, both = split_xy(gram, X_ONE, Y_ONE)
    d = add(keep, recv, [split, both], "first_sum")
    recv = xor_step(d, 2)
    split = local(hold_kernel, f32(RANK, RANK), [split], [d], nbytes=130000, name="hold_split")
    gram = gram_four(gram, both, split, xor_fsdp(split, CORE), [d])
    state = eliminate(0, CUT, gram, gram)
    d = add(d, recv, [state], "second_sum")
    recv = xor_step(d, 3)
    inverse = eliminate(CUT, RANK, state, gram, [d])

    coef = local(
        block_kernel, bf16(CHUNK, RANK), [d, recv, inverse],
        flops=2 * CHUNK * 256 * 256, nbytes=700000, name="block",
    )
    ortho = local(
        ortho_kernel, bf16(LOCAL_ROWS, RANK), [projected, inverse], [coef],
        flops=6 * 256 * 256 * 128, nbytes=300000, name="ortho",
    )
    coef = local(
        functools.partial(join_kernel, 1, CHUNK), bf16(2 * CHUNK, RANK), [coef, xor_step(coef, 1)],
        [ortho], nbytes=CHUNK * 1024, name="join1",
    )

    recv = xor_step(coef, 0)
    squares = local(squares_kernel, f32(8, RANK), [coef], flops=CHUNK * 512, nbytes=400000, name="squares")
    coef, squares = local(
        last_join_kernel, [bf16(HALF, RANK), f32(8, RANK)],
        [coef, recv, squares, pair_z(squares, False), pair_z(squares, True)],
        nbytes=CHUNK * 4096, name="join0",
    )
    coef, squares = local(
        unpack_kernel, [f32(LOCAL_COLS, RANK), f32(8, RANK)],
        [coef, xor_fsdp(coef, CORE), squares, xor_fsdp(squares, CORE)],
        flops=3328 * 128, nbytes=2600000, name="unpack",
    )
    split = turn_z(squares, (1, -2))
    squares = [squares, turn_z(squares, (3, 3)), split, xor_fsdp(split, CORE)]
    new_momentum = finish_momentum(coef, ortho, blended)
    new_weights, new_subspace = finish_weights(squares, coef, ortho, weights)
    return (new_momentum, new_weights, new_subspace)


def solution(mesh):
    placed = (P("fsdp", "tp"), P("fsdp", "tp"), P("fsdp", "tp"), P("tp", None))
    return jax.shard_map(
        on_device,
        mesh=mesh,
        in_specs=placed,
        out_specs=(P("fsdp", "tp"), P("fsdp", "tp"), P("tp", None)),
        check_vma=False,
    )
```

```python
import functools
import math

import jax
import jax.numpy as jnp
from jax import lax
from jax.experimental import pallas as pl
from jax.experimental.pallas import tpu as pltpu
from jax.sharding import PartitionSpec as P

ROWS = 8192
COLS = 26624
RANK = 128

inertia = 0.95
step_size = 0.5
shrinkage = 0.1
epsilon_sq = 1e-06

LOCAL_ROWS = 256
LOCAL_COLS = 3328
TP = 8
FSDP = 32
HALF = LOCAL_COLS // 2
CHUNK = HALF // 4
PIECE = HALF // 8
CUT = 40
WIDE = 256
TILES = LOCAL_COLS // WIDE
STRIPS = ((0, 512), (512, 768), (1280, 768), (2048, 768), (2816, 512))

X_ONE, Y_ONE, X_THREE, Y_THREE, CORE = 3, 9, 7, 25, 1
MASKS = ((X_ONE, X_THREE, Y_THREE, Y_ONE), (Y_ONE, Y_THREE, X_THREE, X_ONE))


def team(f):
    return (f % 2 + f // 2 + f // 8) % 2


Z_PAIRS = (
    ((0, 1), (2, 3), (4, 5), (6, 7)),
    ((1, 2), (3, 4), (5, 6), (7, 0)),
    ((2, 5), (1, 6), (4, 7), (3, 0)),
)

VMEM = pltpu.VMEM
VMEM_SPEC = pl.BlockSpec(memory_space=pltpu.VMEM)
HBM_SPEC = pl.BlockSpec(memory_space=pltpu.HBM)
PARAMS = pltpu.CompilerParams(vmem_limit_bytes=24 * 1024 * 1024)
NT = (((1,), (1,)), ((), ()))
TN = (((0,), (0,)), ((), ()))


def f32(*shape):
    return jax.ShapeDtypeStruct(shape, jnp.float32)


def bf16(*shape):
    return jax.ShapeDtypeStruct(shape, jnp.bfloat16)


def cost(flops, nbytes):
    return pl.CostEstimate(flops=flops, bytes_accessed=nbytes, transcendentals=0)

def swap_z(x, step):
    perm = []
    for f in range(FSDP):
        for a, b in Z_PAIRS[step]:
            one, two = f * TP + (a + f % 2) % TP, f * TP + (b + f % 2) % TP
            perm += [(one, two), (two, one)]
    return lax.ppermute(x, ("fsdp", "tp"), perm)


def pair_z(x, cross):
    perm = [
        (f * TP + z, (f ^ (MASKS[team(f)][0] if cross else 0)) * TP + (z ^ 1))
        for f in range(FSDP) for z in range(TP)
    ]
    return lax.ppermute(x, ("fsdp", "tp"), perm)


def turn_z(x, turns):
    perm = [
        ((f ^ 1) * TP + (z + turns[f % 2] * (1 if z % 2 else -1)) % TP, f * TP + z)
        for f in range(FSDP) for z in range(TP)
    ]
    return lax.ppermute(x, ("fsdp", "tp"), perm)


def xor_fsdp(x, mask):
    return lax.ppermute(x, "fsdp", [(i, i ^ mask) for i in range(FSDP)])


def split_xy(x, x_mask, y_mask):
    split = [(f ^ (y_mask if f % 2 else x_mask), f) for f in range(FSDP)]
    return lax.ppermute(x, "fsdp", split), xor_fsdp(x, x_mask ^ y_mask)


def xor_step(x, k):
    return lax.ppermute(x, "fsdp", [(i, i ^ MASKS[team(i)][k]) for i in range(FSDP)])


def step_bit(k):
    f = lax.axis_index("fsdp")
    place = jnp.where(team(f) == 0, (f // 2) % 4, f // 8)
    return place // 2 if k else place % 2 ^ place // 2


def project_kernel(m_hbm, g_hbm, s_hbm, b_ref, part_ref, m_buf, g_buf, s_buf, sems):
    copies = []
    for i, (start, size) in enumerate(STRIPS):
        cols = pl.ds(start, size)
        copies.append((
            pltpu.make_async_copy(m_hbm.at[:, cols], m_buf.at[:, cols], sems.at[0, i]),
            pltpu.make_async_copy(g_hbm.at[:, cols], g_buf.at[:, cols], sems.at[1, i]),
            pltpu.make_async_copy(s_hbm.at[cols, :], s_buf.at[cols, :], sems.at[2, i]),
        ))
    for trio in copies:
        for copy in trio:
            copy.start()
    for i, trio in enumerate(copies):
        for copy in trio:
            copy.wait()
        start, size = STRIPS[i]
        cols = slice(start, start + size)
        b = (m_buf[:, cols].astype(jnp.float32) + g_buf[:, cols].astype(jnp.float32)).astype(jnp.bfloat16)
        b_ref[:, cols] = b
        part = jnp.dot(b, s_buf[cols, :].astype(jnp.bfloat16), preferred_element_type=jnp.float32)
        if i == 0:
            part_ref[...] = part
        else:
            part_ref[...] += part


def project(momentum, gradient, subspace):
    momentum, gradient, subspace = [
        pltpu.with_memory_space_constraint(x, pltpu.HBM) for x in (momentum, gradient, subspace)
    ]
    return pl.pallas_call(
        project_kernel,
        in_specs=[HBM_SPEC] * 3,
        out_specs=[VMEM_SPEC] * 2,
        out_shape=[bf16(LOCAL_ROWS, LOCAL_COLS), f32(LOCAL_ROWS, RANK)],
        scratch_shapes=[
            VMEM((LOCAL_ROWS, LOCAL_COLS), jnp.bfloat16),
            VMEM((LOCAL_ROWS, LOCAL_COLS), jnp.bfloat16),
            VMEM((LOCAL_COLS, RANK), jnp.float32),
            pltpu.SemaphoreType.DMA((3, len(STRIPS))),
        ],
        compiler_params=PARAMS,
        cost_estimate=cost(2 * 256 * 3328 * 128, 7000000),
        name="project",
    )(momentum, gradient, subspace)


def local(kernel, out_shape, args, after=(), flops=0, nbytes=0, name=None, scratch=()):
    used = len(args)

    def body(*refs):
        kernel(*refs[:used], *refs[used + len(after):])

    single = not isinstance(out_shape, (list, tuple))
    return pl.pallas_call(
        body,
        in_specs=[VMEM_SPEC] * (used + len(after)),
        out_specs=VMEM_SPEC if single else [VMEM_SPEC] * len(out_shape),
        out_shape=out_shape,
        scratch_shapes=list(scratch),
        compiler_params=PARAMS,
        cost_estimate=cost(flops, nbytes),
        name=name,
    )(*args, *after)


def lift_half(p, b_ref, half, target):
    high = p.astype(jnp.bfloat16)
    low = (p - high.astype(jnp.float32)).astype(jnp.bfloat16)
    split = jnp.concatenate([high, low], axis=1)
    for k in range(HALF // 128):
        cols = pl.ds(pl.multiple_of(half * HALF + k * 128, 128), 128)
        d = lax.dot_general(b_ref[:, cols], split, TN, preferred_element_type=jnp.float32)
        target[k * 128:(k + 1) * 128, :] = d[:, :RANK] + d[:, RANK:]


def lift_send_kernel(p_ref, b_ref, send_ref):
    c = team(lax.axis_index("fsdp"))
    p = p_ref[...]
    lift_half(p, b_ref, 1 - c, send_ref)
    send_ref[HALF:, :] = lax.dot_general(
        p, p, TN, precision=lax.Precision.HIGHEST, preferred_element_type=jnp.float32
    )


def lift_keep_kernel(p_ref, b_ref, keep_ref):
    lift_half(p_ref[...], b_ref, team(lax.axis_index("fsdp")), keep_ref)


def split_kernel(k, n, keep_ref, recv_ref, send_ref, next_ref):
    bit = step_bit(k)
    away = pl.ds(pl.multiple_of((1 - bit) * n, 8), n)
    stay = pl.ds(pl.multiple_of(bit * n, 8), n)
    send_ref[...] = keep_ref[away, :] + recv_ref[away, :]
    next_ref[...] = keep_ref[stay, :] + recv_ref[stay, :]


def split_step(k, n, keep, recv, after=()):
    return local(
        functools.partial(split_kernel, k, n), [f32(n, RANK), f32(n, RANK)], [keep, recv], after,
        flops=n * 256, nbytes=n * 2048, name=f"split{k}",
    )


def add_kernel(a_ref, b_ref, out_ref):
    out_ref[...] = a_ref[...] + b_ref[...]


def gram_pair_kernel(sent_ref, recv_ref, out_ref):
    out_ref[...] = sent_ref[HALF:, :] + recv_ref[HALF:, :]


def gram_four_kernel(a_ref, b_ref, c_ref, d_ref, out_ref):
    out_ref[...] = (a_ref[...] + b_ref[...]) + (c_ref[...] + d_ref[...])


def gram_four(a, b, c, d, after):
    return local(gram_four_kernel, f32(RANK, RANK), [a, b, c, d], after, nbytes=400000, name="gram_four")


def hold_kernel(a_ref, out_ref):
    out_ref[...] = a_ref[...]


def add(a, b, after, name):
    return local(add_kernel, f32(*a.shape), [a, b], after, nbytes=3 * 4 * a.size, name=name)


def reciprocal(x):
    r = pl.reciprocal(x, approx=True)
    r = r * (2.0 - x * r)
    return r * (2.0 - x * r)


def unit_scale(rows, lane, sub):
    diagonal = jnp.zeros((8, RANK), jnp.float32)
    for k, row in enumerate(rows):
        diagonal = diagonal + jnp.where(lane == sub + 8 * k, row, 0.0)
    return lax.rsqrt(jnp.sum(diagonal, axis=0, keepdims=True))


def eliminate_kernel(start, stop, in_ref, gram_ref, out_ref):
    groups = RANK // 8
    lane = lax.broadcasted_iota(jnp.int32, (8, RANK), 1)
    sub = lax.broadcasted_iota(jnp.int32, (8, RANK), 0)

    def across(x):
        return jnp.broadcast_to(x, (8, RANK))

    t = [in_ref[8 * r:8 * r + 8, :] for r in range(groups)]
    if start == 0 or stop == RANK:
        gram = [gram_ref[8 * r:8 * r + 8, :] for r in range(groups)]
        scale = unit_scale(gram, lane, sub)
    if start == 0:
        for r in range(groups):
            own = jnp.sum(jnp.where(lane == sub + 8 * r, t[r], 0.0), axis=1, keepdims=True)
            t[r] = t[r] * lax.rsqrt(own) * scale
    for r in range(start // 8, stop // 8):
        cols = {
            k: [across(t[k][:, 8 * r + i:8 * r + i + 1]) for i in range(8)]
            for k in range(r, groups)
        }
        for i in range(0, 8, 2):
            j = 8 * r + i
            p, q = across(cols[r][i][i:i + 1, :]), across(cols[r][i][i + 1:i + 2, :])
            d = across(cols[r][i + 1][i + 1:i + 2, :])
            inv_p = reciprocal(p)
            inv_d = p * reciprocal(p * d - q * q)
            ratio = q * inv_p
            above = {n: across(cols[r][n][i:i + 1, :]) for n in range(i + 2, 8)}
            below = {n: across(cols[r][n][i + 1:i + 2, :]) - ratio * above[n] for n in above}
            at_j, at_next = lane == j, lane == j + 1
            unit_a = jnp.where(at_j, 1.0, across(t[r][i:i + 1, :]))
            new_b = jnp.where(at_j, 0.0, across(t[r][i + 1:i + 2, :])) - ratio * unit_a
            row_a = jnp.where(at_next, 0.0, unit_a)
            row_b = jnp.where(at_next, 1.0, new_b)
            either = at_j | at_next
            for k in range(r, groups):
                first = cols[k][i] * inv_p
                second = (cols[k][i + 1] - first * q) * inv_d
                if k == r:
                    first = jnp.where(sub > i, first, 0.0)
                    second = jnp.where(sub > i + 1, second, 0.0)
                for n in above:
                    cols[k][n] = cols[k][n] - first * above[n] - second * below[n]
                new = jnp.where(either, 0.0, t[k]) - first * row_a - second * row_b
                if k == r:
                    new = jnp.where(sub > i + 1, new, jnp.where(sub == i + 1, new_b, t[k]))
                t[k] = new
    for k in range(groups):
        if stop == RANK:
            row_of = sub + 8 * k
            pivot = jnp.sum(jnp.where(lane == row_of, t[k], 0.0), axis=1, keepdims=True)
            unit = jnp.where(lane < row_of, t[k], jnp.where(lane == row_of, 1.0, 0.0))
            out_ref[8 * k:8 * k + 8, :] = unit * lax.rsqrt(pivot) * scale
        else:
            out_ref[8 * k:8 * k + 8, :] = t[k]


def eliminate(start, stop, state, gram, after=()):
    return local(
        functools.partial(eliminate_kernel, start, stop), f32(RANK, RANK), [state, gram], after,
        flops=4000000, nbytes=(stop - start) * 150000, name=f"eliminate{start}",
    )


def block_kernel(keep_ref, recv_ref, w_ref, out_ref):
    w = w_ref[...].T
    w_high = w.astype(jnp.bfloat16)
    w_low = (w - w_high.astype(jnp.float32)).astype(jnp.bfloat16)
    both = jnp.concatenate([
        jnp.concatenate([w_high, w_low], axis=1),
        jnp.concatenate([w_high, jnp.zeros_like(w_low)], axis=1),
    ], axis=0)
    d = keep_ref[...] + recv_ref[...]
    high = d.astype(jnp.bfloat16)
    low = (d - high.astype(jnp.float32)).astype(jnp.bfloat16)
    out = jnp.dot(jnp.concatenate([high, low], axis=1), both, preferred_element_type=jnp.float32)
    out_ref[...] = (out[:, :RANK] + out[:, RANK:]).astype(jnp.bfloat16)


def ortho_kernel(p_ref, w_ref, out_ref):
    out_ref[...] = lax.dot_general(
        p_ref[...], w_ref[...], NT, precision=lax.Precision.HIGHEST, preferred_element_type=jnp.float32
    ).astype(jnp.bfloat16)


def join_kernel(k, n, mine_ref, recv_ref, out_ref):
    bit = step_bit(k)
    out_ref[pl.ds(pl.multiple_of(bit * n, 16), n), :] = mine_ref[...]
    out_ref[pl.ds(pl.multiple_of((1 - bit) * n, 16), n), :] = recv_ref[...]


def chunk_squares(ref, start):
    rows = ref[start:start + CHUNK, :].astype(jnp.float32)
    return jnp.sum((rows * rows).reshape(CHUNK // 8, 8, RANK), axis=0)


def squares_kernel(ref, out_ref):
    out_ref[...] = chunk_squares(ref, 0) + chunk_squares(ref, CHUNK)


def last_join_kernel(mine_ref, recv_ref, sq_ref, pair_ref, cross_ref, out_ref, sum_ref):
    join_kernel(0, 2 * CHUNK, mine_ref, recv_ref, out_ref)
    other = chunk_squares(recv_ref, 0) + chunk_squares(recv_ref, CHUNK)
    sum_ref[...] = (sq_ref[...] + other) + (pair_ref[...] + cross_ref[...])


def unpack_kernel(own_ref, other_ref, sq_ref, other_sq_ref, coef_ref, sum_ref):
    c = team(lax.axis_index("fsdp"))
    for source, half in ((own_ref, c), (other_ref, 1 - c)):
        for i in range(0, HALF, PIECE):
            rows = source[i:i + PIECE, :].astype(jnp.float32)
            coef_ref[pl.ds(pl.multiple_of(half * HALF + i, 8), PIECE), :] = rows
    sum_ref[...] = sq_ref[...] + other_sq_ref[...]


def stack_kernel(opposite_ref, next_ref, out_ref):
    out_ref[:8, :] = opposite_ref[...]
    out_ref[8:, :] = next_ref[...]


def momentum_kernel(coef_ref, ortho_ref, b_ref, mom_hbm, done_ref, buf, sems):
    ortho = ortho_ref[...]
    copies = []
    for i in range(TILES):
        cols = slice(i * WIDE, (i + 1) * WIDE)
        feedback = lax.dot_general(
            ortho, coef_ref[cols, :].astype(jnp.bfloat16), NT, preferred_element_type=jnp.float32
        )
        buf[:, cols] = (
            b_ref[:, cols].astype(jnp.float32) - (1.0 - inertia) * feedback
        ).astype(jnp.bfloat16)
        at = pl.ds(i * WIDE, WIDE)
        copies.append(pltpu.make_async_copy(buf.at[:, at], mom_hbm.at[:, at], sems.at[i]))
        copies[-1].start()
    for copy in copies:
        copy.wait()
    done_ref[...] = jnp.zeros_like(done_ref)


def finish_momentum(coef, ortho, blended):
    return pl.pallas_call(
        momentum_kernel,
        in_specs=[VMEM_SPEC] * 3,
        out_specs=[HBM_SPEC, VMEM_SPEC],
        out_shape=[bf16(LOCAL_ROWS, LOCAL_COLS), f32(8, RANK)],
        scratch_shapes=[
            VMEM((LOCAL_ROWS, LOCAL_COLS), jnp.bfloat16),
            pltpu.SemaphoreType.DMA((TILES,)),
        ],
        compiler_params=PARAMS,
        cost_estimate=cost(2 * 256 * 3328 * 128, 5000000),
        name="finish_momentum",
    )(coef, ortho, blended)


def weights_kernel(sq_ref, moved_ref, other_ref, coef_ref, ortho_ref, weights_ref, new_hbm, sub_hbm, buf, sub_buf, sems):
    scaling = math.sqrt(ROWS * COLS / RANK)
    moved = moved_ref[...] + other_ref[...]
    squares = (sq_ref[...] + moved[:8, :]) + moved[8:, :]
    norm = 1.0 / jnp.sqrt(jnp.sum(squares, axis=0, keepdims=True) + epsilon_sq)
    ortho = ortho_ref[...]
    copies = []
    for i in range(4):
        at = pl.ds(i * 2 * CHUNK, 2 * CHUNK)
        sub_buf[at, :] = coef_ref[at, :] * norm
        copies.append(pltpu.make_async_copy(sub_buf.at[at, :], sub_hbm.at[at, :], sems.at[0, i]))
        copies[-1].start()
    for i, (start, size) in enumerate(STRIPS):
        for first in range(start, start + size, WIDE):
            cols = slice(first, first + WIDE)
            update = lax.dot_general(
                ortho, sub_buf[cols, :].astype(jnp.bfloat16), NT, preferred_element_type=jnp.float32
            )
            buf[:, cols] = (
                weights_ref[:, cols].astype(jnp.float32) * (1.0 - step_size * shrinkage)
                - step_size * scaling * update
            ).astype(jnp.bfloat16)
        at = pl.ds(start, size)
        copies.append(pltpu.make_async_copy(buf.at[:, at], new_hbm.at[:, at], sems.at[1, i]))
        copies[-1].start()
    for copy in copies:
        copy.wait()


def finish_weights(squares, coef, ortho, weights):
    return pl.pallas_call(
        weights_kernel,
        in_specs=[VMEM_SPEC] * 6,
        out_specs=[HBM_SPEC] * 2,
        out_shape=[bf16(LOCAL_ROWS, LOCAL_COLS), f32(LOCAL_COLS, RANK)],
        scratch_shapes=[
            VMEM((LOCAL_ROWS, LOCAL_COLS), jnp.bfloat16),
            VMEM((LOCAL_COLS, RANK), jnp.float32),
            pltpu.SemaphoreType.DMA((2, len(STRIPS))),
        ],
        compiler_params=PARAMS,
        cost_estimate=cost(2 * 256 * 3328 * 128, 7000000),
        name="finish_weights",
    )(*squares, coef, ortho, weights)


def on_device(momentum, gradient, weights, subspace):
    blended, projected = project(momentum, gradient, subspace)
    for step in range(3):
        projected = projected + swap_z(projected, step)

    send = local(
        lift_send_kernel, f32(HALF + RANK, RANK), [projected, blended],
        flops=2 * 256 * 3328 * 128, nbytes=2000000, name="lift_send",
    )
    recv = xor_fsdp(send, CORE)
    keep = local(
        lift_keep_kernel, f32(HALF, RANK), [projected, blended], [send],
        flops=2 * 256 * 3328 * 128, nbytes=2000000, name="lift_keep",
    )
    n = HALF // 2
    moving, keep = split_step(0, n, keep, recv)
    gram = local(gram_pair_kernel, f32(RANK, RANK), [send, recv], [moving], nbytes=200000, name="gram_pair")
    recv = xor_step(moving, 0)
    split, both = split_xy(gram, X_THREE, Y_THREE)
    gram = gram_four(gram, both, split, xor_fsdp(split, CORE), [])
    n //= 2
    moving, keep = split_step(1, n, keep, recv, [gram])
    recv = xor_step(moving, 1)
    gram = local(hold_kernel, f32(RANK, RANK), [gram], [moving], nbytes=130000, name="hold")
    split, both = split_xy(gram, X_ONE, Y_ONE)
    d = add(keep, recv, [split, both], "first_sum")
    recv = xor_step(d, 2)
    split = local(hold_kernel, f32(RANK, RANK), [split], [d], nbytes=130000, name="hold_split")
    gram = gram_four(gram, both, split, xor_fsdp(split, CORE), [d])
    state = eliminate(0, CUT, gram, gram)
    d = add(d, recv, [state], "second_sum")
    recv = xor_step(d, 3)
    inverse = eliminate(CUT, RANK, state, gram, [d])

    coef = local(
        block_kernel, bf16(CHUNK, RANK), [d, recv, inverse],
        flops=2 * CHUNK * 256 * 256, nbytes=700000, name="block",
    )
    ortho = local(
        ortho_kernel, bf16(LOCAL_ROWS, RANK), [projected, inverse], [coef],
        flops=6 * 256 * 256 * 128, nbytes=300000, name="ortho",
    )
    coef = local(
        functools.partial(join_kernel, 1, CHUNK), bf16(2 * CHUNK, RANK), [coef, xor_step(coef, 1)],
        [ortho], nbytes=CHUNK * 1024, name="join1",
    )

    recv = xor_step(coef, 0)
    squares = local(squares_kernel, f32(8, RANK), [coef], flops=CHUNK * 512, nbytes=400000, name="squares")
    coef, squares = local(
        last_join_kernel, [bf16(HALF, RANK), f32(8, RANK)],
        [coef, recv, squares, pair_z(squares, False), pair_z(squares, True)],
        nbytes=CHUNK * 4096, name="join0",
    )
    opposite = turn_z(squares, (3, 3))
    coef, squares = local(
        unpack_kernel, [f32(LOCAL_COLS, RANK), f32(8, RANK)],
        [coef, xor_fsdp(coef, CORE), squares, xor_fsdp(squares, CORE)],
        flops=3328 * 128, nbytes=20000000, name="unpack",
    )
    new_momentum, done = finish_momentum(coef, ortho, blended)
    moved = local(
        stack_kernel, f32(16, RANK), [opposite, turn_z(squares, (1, -2))], [done],
        nbytes=30000, name="stack",
    )
    squares = [squares, moved, xor_fsdp(moved, CORE)]
    new_weights, new_subspace = finish_weights(squares, coef, ortho, weights)
    return (new_momentum, new_weights, new_subspace)


def solution(mesh):
    placed = (P("fsdp", "tp"), P("fsdp", "tp"), P("fsdp", "tp"), P("tp", None))
    return jax.shard_map(
        on_device,
        mesh=mesh,
        in_specs=placed,
        out_specs=(P("fsdp", "tp"), P("fsdp", "tp"), P("tp", None)),
        check_vma=False,
    )
```

```python
import functools
import math

import jax
import jax.numpy as jnp
from jax import lax
from jax.experimental import pallas as pl
from jax.experimental.pallas import tpu as pltpu
from jax.sharding import PartitionSpec as P

ROWS = 8192
COLS = 26624
RANK = 128

inertia = 0.95
step_size = 0.5
shrinkage = 0.1
epsilon_sq = 1e-06

LOCAL_ROWS = 256
LOCAL_COLS = 3328
TP = 8
FSDP = 32
HALF = LOCAL_COLS // 2
PART = LOCAL_ROWS // 2
CHUNK = HALF // 4
PIECE = HALF // 8
CUT = 40
WIDE = 256
TILES = LOCAL_COLS // WIDE
STRIPS = ((0, 512), (512, 768), (1280, 768), (2048, 768), (2816, 512))

X_ONE, Y_ONE, X_THREE, Y_THREE, CORE = 3, 9, 7, 25, 1
MASKS = ((X_ONE, X_THREE, Y_THREE, Y_ONE), (Y_ONE, Y_THREE, X_THREE, X_ONE))


def team(f):
    return (f % 2 + f // 2 + f // 8) % 2


Z_PAIRS = (
    ((0, 1), (2, 3), (4, 5), (6, 7)),
    ((1, 2), (3, 4), (5, 6), (7, 0)),
    ((2, 5), (1, 6), (4, 7), (3, 0)),
)

VMEM = pltpu.VMEM
VMEM_SPEC = pl.BlockSpec(memory_space=pltpu.VMEM)
HBM_SPEC = pl.BlockSpec(memory_space=pltpu.HBM)
PARAMS = pltpu.CompilerParams(vmem_limit_bytes=24 * 1024 * 1024)
NT = (((1,), (1,)), ((), ()))
TN = (((0,), (0,)), ((), ()))


def f32(*shape):
    return jax.ShapeDtypeStruct(shape, jnp.float32)


def bf16(*shape):
    return jax.ShapeDtypeStruct(shape, jnp.bfloat16)


def cost(flops, nbytes):
    return pl.CostEstimate(flops=flops, bytes_accessed=nbytes, transcendentals=0)

def swap_z(x, step):
    perm = []
    for f in range(FSDP):
        for a, b in Z_PAIRS[step]:
            one, two = f * TP + (a + f % 2) % TP, f * TP + (b + f % 2) % TP
            perm += [(one, two), (two, one)]
    return lax.ppermute(x, ("fsdp", "tp"), perm)


def pair_z(x, cross):
    perm = [
        (f * TP + z, (f ^ (MASKS[team(f)][0] if cross else 0)) * TP + (z ^ 1))
        for f in range(FSDP) for z in range(TP)
    ]
    return lax.ppermute(x, ("fsdp", "tp"), perm)


def turn_z(x, turns):
    perm = [
        ((f ^ 1) * TP + (z + turns[f % 2] * (1 if z % 2 else -1)) % TP, f * TP + z)
        for f in range(FSDP) for z in range(TP)
    ]
    return lax.ppermute(x, ("fsdp", "tp"), perm)


def xor_fsdp(x, mask):
    return lax.ppermute(x, "fsdp", [(i, i ^ mask) for i in range(FSDP)])


def split_xy(x, x_mask, y_mask):
    split = [(f ^ (y_mask if f % 2 else x_mask), f) for f in range(FSDP)]
    return lax.ppermute(x, "fsdp", split), xor_fsdp(x, x_mask ^ y_mask)


def xor_step(x, k):
    return lax.ppermute(x, "fsdp", [(i, i ^ MASKS[team(i)][k]) for i in range(FSDP)])


def step_bit(k):
    f = lax.axis_index("fsdp")
    place = jnp.where(team(f) == 0, (f // 2) % 4, f // 8)
    return place // 2 if k else place % 2 ^ place // 2


def project_kernel(m_hbm, g_hbm, s_hbm, b_ref, top_ref, low_ref, m_buf, g_buf, s_buf, sems):
    copies = []
    for i, (start, size) in enumerate(STRIPS):
        cols = pl.ds(start, size)
        copies.append((
            pltpu.make_async_copy(m_hbm.at[:, cols], m_buf.at[:, cols], sems.at[0, i]),
            pltpu.make_async_copy(g_hbm.at[:, cols], g_buf.at[:, cols], sems.at[1, i]),
            pltpu.make_async_copy(s_hbm.at[cols, :], s_buf.at[cols, :], sems.at[2, i]),
        ))
    for trio in copies:
        for copy in trio:
            copy.start()
    for i, trio in enumerate(copies):
        for copy in trio:
            copy.wait()
        start, size = STRIPS[i]
        cols = slice(start, start + size)
        b = (m_buf[:, cols].astype(jnp.float32) + g_buf[:, cols].astype(jnp.float32)).astype(jnp.bfloat16)
        b_ref[:, cols] = b
        part = jnp.dot(b, s_buf[cols, :].astype(jnp.bfloat16), preferred_element_type=jnp.float32)
        for ref, rows in ((top_ref, part[:PART, :]), (low_ref, part[PART:, :])):
            if i == 0:
                ref[...] = rows
            else:
                ref[...] += rows


def project(momentum, gradient, subspace):
    momentum, gradient, subspace = [
        pltpu.with_memory_space_constraint(x, pltpu.HBM) for x in (momentum, gradient, subspace)
    ]
    return pl.pallas_call(
        project_kernel,
        in_specs=[HBM_SPEC] * 3,
        out_specs=[VMEM_SPEC] * 3,
        out_shape=[bf16(LOCAL_ROWS, LOCAL_COLS), f32(PART, RANK), f32(PART, RANK)],
        scratch_shapes=[
            VMEM((LOCAL_ROWS, LOCAL_COLS), jnp.bfloat16),
            VMEM((LOCAL_ROWS, LOCAL_COLS), jnp.bfloat16),
            VMEM((LOCAL_COLS, RANK), jnp.float32),
            pltpu.SemaphoreType.DMA((3, len(STRIPS))),
        ],
        compiler_params=PARAMS,
        cost_estimate=cost(2 * 256 * 3328 * 128, 7000000),
        name="project",
    )(momentum, gradient, subspace)


def local(kernel, out_shape, args, after=(), flops=0, nbytes=0, name=None, scratch=()):
    used = len(args)

    def body(*refs):
        kernel(*refs[:used], *refs[used + len(after):])

    single = not isinstance(out_shape, (list, tuple))
    return pl.pallas_call(
        body,
        in_specs=[VMEM_SPEC] * (used + len(after)),
        out_specs=VMEM_SPEC if single else [VMEM_SPEC] * len(out_shape),
        out_shape=out_shape,
        scratch_shapes=list(scratch),
        compiler_params=PARAMS,
        cost_estimate=cost(flops, nbytes),
        name=name,
    )(*args, *after)


def lift_half(p, b_ref, half, target):
    high = p.astype(jnp.bfloat16)
    low = (p - high.astype(jnp.float32)).astype(jnp.bfloat16)
    split = jnp.concatenate([high, low], axis=1)
    for k in range(HALF // 128):
        cols = pl.ds(pl.multiple_of(half * HALF + k * 128, 128), 128)
        d = lax.dot_general(b_ref[:, cols], split, TN, preferred_element_type=jnp.float32)
        target[k * 128:(k + 1) * 128, :] = d[:, :RANK] + d[:, RANK:]


def lift_send_kernel(top_ref, low_ref, b_ref, send_ref):
    c = team(lax.axis_index("fsdp"))
    p = jnp.concatenate([top_ref[...], low_ref[...]], axis=0)
    lift_half(p, b_ref, 1 - c, send_ref)
    send_ref[HALF:, :] = lax.dot_general(
        p, p, TN, precision=lax.Precision.HIGHEST, preferred_element_type=jnp.float32
    )


def lift_keep_kernel(top_ref, low_ref, b_ref, keep_ref):
    p = jnp.concatenate([top_ref[...], low_ref[...]], axis=0)
    lift_half(p, b_ref, team(lax.axis_index("fsdp")), keep_ref)


def split_kernel(k, n, keep_ref, recv_ref, send_ref, next_ref):
    bit = step_bit(k)
    away = pl.ds(pl.multiple_of((1 - bit) * n, 8), n)
    stay = pl.ds(pl.multiple_of(bit * n, 8), n)
    send_ref[...] = keep_ref[away, :] + recv_ref[away, :]
    next_ref[...] = keep_ref[stay, :] + recv_ref[stay, :]


def split_step(k, n, keep, recv, after=()):
    return local(
        functools.partial(split_kernel, k, n), [f32(n, RANK), f32(n, RANK)], [keep, recv], after,
        flops=n * 256, nbytes=n * 2048, name=f"split{k}",
    )


def add_kernel(a_ref, b_ref, out_ref):
    out_ref[...] = a_ref[...] + b_ref[...]


def gram_pair_kernel(sent_ref, recv_ref, out_ref):
    out_ref[...] = sent_ref[HALF:, :] + recv_ref[HALF:, :]


def gram_four_kernel(a_ref, b_ref, c_ref, d_ref, out_ref):
    out_ref[...] = (a_ref[...] + b_ref[...]) + (c_ref[...] + d_ref[...])


def gram_four(a, b, c, d, after):
    return local(gram_four_kernel, f32(RANK, RANK), [a, b, c, d], after, nbytes=400000, name="gram_four")


def hold_kernel(a_ref, out_ref):
    out_ref[...] = a_ref[...]


def add(a, b, after, name):
    return local(add_kernel, f32(*a.shape), [a, b], after, nbytes=3 * 4 * a.size, name=name)


def reciprocal(x):
    r = pl.reciprocal(x, approx=True)
    r = r * (2.0 - x * r)
    return r * (2.0 - x * r)


def unit_scale(rows, lane, sub):
    diagonal = jnp.zeros((8, RANK), jnp.float32)
    for k, row in enumerate(rows):
        diagonal = diagonal + jnp.where(lane == sub + 8 * k, row, 0.0)
    return lax.rsqrt(jnp.sum(diagonal, axis=0, keepdims=True))


def eliminate_kernel(start, stop, in_ref, gram_ref, out_ref):
    groups = RANK // 8
    lane = lax.broadcasted_iota(jnp.int32, (8, RANK), 1)
    sub = lax.broadcasted_iota(jnp.int32, (8, RANK), 0)

    def across(x):
        return jnp.broadcast_to(x, (8, RANK))

    t = [in_ref[8 * r:8 * r + 8, :] for r in range(groups)]
    if start == 0 or stop == RANK:
        gram = [gram_ref[8 * r:8 * r + 8, :] for r in range(groups)]
        scale = unit_scale(gram, lane, sub)
    if start == 0:
        for r in range(groups):
            own = jnp.sum(jnp.where(lane == sub + 8 * r, t[r], 0.0), axis=1, keepdims=True)
            t[r] = t[r] * lax.rsqrt(own) * scale
    for r in range(start // 8, stop // 8):
        cols = {
            k: [across(t[k][:, 8 * r + i:8 * r + i + 1]) for i in range(8)]
            for k in range(r, groups)
        }
        for i in range(0, 8, 2):
            j = 8 * r + i
            p, q = across(cols[r][i][i:i + 1, :]), across(cols[r][i][i + 1:i + 2, :])
            d = across(cols[r][i + 1][i + 1:i + 2, :])
            inv_p = reciprocal(p)
            inv_d = p * reciprocal(p * d - q * q)
            ratio = q * inv_p
            above = {n: across(cols[r][n][i:i + 1, :]) for n in range(i + 2, 8)}
            below = {n: across(cols[r][n][i + 1:i + 2, :]) - ratio * above[n] for n in above}
            at_j, at_next = lane == j, lane == j + 1
            unit_a = jnp.where(at_j, 1.0, across(t[r][i:i + 1, :]))
            new_b = jnp.where(at_j, 0.0, across(t[r][i + 1:i + 2, :])) - ratio * unit_a
            row_a = jnp.where(at_next, 0.0, unit_a)
            row_b = jnp.where(at_next, 1.0, new_b)
            either = at_j | at_next
            for k in range(r, groups):
                first = cols[k][i] * inv_p
                second = (cols[k][i + 1] - first * q) * inv_d
                if k == r:
                    first = jnp.where(sub > i, first, 0.0)
                    second = jnp.where(sub > i + 1, second, 0.0)
                for n in above:
                    cols[k][n] = cols[k][n] - first * above[n] - second * below[n]
                new = jnp.where(either, 0.0, t[k]) - first * row_a - second * row_b
                if k == r:
                    new = jnp.where(sub > i + 1, new, jnp.where(sub == i + 1, new_b, t[k]))
                t[k] = new
    for k in range(groups):
        if stop == RANK:
            row_of = sub + 8 * k
            pivot = jnp.sum(jnp.where(lane == row_of, t[k], 0.0), axis=1, keepdims=True)
            unit = jnp.where(lane < row_of, t[k], jnp.where(lane == row_of, 1.0, 0.0))
            out_ref[8 * k:8 * k + 8, :] = unit * lax.rsqrt(pivot) * scale
        else:
            out_ref[8 * k:8 * k + 8, :] = t[k]


def eliminate(start, stop, state, gram, after=()):
    return local(
        functools.partial(eliminate_kernel, start, stop), f32(RANK, RANK), [state, gram], after,
        flops=4000000, nbytes=(stop - start) * 150000, name=f"eliminate{start}",
    )


def block_kernel(keep_ref, recv_ref, w_ref, out_ref):
    w = w_ref[...].T
    w_high = w.astype(jnp.bfloat16)
    w_low = (w - w_high.astype(jnp.float32)).astype(jnp.bfloat16)
    both = jnp.concatenate([
        jnp.concatenate([w_high, w_low], axis=1),
        jnp.concatenate([w_high, jnp.zeros_like(w_low)], axis=1),
    ], axis=0)
    d = keep_ref[...] + recv_ref[...]
    high = d.astype(jnp.bfloat16)
    low = (d - high.astype(jnp.float32)).astype(jnp.bfloat16)
    out = jnp.dot(jnp.concatenate([high, low], axis=1), both, preferred_element_type=jnp.float32)
    out_ref[...] = (out[:, :RANK] + out[:, RANK:]).astype(jnp.bfloat16)


def ortho_kernel(top_ref, low_ref, w_ref, out_ref):
    p = jnp.concatenate([top_ref[...], low_ref[...]], axis=0)
    out_ref[...] = lax.dot_general(
        p, w_ref[...], NT, precision=lax.Precision.HIGHEST, preferred_element_type=jnp.float32
    ).astype(jnp.bfloat16)


def join_kernel(k, n, mine_ref, recv_ref, out_ref):
    bit = step_bit(k)
    out_ref[pl.ds(pl.multiple_of(bit * n, 16), n), :] = mine_ref[...]
    out_ref[pl.ds(pl.multiple_of((1 - bit) * n, 16), n), :] = recv_ref[...]


def chunk_squares(ref, start):
    rows = ref[start:start + CHUNK, :].astype(jnp.float32)
    return jnp.sum((rows * rows).reshape(CHUNK // 8, 8, RANK), axis=0)


def squares_kernel(ref, out_ref):
    out_ref[...] = chunk_squares(ref, 0) + chunk_squares(ref, CHUNK)


def last_join_kernel(mine_ref, recv_ref, sq_ref, pair_ref, cross_ref, out_ref, sum_ref):
    join_kernel(0, 2 * CHUNK, mine_ref, recv_ref, out_ref)
    other = chunk_squares(recv_ref, 0) + chunk_squares(recv_ref, CHUNK)
    sum_ref[...] = (sq_ref[...] + other) + (pair_ref[...] + cross_ref[...])


def unpack_kernel(own_ref, other_ref, sq_ref, other_sq_ref, coef_ref, sum_ref):
    c = team(lax.axis_index("fsdp"))
    for source, half in ((own_ref, c), (other_ref, 1 - c)):
        for i in range(0, HALF, PIECE):
            rows = source[i:i + PIECE, :].astype(jnp.float32)
            coef_ref[pl.ds(pl.multiple_of(half * HALF + i, 8), PIECE), :] = rows
    sum_ref[...] = sq_ref[...] + other_sq_ref[...]


def stack_kernel(opposite_ref, next_ref, out_ref):
    out_ref[:8, :] = opposite_ref[...]
    out_ref[8:, :] = next_ref[...]


def momentum_kernel(coef_ref, ortho_ref, b_ref, mom_hbm, done_ref, buf, sems):
    ortho = ortho_ref[...]
    copies = []
    for i in range(TILES):
        cols = slice(i * WIDE, (i + 1) * WIDE)
        feedback = lax.dot_general(
            ortho, coef_ref[cols, :].astype(jnp.bfloat16), NT, preferred_element_type=jnp.float32
        )
        buf[:, cols] = (
            b_ref[:, cols].astype(jnp.float32) - (1.0 - inertia) * feedback
        ).astype(jnp.bfloat16)
        at = pl.ds(i * WIDE, WIDE)
        copies.append(pltpu.make_async_copy(buf.at[:, at], mom_hbm.at[:, at], sems.at[i]))
        copies[-1].start()
    for copy in copies:
        copy.wait()
    done_ref[...] = jnp.zeros_like(done_ref)


def finish_momentum(coef, ortho, blended):
    return pl.pallas_call(
        momentum_kernel,
        in_specs=[VMEM_SPEC] * 3,
        out_specs=[HBM_SPEC, VMEM_SPEC],
        out_shape=[bf16(LOCAL_ROWS, LOCAL_COLS), f32(8, RANK)],
        scratch_shapes=[
            VMEM((LOCAL_ROWS, LOCAL_COLS), jnp.bfloat16),
            pltpu.SemaphoreType.DMA((TILES,)),
        ],
        compiler_params=PARAMS,
        cost_estimate=cost(2 * 256 * 3328 * 128, 5000000),
        name="finish_momentum",
    )(coef, ortho, blended)


def weights_kernel(sq_ref, moved_ref, other_ref, coef_ref, ortho_ref, weights_ref, new_hbm, sub_hbm, buf, sub_buf, sems):
    scaling = math.sqrt(ROWS * COLS / RANK)
    moved = moved_ref[...] + other_ref[...]
    squares = (sq_ref[...] + moved[:8, :]) + moved[8:, :]
    norm = 1.0 / jnp.sqrt(jnp.sum(squares, axis=0, keepdims=True) + epsilon_sq)
    ortho = ortho_ref[...]
    copies = []
    for i in range(4):
        at = pl.ds(i * 2 * CHUNK, 2 * CHUNK)
        sub_buf[at, :] = coef_ref[at, :] * norm
        copies.append(pltpu.make_async_copy(sub_buf.at[at, :], sub_hbm.at[at, :], sems.at[0, i]))
        copies[-1].start()
    for i, (start, size) in enumerate(STRIPS):
        for first in range(start, start + size, WIDE):
            cols = slice(first, first + WIDE)
            update = lax.dot_general(
                ortho, sub_buf[cols, :].astype(jnp.bfloat16), NT, preferred_element_type=jnp.float32
            )
            buf[:, cols] = (
                weights_ref[:, cols].astype(jnp.float32) * (1.0 - step_size * shrinkage)
                - step_size * scaling * update
            ).astype(jnp.bfloat16)
        at = pl.ds(start, size)
        copies.append(pltpu.make_async_copy(buf.at[:, at], new_hbm.at[:, at], sems.at[1, i]))
        copies[-1].start()
    for copy in copies:
        copy.wait()


def finish_weights(squares, coef, ortho, weights):
    return pl.pallas_call(
        weights_kernel,
        in_specs=[VMEM_SPEC] * 6,
        out_specs=[HBM_SPEC] * 2,
        out_shape=[bf16(LOCAL_ROWS, LOCAL_COLS), f32(LOCAL_COLS, RANK)],
        scratch_shapes=[
            VMEM((LOCAL_ROWS, LOCAL_COLS), jnp.bfloat16),
            VMEM((LOCAL_COLS, RANK), jnp.float32),
            pltpu.SemaphoreType.DMA((2, len(STRIPS))),
        ],
        compiler_params=PARAMS,
        cost_estimate=cost(2 * 256 * 3328 * 128, 7000000),
        name="finish_weights",
    )(*squares, coef, ortho, weights)


def on_device(momentum, gradient, weights, subspace):
    blended, *projected = project(momentum, gradient, subspace)
    for step in range(3):
        projected = [rows + swap_z(rows, step) for rows in projected]

    send = local(
        lift_send_kernel, f32(HALF + RANK, RANK), [*projected, blended],
        flops=2 * 256 * 3328 * 128, nbytes=2000000, name="lift_send",
    )
    recv = xor_fsdp(send, CORE)
    keep = local(
        lift_keep_kernel, f32(HALF, RANK), [*projected, blended], [send],
        flops=2 * 256 * 3328 * 128, nbytes=2000000, name="lift_keep",
    )
    n = HALF // 2
    moving, keep = split_step(0, n, keep, recv)
    gram = local(gram_pair_kernel, f32(RANK, RANK), [send, recv], [moving], nbytes=200000, name="gram_pair")
    recv = xor_step(moving, 0)
    split, both = split_xy(gram, X_THREE, Y_THREE)
    gram = gram_four(gram, both, split, xor_fsdp(split, CORE), [])
    n //= 2
    moving, keep = split_step(1, n, keep, recv, [gram])
    recv = xor_step(moving, 1)
    gram = local(hold_kernel, f32(RANK, RANK), [gram], [moving], nbytes=130000, name="hold")
    split, both = split_xy(gram, X_ONE, Y_ONE)
    d = add(keep, recv, [split, both], "first_sum")
    recv = xor_step(d, 2)
    split = local(hold_kernel, f32(RANK, RANK), [split], [d], nbytes=130000, name="hold_split")
    gram = gram_four(gram, both, split, xor_fsdp(split, CORE), [d])
    state = eliminate(0, CUT, gram, gram)
    d = add(d, recv, [state], "second_sum")
    recv = xor_step(d, 3)
    inverse = eliminate(CUT, RANK, state, gram, [d])

    coef = local(
        block_kernel, bf16(CHUNK, RANK), [d, recv, inverse],
        flops=2 * CHUNK * 256 * 256, nbytes=700000, name="block",
    )
    ortho = local(
        ortho_kernel, bf16(LOCAL_ROWS, RANK), [*projected, inverse], [coef],
        flops=6 * 256 * 256 * 128, nbytes=300000, name="ortho",
    )
    coef = local(
        functools.partial(join_kernel, 1, CHUNK), bf16(2 * CHUNK, RANK), [coef, xor_step(coef, 1)],
        [ortho], nbytes=CHUNK * 1024, name="join1",
    )

    recv = xor_step(coef, 0)
    squares = local(squares_kernel, f32(8, RANK), [coef], flops=CHUNK * 512, nbytes=400000, name="squares")
    coef, squares = local(
        last_join_kernel, [bf16(HALF, RANK), f32(8, RANK)],
        [coef, recv, squares, pair_z(squares, False), pair_z(squares, True)],
        nbytes=CHUNK * 4096, name="join0",
    )
    opposite = turn_z(squares, (3, 3))
    coef, squares = local(
        unpack_kernel, [f32(LOCAL_COLS, RANK), f32(8, RANK)],
        [coef, xor_fsdp(coef, CORE), squares, xor_fsdp(squares, CORE)],
        flops=3328 * 128, nbytes=20000000, name="unpack",
    )
    new_momentum, done = finish_momentum(coef, ortho, blended)
    moved = local(
        stack_kernel, f32(16, RANK), [opposite, turn_z(squares, (1, -2))], [done],
        nbytes=30000, name="stack",
    )
    squares = [squares, moved, xor_fsdp(moved, CORE)]
    new_weights, new_subspace = finish_weights(squares, coef, ortho, weights)
    return (new_momentum, new_weights, new_subspace)


def solution(mesh):
    placed = (P("fsdp", "tp"), P("fsdp", "tp"), P("fsdp", "tp"), P("tp", None))
    return jax.shard_map(
        on_device,
        mesh=mesh,
        in_specs=placed,
        out_specs=(P("fsdp", "tp"), P("fsdp", "tp"), P("tp", None)),
        check_vma=False,
    )
```

```python
import functools
import math

import jax
import jax.numpy as jnp
from jax import lax
from jax.experimental import pallas as pl
from jax.experimental.pallas import tpu as pltpu
from jax.sharding import PartitionSpec as P

ROWS = 8192
COLS = 26624
RANK = 128

inertia = 0.95
step_size = 0.5
shrinkage = 0.1
epsilon_sq = 1e-06

LOCAL_ROWS = 256
LOCAL_COLS = 3328
TP = 8
FSDP = 32
HALF = LOCAL_COLS // 2
PART = LOCAL_ROWS // 2
CHUNK = HALF // 4
PIECE = HALF // 8
CUT = 40
WIDE = 256
TILES = LOCAL_COLS // WIDE
STRIPS = ((0, 512), (512, 768), (1280, 768), (2048, 768), (2816, 512))

X_ONE, Y_ONE, X_THREE, Y_THREE, CORE = 3, 9, 7, 25, 1
MASKS = ((X_ONE, X_THREE, Y_THREE, Y_ONE), (Y_ONE, Y_THREE, X_THREE, X_ONE))


def team(f):
    return (f % 2 + f // 2 + f // 8) % 2


Z_PAIRS = (
    ((0, 1), (2, 3), (4, 5), (6, 7)),
    ((1, 2), (3, 4), (5, 6), (7, 0)),
    ((2, 5), (1, 6), (4, 7), (3, 0)),
)

VMEM = pltpu.VMEM
VMEM_SPEC = pl.BlockSpec(memory_space=pltpu.VMEM)
HBM_SPEC = pl.BlockSpec(memory_space=pltpu.HBM)
PARAMS = pltpu.CompilerParams(vmem_limit_bytes=24 * 1024 * 1024)
NT = (((1,), (1,)), ((), ()))
TN = (((0,), (0,)), ((), ()))


def f32(*shape):
    return jax.ShapeDtypeStruct(shape, jnp.float32)


def bf16(*shape):
    return jax.ShapeDtypeStruct(shape, jnp.bfloat16)


def cost(flops, nbytes):
    return pl.CostEstimate(flops=flops, bytes_accessed=nbytes, transcendentals=0)

def swap_z(x, step):
    perm = []
    for f in range(FSDP):
        for a, b in Z_PAIRS[step]:
            one, two = f * TP + (a + f % 2) % TP, f * TP + (b + f % 2) % TP
            perm += [(one, two), (two, one)]
    return lax.ppermute(x, ("fsdp", "tp"), perm)


def pair_z(x, cross):
    perm = [
        (f * TP + z, (f ^ (MASKS[team(f)][0] if cross else 0)) * TP + (z ^ 1))
        for f in range(FSDP) for z in range(TP)
    ]
    return lax.ppermute(x, ("fsdp", "tp"), perm)


def turn_z(x, turns):
    perm = [
        ((f ^ 1) * TP + (z + turns[f % 2] * (1 if z % 2 else -1)) % TP, f * TP + z)
        for f in range(FSDP) for z in range(TP)
    ]
    return lax.ppermute(x, ("fsdp", "tp"), perm)


def xor_fsdp(x, mask):
    return lax.ppermute(x, "fsdp", [(i, i ^ mask) for i in range(FSDP)])


def split_cores(x, first, second):
    return lax.ppermute(x, "fsdp", [(f ^ (second if f % 2 else first), f) for f in range(FSDP)])


def xor_step(x, k):
    return lax.ppermute(x, "fsdp", [(i, i ^ MASKS[team(i)][k]) for i in range(FSDP)])


def step_bit(k):
    f = lax.axis_index("fsdp")
    place = jnp.where(team(f) == 0, (f // 2) % 4, f // 8)
    return place // 2 if k else place % 2 ^ place // 2


def project_kernel(m_hbm, g_hbm, s_hbm, b_ref, top_ref, low_ref, m_buf, g_buf, s_buf, sems):
    copies = []
    for i, (start, size) in enumerate(STRIPS):
        cols = pl.ds(start, size)
        copies.append((
            pltpu.make_async_copy(m_hbm.at[:, cols], m_buf.at[:, cols], sems.at[0, i]),
            pltpu.make_async_copy(g_hbm.at[:, cols], g_buf.at[:, cols], sems.at[1, i]),
            pltpu.make_async_copy(s_hbm.at[cols, :], s_buf.at[cols, :], sems.at[2, i]),
        ))
    for trio in copies:
        for copy in trio:
            copy.start()
    for i, trio in enumerate(copies):
        for copy in trio:
            copy.wait()
        start, size = STRIPS[i]
        cols = slice(start, start + size)
        b = (m_buf[:, cols].astype(jnp.float32) + g_buf[:, cols].astype(jnp.float32)).astype(jnp.bfloat16)
        b_ref[:, cols] = b
        part = jnp.dot(b, s_buf[cols, :].astype(jnp.bfloat16), preferred_element_type=jnp.float32)
        for ref, rows in ((top_ref, part[:PART, :]), (low_ref, part[PART:, :])):
            if i == 0:
                ref[...] = rows
            else:
                ref[...] += rows


def project(momentum, gradient, subspace):
    momentum, gradient, subspace = [
        pltpu.with_memory_space_constraint(x, pltpu.HBM) for x in (momentum, gradient, subspace)
    ]
    return pl.pallas_call(
        project_kernel,
        in_specs=[HBM_SPEC] * 3,
        out_specs=[VMEM_SPEC] * 3,
        out_shape=[bf16(LOCAL_ROWS, LOCAL_COLS), f32(PART, RANK), f32(PART, RANK)],
        scratch_shapes=[
            VMEM((LOCAL_ROWS, LOCAL_COLS), jnp.bfloat16),
            VMEM((LOCAL_ROWS, LOCAL_COLS), jnp.bfloat16),
            VMEM((LOCAL_COLS, RANK), jnp.float32),
            pltpu.SemaphoreType.DMA((3, len(STRIPS))),
        ],
        compiler_params=PARAMS,
        cost_estimate=cost(2 * 256 * 3328 * 128, 7000000),
        name="project",
    )(momentum, gradient, subspace)


def local(kernel, out_shape, args, after=(), flops=0, nbytes=0, name=None, scratch=()):
    used = len(args)

    def body(*refs):
        kernel(*refs[:used], *refs[used + len(after):])

    single = not isinstance(out_shape, (list, tuple))
    return pl.pallas_call(
        body,
        in_specs=[VMEM_SPEC] * (used + len(after)),
        out_specs=VMEM_SPEC if single else [VMEM_SPEC] * len(out_shape),
        out_shape=out_shape,
        scratch_shapes=list(scratch),
        compiler_params=PARAMS,
        cost_estimate=cost(flops, nbytes),
        name=name,
    )(*args, *after)


def lift_half(p, b_ref, half, target):
    high = p.astype(jnp.bfloat16)
    low = (p - high.astype(jnp.float32)).astype(jnp.bfloat16)
    split = jnp.concatenate([high, low], axis=1)
    for k in range(HALF // 128):
        cols = pl.ds(pl.multiple_of(half * HALF + k * 128, 128), 128)
        d = lax.dot_general(b_ref[:, cols], split, TN, preferred_element_type=jnp.float32)
        target[k * 128:(k + 1) * 128, :] = d[:, :RANK] + d[:, RANK:]


def lift_send_kernel(top_ref, low_ref, b_ref, send_ref):
    c = team(lax.axis_index("fsdp"))
    p = jnp.concatenate([top_ref[...], low_ref[...]], axis=0)
    lift_half(p, b_ref, 1 - c, send_ref)
    send_ref[HALF:, :] = lax.dot_general(
        p, p, TN, precision=lax.Precision.HIGHEST, preferred_element_type=jnp.float32
    )


def lift_keep_kernel(top_ref, low_ref, b_ref, keep_ref):
    p = jnp.concatenate([top_ref[...], low_ref[...]], axis=0)
    lift_half(p, b_ref, team(lax.axis_index("fsdp")), keep_ref)


def split_kernel(k, n, keep_ref, recv_ref, send_ref, next_ref):
    bit = step_bit(k)
    away = pl.ds(pl.multiple_of((1 - bit) * n, 8), n)
    stay = pl.ds(pl.multiple_of(bit * n, 8), n)
    send_ref[...] = keep_ref[away, :] + recv_ref[away, :]
    next_ref[...] = keep_ref[stay, :] + recv_ref[stay, :]


def split_step(k, n, keep, recv, after=()):
    return local(
        functools.partial(split_kernel, k, n), [f32(n, RANK), f32(n, RANK)], [keep, recv], after,
        flops=n * 256, nbytes=n * 2048, name=f"split{k}",
    )


def add_kernel(a_ref, b_ref, out_ref):
    out_ref[...] = a_ref[...] + b_ref[...]


def gram_pair_kernel(sent_ref, recv_ref, out_ref):
    out_ref[...] = sent_ref[HALF:, :] + recv_ref[HALF:, :]


def gram_four_kernel(a_ref, b_ref, c_ref, d_ref, out_ref):
    out_ref[...] = (a_ref[...] + b_ref[...]) + (c_ref[...] + d_ref[...])


def gram_four(a, b, c, d, after):
    return local(gram_four_kernel, f32(RANK, RANK), [a, b, c, d], after, nbytes=400000, name="gram_four")


def hold_kernel(a_ref, out_ref):
    out_ref[...] = a_ref[...]


def add(a, b, after, name):
    return local(add_kernel, f32(*a.shape), [a, b], after, nbytes=12 * a.size, name=name)


def reciprocal(x):
    r = pl.reciprocal(x, approx=True)
    r = r * (2.0 - x * r)
    return r * (2.0 - x * r)


def unit_scale(rows, lane, sub):
    diagonal = jnp.zeros((8, RANK), jnp.float32)
    for k, row in enumerate(rows):
        diagonal = diagonal + jnp.where(lane == sub + 8 * k, row, 0.0)
    return lax.rsqrt(jnp.sum(diagonal, axis=0, keepdims=True))


def eliminate_kernel(start, stop, in_ref, gram_ref, out_ref):
    groups = RANK // 8
    lane = lax.broadcasted_iota(jnp.int32, (8, RANK), 1)
    sub = lax.broadcasted_iota(jnp.int32, (8, RANK), 0)

    def across(x):
        return jnp.broadcast_to(x, (8, RANK))

    t = [in_ref[8 * r:8 * r + 8, :] for r in range(groups)]
    if start == 0 or stop == RANK:
        gram = [gram_ref[8 * r:8 * r + 8, :] for r in range(groups)]
        scale = unit_scale(gram, lane, sub)
    if start == 0:
        for r in range(groups):
            own = jnp.sum(jnp.where(lane == sub + 8 * r, t[r], 0.0), axis=1, keepdims=True)
            t[r] = t[r] * lax.rsqrt(own) * scale
    for r in range(start // 8, stop // 8):
        cols = {
            k: [across(t[k][:, 8 * r + i:8 * r + i + 1]) for i in range(8)]
            for k in range(r, groups)
        }
        for i in range(0, 8, 2):
            j = 8 * r + i
            p, q = across(cols[r][i][i:i + 1, :]), across(cols[r][i][i + 1:i + 2, :])
            d = across(cols[r][i + 1][i + 1:i + 2, :])
            inv_p = reciprocal(p)
            inv_d = p * reciprocal(p * d - q * q)
            ratio = q * inv_p
            above = {n: across(cols[r][n][i:i + 1, :]) for n in range(i + 2, 8)}
            below = {n: across(cols[r][n][i + 1:i + 2, :]) - ratio * above[n] for n in above}
            at_j, at_next = lane == j, lane == j + 1
            unit_a = jnp.where(at_j, 1.0, across(t[r][i:i + 1, :]))
            new_b = jnp.where(at_j, 0.0, across(t[r][i + 1:i + 2, :])) - ratio * unit_a
            row_a = jnp.where(at_next, 0.0, unit_a)
            row_b = jnp.where(at_next, 1.0, new_b)
            either = at_j | at_next
            for k in range(r, groups):
                first = cols[k][i] * inv_p
                second = (cols[k][i + 1] - first * q) * inv_d
                if k == r:
                    first = jnp.where(sub > i, first, 0.0)
                    second = jnp.where(sub > i + 1, second, 0.0)
                for n in above:
                    cols[k][n] = cols[k][n] - first * above[n] - second * below[n]
                new = jnp.where(either, 0.0, t[k]) - first * row_a - second * row_b
                if k == r:
                    new = jnp.where(sub > i + 1, new, jnp.where(sub == i + 1, new_b, t[k]))
                t[k] = new
    for k in range(groups):
        if stop == RANK:
            row_of = sub + 8 * k
            pivot = jnp.sum(jnp.where(lane == row_of, t[k], 0.0), axis=1, keepdims=True)
            unit = jnp.where(lane < row_of, t[k], jnp.where(lane == row_of, 1.0, 0.0))
            out_ref[8 * k:8 * k + 8, :] = unit * lax.rsqrt(pivot) * scale
        else:
            out_ref[8 * k:8 * k + 8, :] = t[k]


def eliminate(start, stop, state, gram, after=()):
    return local(
        functools.partial(eliminate_kernel, start, stop), f32(RANK, RANK), [state, gram], after,
        flops=4000000, nbytes=(stop - start) * 150000, name=f"eliminate{start}",
    )


def block_kernel(keep_ref, recv_ref, w_ref, out_ref):
    w = w_ref[...].T
    w_high = w.astype(jnp.bfloat16)
    w_low = (w - w_high.astype(jnp.float32)).astype(jnp.bfloat16)
    both = jnp.concatenate([
        jnp.concatenate([w_high, w_low], axis=1),
        jnp.concatenate([w_high, jnp.zeros_like(w_low)], axis=1),
    ], axis=0)
    d = keep_ref[...] + recv_ref[...]
    high = d.astype(jnp.bfloat16)
    low = (d - high.astype(jnp.float32)).astype(jnp.bfloat16)
    out = jnp.dot(jnp.concatenate([high, low], axis=1), both, preferred_element_type=jnp.float32)
    out_ref[...] = (out[:, :RANK] + out[:, RANK:]).astype(jnp.bfloat16)


def ortho_kernel(top_ref, low_ref, w_ref, out_ref):
    p = jnp.concatenate([top_ref[...], low_ref[...]], axis=0)
    out_ref[...] = lax.dot_general(
        p, w_ref[...], NT, precision=lax.Precision.HIGHEST, preferred_element_type=jnp.float32
    ).astype(jnp.bfloat16)


def join_kernel(k, n, mine_ref, recv_ref, out_ref):
    bit = step_bit(k)
    out_ref[pl.ds(pl.multiple_of(bit * n, 16), n), :] = mine_ref[...]
    out_ref[pl.ds(pl.multiple_of((1 - bit) * n, 16), n), :] = recv_ref[...]


def chunk_squares(ref, start):
    rows = ref[start:start + CHUNK, :].astype(jnp.float32)
    return jnp.sum((rows * rows).reshape(CHUNK // 8, 8, RANK), axis=0)


def squares_kernel(ref, out_ref):
    out_ref[...] = chunk_squares(ref, 0) + chunk_squares(ref, CHUNK)


def last_join_kernel(mine_ref, recv_ref, sq_ref, pair_ref, cross_ref, out_ref, sum_ref):
    join_kernel(0, 2 * CHUNK, mine_ref, recv_ref, out_ref)
    other = chunk_squares(recv_ref, 0) + chunk_squares(recv_ref, CHUNK)
    sum_ref[...] = (sq_ref[...] + other) + (pair_ref[...] + cross_ref[...])


def unpack_kernel(own_ref, other_ref, sq_ref, other_sq_ref, coef_ref, sum_ref):
    c = team(lax.axis_index("fsdp"))
    for source, half in ((own_ref, c), (other_ref, 1 - c)):
        for i in range(0, HALF, PIECE):
            rows = source[i:i + PIECE, :].astype(jnp.float32)
            coef_ref[pl.ds(pl.multiple_of(half * HALF + i, 8), PIECE), :] = rows
    sum_ref[...] = sq_ref[...] + other_sq_ref[...]


def stack_kernel(opposite_ref, next_ref, out_ref):
    out_ref[:8, :] = opposite_ref[...]
    out_ref[8:, :] = next_ref[...]


def momentum_kernel(coef_ref, ortho_ref, b_ref, mom_hbm, done_ref, buf, sems):
    ortho = ortho_ref[...]
    copies = []
    for i in range(TILES):
        cols = slice(i * WIDE, (i + 1) * WIDE)
        feedback = lax.dot_general(
            ortho, coef_ref[cols, :].astype(jnp.bfloat16), NT, preferred_element_type=jnp.float32
        )
        buf[:, cols] = (
            b_ref[:, cols].astype(jnp.float32) - (1.0 - inertia) * feedback
        ).astype(jnp.bfloat16)
        at = pl.ds(i * WIDE, WIDE)
        copies.append(pltpu.make_async_copy(buf.at[:, at], mom_hbm.at[:, at], sems.at[i]))
        copies[-1].start()
    for copy in copies:
        copy.wait()
    done_ref[...] = jnp.zeros_like(done_ref)


def finish_momentum(coef, ortho, blended):
    return pl.pallas_call(
        momentum_kernel,
        in_specs=[VMEM_SPEC] * 3,
        out_specs=[HBM_SPEC, VMEM_SPEC],
        out_shape=[bf16(LOCAL_ROWS, LOCAL_COLS), f32(8, RANK)],
        scratch_shapes=[
            VMEM((LOCAL_ROWS, LOCAL_COLS), jnp.bfloat16),
            pltpu.SemaphoreType.DMA((TILES,)),
        ],
        compiler_params=PARAMS,
        cost_estimate=cost(2 * 256 * 3328 * 128, 5000000),
        name="finish_momentum",
    )(coef, ortho, blended)


def weights_kernel(sq_ref, moved_ref, other_ref, coef_ref, ortho_ref, weights_ref, new_hbm, sub_hbm, buf, sub_buf, sems):
    scaling = math.sqrt(ROWS * COLS / RANK)
    moved = moved_ref[...] + other_ref[...]
    squares = (sq_ref[...] + moved[:8, :]) + moved[8:, :]
    norm = 1.0 / jnp.sqrt(jnp.sum(squares, axis=0, keepdims=True) + epsilon_sq)
    ortho = ortho_ref[...]
    copies = []
    for i in range(4):
        at = pl.ds(i * 2 * CHUNK, 2 * CHUNK)
        sub_buf[at, :] = coef_ref[at, :] * norm
        copies.append(pltpu.make_async_copy(sub_buf.at[at, :], sub_hbm.at[at, :], sems.at[0, i]))
        copies[-1].start()
    for i, (start, size) in enumerate(STRIPS):
        for first in range(start, start + size, WIDE):
            cols = slice(first, first + WIDE)
            update = lax.dot_general(
                ortho, sub_buf[cols, :].astype(jnp.bfloat16), NT, preferred_element_type=jnp.float32
            )
            buf[:, cols] = (
                weights_ref[:, cols].astype(jnp.float32) * (1.0 - step_size * shrinkage)
                - step_size * scaling * update
            ).astype(jnp.bfloat16)
        at = pl.ds(start, size)
        copies.append(pltpu.make_async_copy(buf.at[:, at], new_hbm.at[:, at], sems.at[1, i]))
        copies[-1].start()
    for copy in copies:
        copy.wait()


def finish_weights(squares, coef, ortho, weights):
    return pl.pallas_call(
        weights_kernel,
        in_specs=[VMEM_SPEC] * 6,
        out_specs=[HBM_SPEC] * 2,
        out_shape=[bf16(LOCAL_ROWS, LOCAL_COLS), f32(LOCAL_COLS, RANK)],
        scratch_shapes=[
            VMEM((LOCAL_ROWS, LOCAL_COLS), jnp.bfloat16),
            VMEM((LOCAL_COLS, RANK), jnp.float32),
            pltpu.SemaphoreType.DMA((2, len(STRIPS))),
        ],
        compiler_params=PARAMS,
        cost_estimate=cost(2 * 256 * 3328 * 128, 7000000),
        name="finish_weights",
    )(*squares, coef, ortho, weights)


def on_device(momentum, gradient, weights, subspace):
    blended, *projected = project(momentum, gradient, subspace)
    for step in range(3):
        projected = [rows + swap_z(rows, step) for rows in projected]

    send = local(
        lift_send_kernel, f32(HALF + RANK, RANK), [*projected, blended],
        flops=2 * 256 * 3328 * 128, nbytes=2000000, name="lift_send",
    )
    recv = xor_fsdp(send, CORE)
    keep = local(
        lift_keep_kernel, f32(HALF, RANK), [*projected, blended], [send],
        flops=2 * 256 * 3328 * 128, nbytes=2000000, name="lift_keep",
    )
    n = HALF // 2
    moving, keep = split_step(0, n, keep, recv)
    gram = local(gram_pair_kernel, f32(RANK, RANK), [send, recv], [moving], nbytes=200000, name="gram_pair")
    recv = xor_step(moving, 0)
    split = split_cores(gram, X_THREE, X_THREE ^ Y_THREE ^ CORE)
    gram = gram_four(gram, xor_fsdp(gram, Y_THREE), split, xor_fsdp(split, CORE), [])
    n //= 2
    moving, keep = split_step(1, n, keep, recv, [gram])
    recv = xor_step(moving, 1)
    gram = local(hold_kernel, f32(RANK, RANK), [gram], [moving], nbytes=130000, name="hold")
    split, both = split_cores(gram, X_ONE, Y_ONE), xor_fsdp(gram, X_ONE ^ Y_ONE)
    d = add(keep, recv, [split, both], "first_sum")
    recv = xor_step(d, 2)
    split = local(hold_kernel, f32(RANK, RANK), [split], [d], nbytes=130000, name="hold_split")
    gram = gram_four(gram, both, split, xor_fsdp(split, CORE), [d])
    state = eliminate(0, CUT, gram, gram)
    d = add(d, recv, [state], "second_sum")
    recv = xor_step(d, 3)
    inverse = eliminate(CUT, RANK, state, gram, [d])

    coef = local(
        block_kernel, bf16(CHUNK, RANK), [d, recv, inverse],
        flops=2 * CHUNK * 256 * 256, nbytes=700000, name="block",
    )
    ortho = local(
        ortho_kernel, bf16(LOCAL_ROWS, RANK), [*projected, inverse], [coef],
        flops=6 * 256 * 256 * 128, nbytes=300000, name="ortho",
    )
    coef = local(
        functools.partial(join_kernel, 1, CHUNK), bf16(2 * CHUNK, RANK), [coef, xor_step(coef, 1)],
        [ortho], nbytes=CHUNK * 1024, name="join1",
    )

    recv = xor_step(coef, 0)
    squares = local(squares_kernel, f32(8, RANK), [coef], flops=CHUNK * 512, nbytes=400000, name="squares")
    coef, squares = local(
        last_join_kernel, [bf16(HALF, RANK), f32(8, RANK)],
        [coef, recv, squares, pair_z(squares, False), pair_z(squares, True)],
        nbytes=CHUNK * 4096, name="join0",
    )
    opposite = turn_z(squares, (3, 3))
    coef, squares = local(
        unpack_kernel, [f32(LOCAL_COLS, RANK), f32(8, RANK)],
        [coef, xor_fsdp(coef, CORE), squares, xor_fsdp(squares, CORE)],
        flops=3328 * 128, nbytes=20000000, name="unpack",
    )
    new_momentum, done = finish_momentum(coef, ortho, blended)
    moved = local(
        stack_kernel, f32(16, RANK), [opposite, turn_z(squares, (1, -2))], [done],
        nbytes=30000, name="stack",
    )
    squares = [squares, moved, xor_fsdp(moved, CORE)]
    new_weights, new_subspace = finish_weights(squares, coef, ortho, weights)
    return (new_momentum, new_weights, new_subspace)


def solution(mesh):
    placed = (P("fsdp", "tp"), P("fsdp", "tp"), P("fsdp", "tp"), P("tp", None))
    return jax.shard_map(
        on_device,
        mesh=mesh,
        in_specs=placed,
        out_specs=(P("fsdp", "tp"), P("fsdp", "tp"), P("tp", None)),
        check_vma=False,
    )
```

```python
import functools
import math

import jax
import jax.numpy as jnp
from jax import lax
from jax.experimental import pallas as pl
from jax.experimental.pallas import tpu as pltpu
from jax.sharding import PartitionSpec as P

ROWS = 8192
COLS = 26624
RANK = 128

inertia = 0.95
step_size = 0.5
shrinkage = 0.1
epsilon_sq = 1e-06

LOCAL_ROWS = 256
LOCAL_COLS = 3328
TP = 8
FSDP = 32
HALF = LOCAL_COLS // 2
PART = LOCAL_ROWS // 2
CHUNK = HALF // 4
PIECE = HALF // 8
CUT = 40
WIDE = 256
TILES = LOCAL_COLS // WIDE
STRIPS = ((0, 512), (512, 768), (1280, 768), (2048, 768), (2816, 512))

X_ONE, Y_ONE, X_THREE, Y_THREE, CORE = 3, 9, 7, 25, 1
MASKS = ((X_ONE, X_THREE, Y_THREE, Y_ONE), (Y_ONE, Y_THREE, X_THREE, X_ONE))


def team(f):
    return (f % 2 + f // 2 + f // 8) % 2


Z_PAIRS = (
    ((0, 1), (2, 3), (4, 5), (6, 7)),
    ((1, 2), (3, 4), (5, 6), (7, 0)),
    ((2, 5), (1, 6), (4, 7), (3, 0)),
)

VMEM = pltpu.VMEM
VMEM_SPEC = pl.BlockSpec(memory_space=pltpu.VMEM)
HBM_SPEC = pl.BlockSpec(memory_space=pltpu.HBM)
PARAMS = pltpu.CompilerParams(vmem_limit_bytes=24 * 1024 * 1024)
NT = (((1,), (1,)), ((), ()))
TN = (((0,), (0,)), ((), ()))


def f32(*shape):
    return jax.ShapeDtypeStruct(shape, jnp.float32)


def bf16(*shape):
    return jax.ShapeDtypeStruct(shape, jnp.bfloat16)


def cost(flops, nbytes):
    return pl.CostEstimate(flops=flops, bytes_accessed=nbytes, transcendentals=0)

def swap_z(x, step):
    perm = []
    for f in range(FSDP):
        for a, b in Z_PAIRS[step]:
            one, two = f * TP + (a + f % 2) % TP, f * TP + (b + f % 2) % TP
            perm += [(one, two), (two, one)]
    return lax.ppermute(x, ("fsdp", "tp"), perm)


def pair_z(x, cross):
    perm = [
        (f * TP + z, (f ^ (MASKS[team(f)][0] if cross else 0)) * TP + (z ^ 1))
        for f in range(FSDP) for z in range(TP)
    ]
    return lax.ppermute(x, ("fsdp", "tp"), perm)


def turn_z(x, turns):
    perm = [
        ((f ^ 1) * TP + (z + turns[f % 2] * (1 if z % 2 else -1)) % TP, f * TP + z)
        for f in range(FSDP) for z in range(TP)
    ]
    return lax.ppermute(x, ("fsdp", "tp"), perm)


def xor_fsdp(x, mask):
    return lax.ppermute(x, "fsdp", [(i, i ^ mask) for i in range(FSDP)])


def split_cores(x, first, second):
    return lax.ppermute(x, "fsdp", [(f ^ (second if f % 2 else first), f) for f in range(FSDP)])


def xor_step(x, k):
    return lax.ppermute(x, "fsdp", [(i, i ^ MASKS[team(i)][k]) for i in range(FSDP)])


def step_bit(k):
    f = lax.axis_index("fsdp")
    place = jnp.where(team(f) == 0, (f // 2) % 4, f // 8)
    return place // 2 if k else place % 2 ^ place // 2


def project_kernel(m_hbm, g_hbm, s_hbm, b_ref, top_ref, low_ref, m_buf, g_buf, s_buf, sems):
    copies = []
    for i, (start, size) in enumerate(STRIPS):
        cols = pl.ds(start, size)
        copies.append((
            pltpu.make_async_copy(m_hbm.at[:, cols], m_buf.at[:, cols], sems.at[0, i]),
            pltpu.make_async_copy(g_hbm.at[:, cols], g_buf.at[:, cols], sems.at[1, i]),
            pltpu.make_async_copy(s_hbm.at[cols, :], s_buf.at[cols, :], sems.at[2, i]),
        ))
    for trio in copies:
        for copy in trio:
            copy.start()
    for i, trio in enumerate(copies):
        for copy in trio:
            copy.wait()
        start, size = STRIPS[i]
        cols = slice(start, start + size)
        b = (m_buf[:, cols].astype(jnp.float32) + g_buf[:, cols].astype(jnp.float32)).astype(jnp.bfloat16)
        b_ref[:, cols] = b
        part = jnp.dot(b, s_buf[cols, :].astype(jnp.bfloat16), preferred_element_type=jnp.float32)
        for ref, rows in ((top_ref, part[:PART, :]), (low_ref, part[PART:, :])):
            if i == 0:
                ref[...] = rows
            else:
                ref[...] += rows


def project(momentum, gradient, subspace):
    momentum, gradient, subspace = [
        pltpu.with_memory_space_constraint(x, pltpu.HBM) for x in (momentum, gradient, subspace)
    ]
    return pl.pallas_call(
        project_kernel,
        in_specs=[HBM_SPEC] * 3,
        out_specs=[VMEM_SPEC] * 3,
        out_shape=[bf16(LOCAL_ROWS, LOCAL_COLS), f32(PART, RANK), f32(PART, RANK)],
        scratch_shapes=[
            VMEM((LOCAL_ROWS, LOCAL_COLS), jnp.bfloat16),
            VMEM((LOCAL_ROWS, LOCAL_COLS), jnp.bfloat16),
            VMEM((LOCAL_COLS, RANK), jnp.float32),
            pltpu.SemaphoreType.DMA((3, len(STRIPS))),
        ],
        compiler_params=PARAMS,
        cost_estimate=cost(2 * 256 * 3328 * 128, 7000000),
        name="project",
    )(momentum, gradient, subspace)


def local(kernel, out_shape, args, after=(), flops=0, nbytes=0, name=None, scratch=()):
    used = len(args)

    def body(*refs):
        kernel(*refs[:used], *refs[used + len(after):])

    single = not isinstance(out_shape, (list, tuple))
    return pl.pallas_call(
        body,
        in_specs=[VMEM_SPEC] * (used + len(after)),
        out_specs=VMEM_SPEC if single else [VMEM_SPEC] * len(out_shape),
        out_shape=out_shape,
        scratch_shapes=list(scratch),
        compiler_params=PARAMS,
        cost_estimate=cost(flops, nbytes),
        name=name,
    )(*args, *after)


def lift_half(p, b_ref, half, target):
    high = p.astype(jnp.bfloat16)
    low = (p - high.astype(jnp.float32)).astype(jnp.bfloat16)
    split = jnp.concatenate([high, low], axis=1)
    for k in range(HALF // 128):
        cols = pl.ds(pl.multiple_of(half * HALF + k * 128, 128), 128)
        d = lax.dot_general(b_ref[:, cols], split, TN, preferred_element_type=jnp.float32)
        target[k * 128:(k + 1) * 128, :] = d[:, :RANK] + d[:, RANK:]


def lift_send_kernel(top_ref, low_ref, b_ref, send_ref):
    c = team(lax.axis_index("fsdp"))
    p = jnp.concatenate([top_ref[...], low_ref[...]], axis=0)
    lift_half(p, b_ref, 1 - c, send_ref)
    send_ref[HALF:, :] = lax.dot_general(
        p, p, TN, precision=lax.Precision.HIGHEST, preferred_element_type=jnp.float32
    )


def lift_keep_kernel(top_ref, low_ref, b_ref, keep_ref):
    p = jnp.concatenate([top_ref[...], low_ref[...]], axis=0)
    lift_half(p, b_ref, team(lax.axis_index("fsdp")), keep_ref)


def split_kernel(k, n, keep_ref, recv_ref, send_ref, next_ref):
    bit = step_bit(k)
    away = pl.ds(pl.multiple_of((1 - bit) * n, 8), n)
    stay = pl.ds(pl.multiple_of(bit * n, 8), n)
    send_ref[...] = keep_ref[away, :] + recv_ref[away, :]
    next_ref[...] = keep_ref[stay, :] + recv_ref[stay, :]


def split_step(k, n, keep, recv, after=()):
    return local(
        functools.partial(split_kernel, k, n), [f32(n, RANK), f32(n, RANK)], [keep, recv], after,
        flops=n * 256, nbytes=n * 2048, name=f"split{k}",
    )


def add_kernel(a_ref, b_ref, out_ref):
    out_ref[...] = a_ref[...] + b_ref[...]


def gram_pair_kernel(sent_ref, recv_ref, out_ref):
    out_ref[...] = sent_ref[HALF:, :] + recv_ref[HALF:, :]


def gram_four_kernel(a_ref, b_ref, c_ref, d_ref, out_ref):
    out_ref[...] = (a_ref[...] + b_ref[...]) + (c_ref[...] + d_ref[...])


def gram_four(a, b, c, d, after):
    return local(gram_four_kernel, f32(RANK, RANK), [a, b, c, d], after, nbytes=400000, name="gram_four")


def hold_kernel(a_ref, out_ref):
    out_ref[...] = a_ref[...]


def add(a, b, after, name):
    return local(add_kernel, f32(*a.shape), [a, b], after, nbytes=12 * a.size, name=name)


def reciprocal(x):
    r = pl.reciprocal(x, approx=True)
    r = r * (2.0 - x * r)
    return r * (2.0 - x * r)


def unit_scale(rows, lane, sub):
    diagonal = jnp.zeros((8, RANK), jnp.float32)
    for k, row in enumerate(rows):
        diagonal = diagonal + jnp.where(lane == sub + 8 * k, row, 0.0)
    return lax.rsqrt(jnp.sum(diagonal, axis=0, keepdims=True))


def eliminate_kernel(start, stop, in_ref, gram_ref, out_ref):
    groups = RANK // 8
    lane = lax.broadcasted_iota(jnp.int32, (8, RANK), 1)
    sub = lax.broadcasted_iota(jnp.int32, (8, RANK), 0)

    def across(x):
        return jnp.broadcast_to(x, (8, RANK))

    t = [in_ref[8 * r:8 * r + 8, :] for r in range(groups)]
    if start == 0 or stop == RANK:
        gram = [gram_ref[8 * r:8 * r + 8, :] for r in range(groups)]
        scale = unit_scale(gram, lane, sub)
    if start == 0:
        for r in range(groups):
            own = jnp.sum(jnp.where(lane == sub + 8 * r, t[r], 0.0), axis=1, keepdims=True)
            t[r] = t[r] * lax.rsqrt(own) * scale
    for r in range(start // 8, stop // 8):
        cols = {
            k: [across(t[k][:, 8 * r + i:8 * r + i + 1]) for i in range(8)]
            for k in range(r, groups)
        }
        for i in range(0, 8, 2):
            j = 8 * r + i
            p, q = across(cols[r][i][i:i + 1, :]), across(cols[r][i][i + 1:i + 2, :])
            d = across(cols[r][i + 1][i + 1:i + 2, :])
            inv_p = reciprocal(p)
            inv_d = p * reciprocal(p * d - q * q)
            ratio = q * inv_p
            above = {n: across(cols[r][n][i:i + 1, :]) for n in range(i + 2, 8)}
            below = {n: across(cols[r][n][i + 1:i + 2, :]) - ratio * above[n] for n in above}
            at_j, at_next = lane == j, lane == j + 1
            unit_a = jnp.where(at_j, 1.0, across(t[r][i:i + 1, :]))
            new_b = jnp.where(at_j, 0.0, across(t[r][i + 1:i + 2, :])) - ratio * unit_a
            row_a = jnp.where(at_next, 0.0, unit_a)
            row_b = jnp.where(at_next, 1.0, new_b)
            either = at_j | at_next
            for k in range(r, groups):
                first = cols[k][i] * inv_p
                second = (cols[k][i + 1] - first * q) * inv_d
                if k == r:
                    first = jnp.where(sub > i, first, 0.0)
                    second = jnp.where(sub > i + 1, second, 0.0)
                for n in above:
                    cols[k][n] = cols[k][n] - first * above[n] - second * below[n]
                new = jnp.where(either, 0.0, t[k]) - first * row_a - second * row_b
                if k == r:
                    new = jnp.where(sub > i + 1, new, jnp.where(sub == i + 1, new_b, t[k]))
                t[k] = new
    for k in range(groups):
        if stop == RANK:
            row_of = sub + 8 * k
            pivot = jnp.sum(jnp.where(lane == row_of, t[k], 0.0), axis=1, keepdims=True)
            unit = jnp.where(lane < row_of, t[k], jnp.where(lane == row_of, 1.0, 0.0))
            out_ref[8 * k:8 * k + 8, :] = unit * lax.rsqrt(pivot) * scale
        else:
            out_ref[8 * k:8 * k + 8, :] = t[k]


def eliminate(start, stop, state, gram, after=()):
    return local(
        functools.partial(eliminate_kernel, start, stop), f32(RANK, RANK), [state, gram], after,
        flops=4000000, nbytes=(stop - start) * 150000, name=f"eliminate{start}",
    )


def block_kernel(keep_ref, recv_ref, w_ref, out_ref):
    w = w_ref[...].T
    w_high = w.astype(jnp.bfloat16)
    w_low = (w - w_high.astype(jnp.float32)).astype(jnp.bfloat16)
    both = jnp.concatenate([
        jnp.concatenate([w_high, w_low], axis=1),
        jnp.concatenate([w_high, jnp.zeros_like(w_low)], axis=1),
    ], axis=0)
    d = keep_ref[...] + recv_ref[...]
    high = d.astype(jnp.bfloat16)
    low = (d - high.astype(jnp.float32)).astype(jnp.bfloat16)
    out = jnp.dot(jnp.concatenate([high, low], axis=1), both, preferred_element_type=jnp.float32)
    out_ref[...] = (out[:, :RANK] + out[:, RANK:]).astype(jnp.bfloat16)


def ortho_kernel(top_ref, low_ref, w_ref, out_ref):
    p = jnp.concatenate([top_ref[...], low_ref[...]], axis=0)
    out_ref[...] = lax.dot_general(
        p, w_ref[...], NT, precision=lax.Precision.HIGHEST, preferred_element_type=jnp.float32
    ).astype(jnp.bfloat16)


def join_kernel(k, n, mine_ref, recv_ref, out_ref):
    bit = step_bit(k)
    out_ref[pl.ds(pl.multiple_of(bit * n, 16), n), :] = mine_ref[...]
    out_ref[pl.ds(pl.multiple_of((1 - bit) * n, 16), n), :] = recv_ref[...]


def chunk_squares(ref, start):
    rows = ref[start:start + CHUNK, :].astype(jnp.float32)
    return jnp.sum((rows * rows).reshape(CHUNK // 8, 8, RANK), axis=0)


def squares_kernel(ref, out_ref):
    out_ref[...] = chunk_squares(ref, 0) + chunk_squares(ref, CHUNK)


def last_join_kernel(mine_ref, recv_ref, sq_ref, pair_ref, cross_ref, out_ref, sum_ref):
    join_kernel(0, 2 * CHUNK, mine_ref, recv_ref, out_ref)
    other = chunk_squares(recv_ref, 0) + chunk_squares(recv_ref, CHUNK)
    sum_ref[...] = (sq_ref[...] + other) + (pair_ref[...] + cross_ref[...])


def unpack_kernel(own_ref, other_ref, sq_ref, other_sq_ref, coef_ref, sum_ref):
    c = team(lax.axis_index("fsdp"))
    for source, half in ((own_ref, c), (other_ref, 1 - c)):
        for i in range(0, HALF, PIECE):
            coef_ref[pl.ds(pl.multiple_of(half * HALF + i, 16), PIECE), :] = source[i:i + PIECE, :]
    sum_ref[...] = sq_ref[...] + other_sq_ref[...]


def stack_kernel(opposite_ref, next_ref, out_ref):
    out_ref[:8, :] = opposite_ref[...]
    out_ref[8:, :] = next_ref[...]


def momentum_kernel(coef_ref, ortho_ref, b_ref, mom_hbm, done_ref, buf, sems):
    ortho = ortho_ref[...]
    copies = []
    for i in range(TILES):
        cols = slice(i * WIDE, (i + 1) * WIDE)
        feedback = lax.dot_general(
            ortho, coef_ref[cols, :], NT, preferred_element_type=jnp.float32
        )
        buf[:, cols] = (
            b_ref[:, cols].astype(jnp.float32) - (1.0 - inertia) * feedback
        ).astype(jnp.bfloat16)
        at = pl.ds(i * WIDE, WIDE)
        copies.append(pltpu.make_async_copy(buf.at[:, at], mom_hbm.at[:, at], sems.at[i]))
        copies[-1].start()
    for copy in copies:
        copy.wait()
    done_ref[...] = jnp.zeros_like(done_ref)


def finish_momentum(coef, ortho, blended):
    return pl.pallas_call(
        momentum_kernel,
        in_specs=[VMEM_SPEC] * 3,
        out_specs=[HBM_SPEC, VMEM_SPEC],
        out_shape=[bf16(LOCAL_ROWS, LOCAL_COLS), f32(8, RANK)],
        scratch_shapes=[
            VMEM((LOCAL_ROWS, LOCAL_COLS), jnp.bfloat16),
            pltpu.SemaphoreType.DMA((TILES,)),
        ],
        compiler_params=PARAMS,
        cost_estimate=cost(2 * 256 * 3328 * 128, 5000000),
        name="finish_momentum",
    )(coef, ortho, blended)


def weights_kernel(sq_ref, moved_ref, other_ref, coef_ref, ortho_ref, weights_ref, new_hbm, sub_hbm, buf, sub_buf, sems):
    scaling = math.sqrt(ROWS * COLS / RANK)
    moved = moved_ref[...] + other_ref[...]
    squares = (sq_ref[...] + moved[:8, :]) + moved[8:, :]
    norm = 1.0 / jnp.sqrt(jnp.sum(squares, axis=0, keepdims=True) + epsilon_sq)
    ortho = (ortho_ref[...].astype(jnp.float32) * norm).astype(jnp.bfloat16)
    copies = []
    for i in range(4):
        at = pl.ds(i * 2 * CHUNK, 2 * CHUNK)
        sub_buf[at, :] = coef_ref[at, :].astype(jnp.float32) * norm
        copies.append(pltpu.make_async_copy(sub_buf.at[at, :], sub_hbm.at[at, :], sems.at[0, i]))
        copies[-1].start()
    for i, (start, size) in enumerate(STRIPS):
        for first in range(start, start + size, WIDE):
            cols = slice(first, first + WIDE)
            update = lax.dot_general(
                ortho, coef_ref[cols, :], NT, preferred_element_type=jnp.float32
            )
            buf[:, cols] = (
                weights_ref[:, cols].astype(jnp.float32) * (1.0 - step_size * shrinkage)
                - step_size * scaling * update
            ).astype(jnp.bfloat16)
        at = pl.ds(start, size)
        copies.append(pltpu.make_async_copy(buf.at[:, at], new_hbm.at[:, at], sems.at[1, i]))
        copies[-1].start()
    for copy in copies:
        copy.wait()


def finish_weights(squares, coef, ortho, weights):
    return pl.pallas_call(
        weights_kernel,
        in_specs=[VMEM_SPEC] * 6,
        out_specs=[HBM_SPEC] * 2,
        out_shape=[bf16(LOCAL_ROWS, LOCAL_COLS), f32(LOCAL_COLS, RANK)],
        scratch_shapes=[
            VMEM((LOCAL_ROWS, LOCAL_COLS), jnp.bfloat16),
            VMEM((LOCAL_COLS, RANK), jnp.float32),
            pltpu.SemaphoreType.DMA((2, len(STRIPS))),
        ],
        compiler_params=PARAMS,
        cost_estimate=cost(2 * 256 * 3328 * 128, 7000000),
        name="finish_weights",
    )(*squares, coef, ortho, weights)


def on_device(momentum, gradient, weights, subspace):
    blended, *projected = project(momentum, gradient, subspace)
    for step in range(3):
        projected = [rows + swap_z(rows, step) for rows in projected]

    send = local(
        lift_send_kernel, f32(HALF + RANK, RANK), [*projected, blended],
        flops=2 * 256 * 3328 * 128, nbytes=2000000, name="lift_send",
    )
    recv = xor_fsdp(send, CORE)
    keep = local(
        lift_keep_kernel, f32(HALF, RANK), [*projected, blended], [send],
        flops=2 * 256 * 3328 * 128, nbytes=2000000, name="lift_keep",
    )
    n = HALF // 2
    moving, keep = split_step(0, n, keep, recv)
    gram = local(gram_pair_kernel, f32(RANK, RANK), [send, recv], [moving], nbytes=200000, name="gram_pair")
    recv = xor_step(moving, 0)
    split = split_cores(gram, X_THREE, X_THREE ^ Y_THREE ^ CORE)
    gram = gram_four(gram, xor_fsdp(gram, Y_THREE), split, xor_fsdp(split, CORE), [])
    n //= 2
    moving, keep = split_step(1, n, keep, recv, [gram])
    recv = xor_step(moving, 1)
    gram = local(hold_kernel, f32(RANK, RANK), [gram], [moving], nbytes=130000, name="hold")
    split, both = split_cores(gram, X_ONE, Y_ONE), xor_fsdp(gram, X_ONE ^ Y_ONE)
    d = add(keep, recv, [split, both], "first_sum")
    recv = xor_step(d, 2)
    split = local(hold_kernel, f32(RANK, RANK), [split], [d], nbytes=130000, name="hold_split")
    gram = gram_four(gram, both, split, xor_fsdp(split, CORE), [d])
    state = eliminate(0, CUT, gram, gram)
    d = add(d, recv, [state], "second_sum")
    recv = xor_step(d, 3)
    inverse = eliminate(CUT, RANK, state, gram, [d])

    coef = local(
        block_kernel, bf16(CHUNK, RANK), [d, recv, inverse],
        flops=2 * CHUNK * 256 * 256, nbytes=700000, name="block",
    )
    ortho = local(
        ortho_kernel, bf16(LOCAL_ROWS, RANK), [*projected, inverse], [coef],
        flops=6 * 256 * 256 * 128, nbytes=300000, name="ortho",
    )
    coef = local(
        functools.partial(join_kernel, 1, CHUNK), bf16(2 * CHUNK, RANK), [coef, xor_step(coef, 1)],
        [ortho], nbytes=CHUNK * 1024, name="join1",
    )

    recv = xor_step(coef, 0)
    squares = local(squares_kernel, f32(8, RANK), [coef], flops=CHUNK * 512, nbytes=400000, name="squares")
    coef, squares = local(
        last_join_kernel, [bf16(HALF, RANK), f32(8, RANK)],
        [coef, recv, squares, pair_z(squares, False), pair_z(squares, True)],
        nbytes=CHUNK * 4096, name="join0",
    )
    opposite = turn_z(squares, (3, 3))
    coef, squares = local(
        unpack_kernel, [bf16(LOCAL_COLS, RANK), f32(8, RANK)],
        [coef, xor_fsdp(coef, CORE), squares, xor_fsdp(squares, CORE)],
        flops=3328 * 128, nbytes=20000000, name="unpack",
    )
    new_momentum, done = finish_momentum(coef, ortho, blended)
    moved = local(
        stack_kernel, f32(16, RANK), [opposite, turn_z(squares, (1, -2))], [done],
        nbytes=30000, name="stack",
    )
    squares = [squares, moved, xor_fsdp(moved, CORE)]
    new_weights, new_subspace = finish_weights(squares, coef, ortho, weights)
    return (new_momentum, new_weights, new_subspace)


def solution(mesh):
    placed = (P("fsdp", "tp"), P("fsdp", "tp"), P("fsdp", "tp"), P("tp", None))
    return jax.shard_map(
        on_device,
        mesh=mesh,
        in_specs=placed,
        out_specs=(P("fsdp", "tp"), P("fsdp", "tp"), P("tp", None)),
        check_vma=False,
    )
```

```python
import functools
import math

import jax
import jax.numpy as jnp
from jax import lax
from jax.experimental import pallas as pl
from jax.experimental.pallas import tpu as pltpu
from jax.sharding import PartitionSpec as P

ROWS = 8192
COLS = 26624
RANK = 128

inertia = 0.95
step_size = 0.5
shrinkage = 0.1
epsilon_sq = 1e-06

LOCAL_ROWS = 256
LOCAL_COLS = 3328
TP = 8
FSDP = 32
HALF = LOCAL_COLS // 2
PART = LOCAL_ROWS // 2
CHUNK = HALF // 4
PIECE = HALF // 8
CUT = 40
WIDE = 256
TILES = LOCAL_COLS // WIDE
STRIPS = ((0, 512), (512, 768), (1280, 768), (2048, 768), (2816, 256), (3072, 256))

X_ONE, Y_ONE, X_THREE, Y_THREE, CORE = 3, 9, 7, 25, 1
MASKS = ((X_ONE, X_THREE, Y_THREE, Y_ONE), (Y_ONE, Y_THREE, X_THREE, X_ONE))


def team(f):
    return (f % 2 + f // 2 + f // 8) % 2


Z_PAIRS = (
    ((0, 1), (2, 3), (4, 5), (6, 7)),
    ((1, 2), (3, 4), (5, 6), (7, 0)),
    ((2, 5), (1, 6), (4, 7), (3, 0)),
)

VMEM = pltpu.VMEM
VMEM_SPEC = pl.BlockSpec(memory_space=pltpu.VMEM)
HBM_SPEC = pl.BlockSpec(memory_space=pltpu.HBM)
PARAMS = pltpu.CompilerParams(vmem_limit_bytes=24 * 1024 * 1024)
NT = (((1,), (1,)), ((), ()))
TN = (((0,), (0,)), ((), ()))


def f32(*shape):
    return jax.ShapeDtypeStruct(shape, jnp.float32)


def bf16(*shape):
    return jax.ShapeDtypeStruct(shape, jnp.bfloat16)


def cost(flops, nbytes):
    return pl.CostEstimate(flops=flops, bytes_accessed=nbytes, transcendentals=0)

def swap_z(x, step):
    perm = []
    for f in range(FSDP):
        for a, b in Z_PAIRS[step]:
            one, two = f * TP + (a + f % 2) % TP, f * TP + (b + f % 2) % TP
            perm += [(one, two), (two, one)]
    return lax.ppermute(x, ("fsdp", "tp"), perm)


def pair_z(x, cross):
    perm = [
        (f * TP + z, (f ^ (MASKS[team(f)][0] if cross else 0)) * TP + (z ^ 1))
        for f in range(FSDP) for z in range(TP)
    ]
    return lax.ppermute(x, ("fsdp", "tp"), perm)


def turn_z(x, turns):
    perm = [
        ((f ^ 1) * TP + (z + turns[f % 2] * (1 if z % 2 else -1)) % TP, f * TP + z)
        for f in range(FSDP) for z in range(TP)
    ]
    return lax.ppermute(x, ("fsdp", "tp"), perm)


def xor_fsdp(x, mask):
    return lax.ppermute(x, "fsdp", [(i, i ^ mask) for i in range(FSDP)])


def split_cores(x, first, second):
    return lax.ppermute(x, "fsdp", [(f ^ (second if f % 2 else first), f) for f in range(FSDP)])


def xor_step(x, k):
    return lax.ppermute(x, "fsdp", [(i, i ^ MASKS[team(i)][k]) for i in range(FSDP)])


def step_bit(k):
    f = lax.axis_index("fsdp")
    place = jnp.where(team(f) == 0, (f // 2) % 4, f // 8)
    return place // 2 if k else place % 2 ^ place // 2


def project_kernel(m_hbm, g_hbm, s_hbm, b_ref, top_ref, low_ref, m_buf, g_buf, s_buf, sems):
    copies = []
    for i, (start, size) in enumerate(STRIPS):
        cols = pl.ds(start, size)
        copies.append((
            pltpu.make_async_copy(m_hbm.at[:, cols], m_buf.at[:, cols], sems.at[0, i]),
            pltpu.make_async_copy(g_hbm.at[:, cols], g_buf.at[:, cols], sems.at[1, i]),
            pltpu.make_async_copy(s_hbm.at[cols, :], s_buf.at[cols, :], sems.at[2, i]),
        ))
    for trio in copies:
        for copy in trio:
            copy.start()
    for i, trio in enumerate(copies):
        for copy in trio:
            copy.wait()
        start, size = STRIPS[i]
        cols = slice(start, start + size)
        b = (m_buf[:, cols].astype(jnp.float32) + g_buf[:, cols].astype(jnp.float32)).astype(jnp.bfloat16)
        b_ref[:, cols] = b
        part = jnp.dot(b, s_buf[cols, :].astype(jnp.bfloat16), preferred_element_type=jnp.float32)
        for ref, rows in ((top_ref, part[:PART, :]), (low_ref, part[PART:, :])):
            if i == 0:
                ref[...] = rows
            else:
                ref[...] += rows


def project(momentum, gradient, subspace):
    momentum, gradient, subspace = [
        pltpu.with_memory_space_constraint(x, pltpu.HBM) for x in (momentum, gradient, subspace)
    ]
    return pl.pallas_call(
        project_kernel,
        in_specs=[HBM_SPEC] * 3,
        out_specs=[VMEM_SPEC] * 3,
        out_shape=[bf16(LOCAL_ROWS, LOCAL_COLS), f32(PART, RANK), f32(PART, RANK)],
        scratch_shapes=[
            VMEM((LOCAL_ROWS, LOCAL_COLS), jnp.bfloat16),
            VMEM((LOCAL_ROWS, LOCAL_COLS), jnp.bfloat16),
            VMEM((LOCAL_COLS, RANK), jnp.float32),
            pltpu.SemaphoreType.DMA((3, len(STRIPS))),
        ],
        compiler_params=PARAMS,
        cost_estimate=cost(2 * 256 * 3328 * 128, 7000000),
        name="project",
    )(momentum, gradient, subspace)


def local(kernel, out_shape, args, after=(), flops=0, nbytes=0, name=None, scratch=()):
    used = len(args)

    def body(*refs):
        kernel(*refs[:used], *refs[used + len(after):])

    single = not isinstance(out_shape, (list, tuple))
    return pl.pallas_call(
        body,
        in_specs=[VMEM_SPEC] * (used + len(after)),
        out_specs=VMEM_SPEC if single else [VMEM_SPEC] * len(out_shape),
        out_shape=out_shape,
        scratch_shapes=list(scratch),
        compiler_params=PARAMS,
        cost_estimate=cost(flops, nbytes),
        name=name,
    )(*args, *after)


def lift_half(p, b_ref, half, target):
    high = p.astype(jnp.bfloat16)
    low = (p - high.astype(jnp.float32)).astype(jnp.bfloat16)
    split = jnp.concatenate([high, low], axis=1)
    for k in range(HALF // 128):
        cols = pl.ds(pl.multiple_of(half * HALF + k * 128, 128), 128)
        d = lax.dot_general(b_ref[:, cols], split, TN, preferred_element_type=jnp.float32)
        target[k * 128:(k + 1) * 128, :] = d[:, :RANK] + d[:, RANK:]


def lift_send_kernel(top_ref, low_ref, b_ref, send_ref):
    c = team(lax.axis_index("fsdp"))
    p = jnp.concatenate([top_ref[...], low_ref[...]], axis=0)
    lift_half(p, b_ref, 1 - c, send_ref)
    send_ref[HALF:, :] = lax.dot_general(
        p, p, TN, precision=lax.Precision.HIGHEST, preferred_element_type=jnp.float32
    )


def lift_keep_kernel(top_ref, low_ref, b_ref, keep_ref):
    p = jnp.concatenate([top_ref[...], low_ref[...]], axis=0)
    lift_half(p, b_ref, team(lax.axis_index("fsdp")), keep_ref)


def split_kernel(k, n, keep_ref, recv_ref, send_ref, next_ref):
    bit = step_bit(k)
    away = pl.ds(pl.multiple_of((1 - bit) * n, 8), n)
    stay = pl.ds(pl.multiple_of(bit * n, 8), n)
    send_ref[...] = keep_ref[away, :] + recv_ref[away, :]
    next_ref[...] = keep_ref[stay, :] + recv_ref[stay, :]


def split_step(k, n, keep, recv, after=()):
    return local(
        functools.partial(split_kernel, k, n), [f32(n, RANK), f32(n, RANK)], [keep, recv], after,
        flops=n * 256, nbytes=n * 2048, name=f"split{k}",
    )


def add_kernel(a_ref, b_ref, out_ref):
    out_ref[...] = a_ref[...] + b_ref[...]


def gram_pair_kernel(sent_ref, recv_ref, out_ref):
    out_ref[...] = sent_ref[HALF:, :] + recv_ref[HALF:, :]


def gram_four_kernel(a_ref, b_ref, c_ref, d_ref, out_ref):
    out_ref[...] = (a_ref[...] + b_ref[...]) + (c_ref[...] + d_ref[...])


def gram_four(a, b, c, d, after):
    return local(gram_four_kernel, f32(RANK, RANK), [a, b, c, d], after, nbytes=400000, name="gram_four")


def hold_kernel(a_ref, out_ref):
    out_ref[...] = a_ref[...]


def add(a, b, after, name):
    return local(add_kernel, f32(*a.shape), [a, b], after, nbytes=12 * a.size, name=name)


def reciprocal(x):
    r = pl.reciprocal(x, approx=True)
    r = r * (2.0 - x * r)
    return r * (2.0 - x * r)


def unit_scale(rows, lane, sub):
    diagonal = jnp.zeros((8, RANK), jnp.float32)
    for k, row in enumerate(rows):
        diagonal = diagonal + jnp.where(lane == sub + 8 * k, row, 0.0)
    return lax.rsqrt(jnp.sum(diagonal, axis=0, keepdims=True))


def eliminate_kernel(start, stop, in_ref, gram_ref, out_ref, terms_ref=None):
    groups = RANK // 8
    lane = lax.broadcasted_iota(jnp.int32, (8, RANK), 1)
    sub = lax.broadcasted_iota(jnp.int32, (8, RANK), 0)

    def across(x):
        return jnp.broadcast_to(x, (8, RANK))

    t = [in_ref[8 * r:8 * r + 8, :] for r in range(groups)]
    if start == 0 or stop == RANK:
        gram = [gram_ref[8 * r:8 * r + 8, :] for r in range(groups)]
        scale = unit_scale(gram, lane, sub)
    if start == 0:
        for r in range(groups):
            own = jnp.sum(jnp.where(lane == sub + 8 * r, t[r], 0.0), axis=1, keepdims=True)
            t[r] = t[r] * lax.rsqrt(own) * scale
    for r in range(start // 8, stop // 8):
        cols = {
            k: [across(t[k][:, 8 * r + i:8 * r + i + 1]) for i in range(8)]
            for k in range(r, groups)
        }
        for i in range(0, 8, 2):
            j = 8 * r + i
            p, q = across(cols[r][i][i:i + 1, :]), across(cols[r][i][i + 1:i + 2, :])
            d = across(cols[r][i + 1][i + 1:i + 2, :])
            inv_p = reciprocal(p)
            inv_d = p * reciprocal(p * d - q * q)
            ratio = q * inv_p
            above = {n: across(cols[r][n][i:i + 1, :]) for n in range(i + 2, 8)}
            below = {n: across(cols[r][n][i + 1:i + 2, :]) - ratio * above[n] for n in above}
            at_j, at_next = lane == j, lane == j + 1
            unit_a = jnp.where(at_j, 1.0, across(t[r][i:i + 1, :]))
            new_b = jnp.where(at_j, 0.0, across(t[r][i + 1:i + 2, :])) - ratio * unit_a
            row_a = jnp.where(at_next, 0.0, unit_a)
            row_b = jnp.where(at_next, 1.0, new_b)
            either = at_j | at_next
            for k in range(r, groups):
                first = cols[k][i] * inv_p
                second = (cols[k][i + 1] - first * q) * inv_d
                if k == r:
                    first = jnp.where(sub > i, first, 0.0)
                    second = jnp.where(sub > i + 1, second, 0.0)
                for n in above:
                    cols[k][n] = cols[k][n] - first * above[n] - second * below[n]
                new = jnp.where(either, 0.0, t[k]) - first * row_a - second * row_b
                if k == r:
                    new = jnp.where(sub > i + 1, new, jnp.where(sub == i + 1, new_b, t[k]))
                t[k] = new
    for k in range(groups):
        if stop == RANK:
            row_of = sub + 8 * k
            pivot = jnp.sum(jnp.where(lane == row_of, t[k], 0.0), axis=1, keepdims=True)
            unit = jnp.where(lane < row_of, t[k], jnp.where(lane == row_of, 1.0, 0.0))
            out_ref[8 * k:8 * k + 8, :] = unit * lax.rsqrt(pivot) * scale
        else:
            out_ref[8 * k:8 * k + 8, :] = t[k]
    if stop == RANK:
        w = out_ref[...].T
        w_high = w.astype(jnp.bfloat16)
        w_low = (w - w_high.astype(jnp.float32)).astype(jnp.bfloat16)
        terms_ref[:RANK, :] = jnp.concatenate([w_high, w_low], axis=1)
        terms_ref[RANK:, :] = jnp.concatenate([w_high, jnp.zeros_like(w_low)], axis=1)


def eliminate(start, stop, state, gram, after=()):
    shape = f32(RANK, RANK)
    return local(
        functools.partial(eliminate_kernel, start, stop),
        [shape, bf16(2 * RANK, 2 * RANK)] if stop == RANK else shape, [state, gram], after,
        flops=4000000, nbytes=(stop - start) * 150000, name=f"eliminate{start}",
    )


def block_kernel(keep_ref, recv_ref, terms_ref, out_ref):
    d = keep_ref[...] + recv_ref[...]
    high = d.astype(jnp.bfloat16)
    low = (d - high.astype(jnp.float32)).astype(jnp.bfloat16)
    out = jnp.dot(
        jnp.concatenate([high, low], axis=1), terms_ref[...], preferred_element_type=jnp.float32
    )
    out_ref[...] = (out[:, :RANK] + out[:, RANK:]).astype(jnp.bfloat16)


def ortho_kernel(top_ref, low_ref, w_ref, out_ref):
    p = jnp.concatenate([top_ref[...], low_ref[...]], axis=0)
    out_ref[...] = lax.dot_general(
        p, w_ref[...], NT, precision=lax.Precision.HIGHEST, preferred_element_type=jnp.float32
    ).astype(jnp.bfloat16)


def join_kernel(k, n, mine_ref, recv_ref, out_ref):
    bit = step_bit(k)
    out_ref[pl.ds(pl.multiple_of(bit * n, 16), n), :] = mine_ref[...]
    out_ref[pl.ds(pl.multiple_of((1 - bit) * n, 16), n), :] = recv_ref[...]


def chunk_squares(ref, start):
    rows = ref[start:start + CHUNK, :].astype(jnp.float32)
    return jnp.sum((rows * rows).reshape(CHUNK // 8, 8, RANK), axis=0)


def squares_kernel(ref, out_ref):
    out_ref[...] = chunk_squares(ref, 0) + chunk_squares(ref, CHUNK)


def last_join_kernel(mine_ref, recv_ref, sq_ref, pair_ref, cross_ref, out_ref, sum_ref):
    join_kernel(0, 2 * CHUNK, mine_ref, recv_ref, out_ref)
    other = chunk_squares(recv_ref, 0) + chunk_squares(recv_ref, CHUNK)
    sum_ref[...] = (sq_ref[...] + other) + (pair_ref[...] + cross_ref[...])


def unpack_kernel(own_ref, other_ref, coef_ref):
    c = team(lax.axis_index("fsdp"))
    for source, half in ((own_ref, c), (other_ref, 1 - c)):
        for i in range(0, HALF, PIECE):
            rows = source[i:i + PIECE, :].astype(jnp.float32)
            coef_ref[pl.ds(pl.multiple_of(half * HALF + i, 8), PIECE), :] = rows


def stack_kernel(opposite_ref, next_ref, out_ref):
    out_ref[:8, :] = opposite_ref[...]
    out_ref[8:, :] = next_ref[...]


def momentum_kernel(coef_ref, ortho_ref, b_ref, mom_hbm, done_ref, buf, sems):
    ortho = ortho_ref[...]
    copies = []
    for i in range(TILES):
        cols = slice(i * WIDE, (i + 1) * WIDE)
        feedback = lax.dot_general(
            ortho, coef_ref[cols, :].astype(jnp.bfloat16), NT, preferred_element_type=jnp.float32
        )
        buf[:, cols] = (
            b_ref[:, cols].astype(jnp.float32) - (1.0 - inertia) * feedback
        ).astype(jnp.bfloat16)
        at = pl.ds(i * WIDE, WIDE)
        copies.append(pltpu.make_async_copy(buf.at[:, at], mom_hbm.at[:, at], sems.at[i]))
        copies[-1].start()
    for copy in copies:
        copy.wait()
    done_ref[...] = jnp.zeros_like(done_ref)


def finish_momentum(coef, ortho, blended):
    return pl.pallas_call(
        momentum_kernel,
        in_specs=[VMEM_SPEC] * 3,
        out_specs=[HBM_SPEC, VMEM_SPEC],
        out_shape=[bf16(LOCAL_ROWS, LOCAL_COLS), f32(8, RANK)],
        scratch_shapes=[
            VMEM((LOCAL_ROWS, LOCAL_COLS), jnp.bfloat16),
            pltpu.SemaphoreType.DMA((TILES,)),
        ],
        compiler_params=PARAMS,
        cost_estimate=cost(2 * 256 * 3328 * 128, 5000000),
        name="finish_momentum",
    )(coef, ortho, blended)


def weights_kernel(sq_ref, moved_ref, other_ref, coef_ref, ortho_ref, weights_ref, new_hbm, sub_hbm, buf, sub_buf, sems):
    scaling = math.sqrt(ROWS * COLS / RANK)
    moved = moved_ref[...] + other_ref[...]
    squares = (sq_ref[...] + moved[:8, :]) + moved[8:, :]
    norm = 1.0 / jnp.sqrt(jnp.sum(squares, axis=0, keepdims=True) + epsilon_sq)
    ortho = ortho_ref[...]
    copies = []
    for i in range(4):
        at = pl.ds(i * 2 * CHUNK, 2 * CHUNK)
        sub_buf[at, :] = coef_ref[at, :] * norm
        copies.append(pltpu.make_async_copy(sub_buf.at[at, :], sub_hbm.at[at, :], sems.at[0, i]))
        copies[-1].start()
    for i, (start, size) in enumerate(STRIPS):
        for first in range(start, start + size, WIDE):
            cols = slice(first, first + WIDE)
            update = lax.dot_general(
                ortho, sub_buf[cols, :].astype(jnp.bfloat16), NT, preferred_element_type=jnp.float32
            )
            buf[:, cols] = (
                weights_ref[:, cols].astype(jnp.float32) * (1.0 - step_size * shrinkage)
                - step_size * scaling * update
            ).astype(jnp.bfloat16)
        at = pl.ds(start, size)
        copies.append(pltpu.make_async_copy(buf.at[:, at], new_hbm.at[:, at], sems.at[1, i]))
        copies[-1].start()
    for copy in copies:
        copy.wait()


def finish_weights(squares, coef, ortho, weights):
    return pl.pallas_call(
        weights_kernel,
        in_specs=[VMEM_SPEC] * 6,
        out_specs=[HBM_SPEC] * 2,
        out_shape=[bf16(LOCAL_ROWS, LOCAL_COLS), f32(LOCAL_COLS, RANK)],
        scratch_shapes=[
            VMEM((LOCAL_ROWS, LOCAL_COLS), jnp.bfloat16),
            VMEM((LOCAL_COLS, RANK), jnp.float32),
            pltpu.SemaphoreType.DMA((2, len(STRIPS))),
        ],
        compiler_params=PARAMS,
        cost_estimate=cost(2 * 256 * 3328 * 128, 7000000),
        name="finish_weights",
    )(*squares, coef, ortho, weights)


def on_device(momentum, gradient, weights, subspace):
    blended, *projected = project(momentum, gradient, subspace)
    for step in range(3):
        projected = [rows + swap_z(rows, step) for rows in projected]

    send = local(
        lift_send_kernel, f32(HALF + RANK, RANK), [*projected, blended],
        flops=2 * 256 * 3328 * 128, nbytes=2000000, name="lift_send",
    )
    recv = xor_fsdp(send, CORE)
    keep = local(
        lift_keep_kernel, f32(HALF, RANK), [*projected, blended], [send],
        flops=2 * 256 * 3328 * 128, nbytes=2000000, name="lift_keep",
    )
    n = HALF // 2
    moving, keep = split_step(0, n, keep, recv)
    gram = local(gram_pair_kernel, f32(RANK, RANK), [send, recv], [moving], nbytes=200000, name="gram_pair")
    recv = xor_step(moving, 0)
    split = split_cores(gram, X_THREE, X_THREE ^ Y_THREE ^ CORE)
    gram = gram_four(gram, xor_fsdp(gram, Y_THREE), split, xor_fsdp(split, CORE), [])
    n //= 2
    moving, keep = split_step(1, n, keep, recv, [gram])
    recv = xor_step(moving, 1)
    gram = local(hold_kernel, f32(RANK, RANK), [gram], [moving], nbytes=130000, name="hold")
    split, both = split_cores(gram, X_ONE, Y_ONE), xor_fsdp(gram, X_ONE ^ Y_ONE)
    d = add(keep, recv, [split, both], "first_sum")
    recv = xor_step(d, 2)
    split = local(hold_kernel, f32(RANK, RANK), [split], [d], nbytes=130000, name="hold_split")
    gram = gram_four(gram, both, split, xor_fsdp(split, CORE), [d])
    state = eliminate(0, CUT, gram, gram)
    d = add(d, recv, [state], "second_sum")
    recv = xor_step(d, 3)
    inverse, terms = eliminate(CUT, RANK, state, gram, [d])

    coef = local(
        block_kernel, bf16(CHUNK, RANK), [d, recv, terms],
        flops=2 * CHUNK * 256 * 256, nbytes=700000, name="block",
    )
    ortho = local(
        ortho_kernel, bf16(LOCAL_ROWS, RANK), [*projected, inverse], [coef],
        flops=6 * 256 * 256 * 128, nbytes=300000, name="ortho",
    )
    coef = local(
        functools.partial(join_kernel, 1, CHUNK), bf16(2 * CHUNK, RANK), [coef, xor_step(coef, 1)],
        [ortho], nbytes=CHUNK * 1024, name="join1",
    )

    recv = xor_step(coef, 0)
    squares = local(squares_kernel, f32(8, RANK), [coef], flops=CHUNK * 512, nbytes=400000, name="squares")
    coef, squares = local(
        last_join_kernel, [bf16(HALF, RANK), f32(8, RANK)],
        [coef, recv, squares, pair_z(squares, False), pair_z(squares, True)],
        nbytes=CHUNK * 4096, name="join0",
    )
    opposite = turn_z(squares, (3, 3))
    other = xor_fsdp(coef, CORE)
    squares = add(squares, xor_fsdp(squares, CORE), [], "add_core")
    coef = local(
        unpack_kernel, f32(LOCAL_COLS, RANK), [coef, other], [squares],
        flops=3328 * 128, nbytes=2600000, name="unpack",
    )
    new_momentum, done = finish_momentum(coef, ortho, blended)
    moved = local(
        stack_kernel, f32(16, RANK), [opposite, turn_z(squares, (1, -2))], [done],
        nbytes=30000, name="stack",
    )
    squares = [squares, moved, xor_fsdp(moved, CORE)]
    new_weights, new_subspace = finish_weights(squares, coef, ortho, weights)
    return (new_momentum, new_weights, new_subspace)


def solution(mesh):
    placed = (P("fsdp", "tp"), P("fsdp", "tp"), P("fsdp", "tp"), P("tp", None))
    return jax.shard_map(
        on_device,
        mesh=mesh,
        in_specs=placed,
        out_specs=(P("fsdp", "tp"), P("fsdp", "tp"), P("tp", None)),
        check_vma=False,
    )
```

```python
import functools
import math

import jax
import jax.numpy as jnp
from jax import lax
from jax.experimental import pallas as pl
from jax.experimental.pallas import tpu as pltpu
from jax.sharding import PartitionSpec as P

ROWS = 8192
COLS = 26624
RANK = 128

inertia = 0.95
step_size = 0.5
shrinkage = 0.1
epsilon_sq = 1e-06

LOCAL_ROWS = 256
LOCAL_COLS = 3328
TP = 8
FSDP = 32
HALF = LOCAL_COLS // 2
PART = LOCAL_ROWS // 2
CHUNK = HALF // 4
PIECE = HALF // 8
CUT = 40
WIDE = 256
TILES = LOCAL_COLS // WIDE
STRIPS = ((0, 512), (512, 768), (1280, 768), (2048, 768), (2816, 512))

X_ONE, Y_ONE, X_THREE, Y_THREE, CORE = 3, 9, 7, 25, 1
MASKS = ((X_ONE, X_THREE, Y_THREE, Y_ONE), (Y_ONE, Y_THREE, X_THREE, X_ONE))


def team(f):
    return (f % 2 + f // 2 + f // 8) % 2


Z_PAIRS = (
    ((0, 1), (2, 3), (4, 5), (6, 7)),
    ((1, 2), (3, 4), (5, 6), (7, 0)),
    ((2, 5), (1, 6), (4, 7), (3, 0)),
)

VMEM = pltpu.VMEM
VMEM_SPEC = pl.BlockSpec(memory_space=pltpu.VMEM)
HBM_SPEC = pl.BlockSpec(memory_space=pltpu.HBM)
PARAMS = pltpu.CompilerParams(vmem_limit_bytes=24 * 1024 * 1024)
NT = (((1,), (1,)), ((), ()))
TN = (((0,), (0,)), ((), ()))


def f32(*shape):
    return jax.ShapeDtypeStruct(shape, jnp.float32)


def bf16(*shape):
    return jax.ShapeDtypeStruct(shape, jnp.bfloat16)


def cost(flops, nbytes):
    return pl.CostEstimate(flops=flops, bytes_accessed=nbytes, transcendentals=0)

def swap_z(x, step):
    perm = []
    for f in range(FSDP):
        for a, b in Z_PAIRS[step]:
            one, two = f * TP + (a + f % 2) % TP, f * TP + (b + f % 2) % TP
            perm += [(one, two), (two, one)]
    return lax.ppermute(x, ("fsdp", "tp"), perm)


def pair_z(x, cross):
    perm = [
        (f * TP + z, (f ^ (MASKS[team(f)][0] if cross else 0)) * TP + (z ^ 1))
        for f in range(FSDP) for z in range(TP)
    ]
    return lax.ppermute(x, ("fsdp", "tp"), perm)


def turn_z(x, turns):
    perm = [
        ((f ^ 1) * TP + (z + turns[f % 2] * (1 if z % 2 else -1)) % TP, f * TP + z)
        for f in range(FSDP) for z in range(TP)
    ]
    return lax.ppermute(x, ("fsdp", "tp"), perm)


def xor_fsdp(x, mask):
    return lax.ppermute(x, "fsdp", [(i, i ^ mask) for i in range(FSDP)])


def split_cores(x, first, second):
    return lax.ppermute(x, "fsdp", [(f ^ (second if f % 2 else first), f) for f in range(FSDP)])


def xor_step(x, k):
    return lax.ppermute(x, "fsdp", [(i, i ^ MASKS[team(i)][k]) for i in range(FSDP)])


def step_bit(k):
    f = lax.axis_index("fsdp")
    place = jnp.where(team(f) == 0, (f // 2) % 4, f // 8)
    return place // 2 if k else place % 2 ^ place // 2


def project_kernel(m_hbm, g_hbm, s_hbm, b_ref, top_ref, low_ref, m_buf, g_buf, s_buf, sems):
    copies = []
    for i, (start, size) in enumerate(STRIPS):
        cols = pl.ds(start, size)
        copies.append((
            pltpu.make_async_copy(m_hbm.at[:, cols], m_buf.at[:, cols], sems.at[0, i]),
            pltpu.make_async_copy(g_hbm.at[:, cols], g_buf.at[:, cols], sems.at[1, i]),
            pltpu.make_async_copy(s_hbm.at[cols, :], s_buf.at[cols, :], sems.at[2, i]),
        ))
    for trio in copies:
        for copy in trio:
            copy.start()
    for i, trio in enumerate(copies):
        for copy in trio:
            copy.wait()
        start, size = STRIPS[i]
        cols = slice(start, start + size)
        b = (m_buf[:, cols].astype(jnp.float32) + g_buf[:, cols].astype(jnp.float32)).astype(jnp.bfloat16)
        b_ref[:, cols] = b
        part = jnp.dot(b, s_buf[cols, :].astype(jnp.bfloat16), preferred_element_type=jnp.float32)
        for ref, rows in ((top_ref, part[:PART, :]), (low_ref, part[PART:, :])):
            if i == 0:
                ref[...] = rows
            else:
                ref[...] += rows


def project(momentum, gradient, subspace):
    momentum, gradient, subspace = [
        pltpu.with_memory_space_constraint(x, pltpu.HBM) for x in (momentum, gradient, subspace)
    ]
    return pl.pallas_call(
        project_kernel,
        in_specs=[HBM_SPEC] * 3,
        out_specs=[VMEM_SPEC] * 3,
        out_shape=[bf16(LOCAL_ROWS, LOCAL_COLS), f32(PART, RANK), f32(PART, RANK)],
        scratch_shapes=[
            VMEM((LOCAL_ROWS, LOCAL_COLS), jnp.bfloat16),
            VMEM((LOCAL_ROWS, LOCAL_COLS), jnp.bfloat16),
            VMEM((LOCAL_COLS, RANK), jnp.float32),
            pltpu.SemaphoreType.DMA((3, len(STRIPS))),
        ],
        compiler_params=PARAMS,
        cost_estimate=cost(2 * 256 * 3328 * 128, 7000000),
        name="project",
    )(momentum, gradient, subspace)


def local(kernel, out_shape, args, after=(), flops=0, nbytes=0, name=None, scratch=()):
    used = len(args)

    def body(*refs):
        kernel(*refs[:used], *refs[used + len(after):])

    single = not isinstance(out_shape, (list, tuple))
    return pl.pallas_call(
        body,
        in_specs=[VMEM_SPEC] * (used + len(after)),
        out_specs=VMEM_SPEC if single else [VMEM_SPEC] * len(out_shape),
        out_shape=out_shape,
        scratch_shapes=list(scratch),
        compiler_params=PARAMS,
        cost_estimate=cost(flops, nbytes),
        name=name,
    )(*args, *after)


def lift_half(p, b_ref, half, target):
    high = p.astype(jnp.bfloat16)
    low = (p - high.astype(jnp.float32)).astype(jnp.bfloat16)
    split = jnp.concatenate([high, low], axis=1)
    for k in range(HALF // 128):
        cols = pl.ds(pl.multiple_of(half * HALF + k * 128, 128), 128)
        d = lax.dot_general(b_ref[:, cols], split, TN, preferred_element_type=jnp.float32)
        target[k * 128:(k + 1) * 128, :] = d[:, :RANK] + d[:, RANK:]


def lift_send_kernel(top_ref, low_ref, b_ref, send_ref):
    c = team(lax.axis_index("fsdp"))
    p = jnp.concatenate([top_ref[...], low_ref[...]], axis=0)
    lift_half(p, b_ref, 1 - c, send_ref)
    send_ref[HALF:, :] = lax.dot_general(
        p, p, TN, precision=lax.Precision.HIGHEST, preferred_element_type=jnp.float32
    )


def lift_keep_kernel(top_ref, low_ref, b_ref, keep_ref):
    p = jnp.concatenate([top_ref[...], low_ref[...]], axis=0)
    lift_half(p, b_ref, team(lax.axis_index("fsdp")), keep_ref)


def split_kernel(k, n, keep_ref, recv_ref, send_ref, next_ref):
    bit = step_bit(k)
    away = pl.ds(pl.multiple_of((1 - bit) * n, 8), n)
    stay = pl.ds(pl.multiple_of(bit * n, 8), n)
    send_ref[...] = keep_ref[away, :] + recv_ref[away, :]
    next_ref[...] = keep_ref[stay, :] + recv_ref[stay, :]


def split_step(k, n, keep, recv, after=()):
    return local(
        functools.partial(split_kernel, k, n), [f32(n, RANK), f32(n, RANK)], [keep, recv], after,
        flops=n * 256, nbytes=n * 2048, name=f"split{k}",
    )


def add_kernel(a_ref, b_ref, out_ref):
    out_ref[...] = a_ref[...] + b_ref[...]


def gram_pair_kernel(sent_ref, recv_ref, out_ref):
    out_ref[...] = sent_ref[HALF:, :] + recv_ref[HALF:, :]


def gram_four_kernel(a_ref, b_ref, c_ref, d_ref, out_ref):
    out_ref[...] = (a_ref[...] + b_ref[...]) + (c_ref[...] + d_ref[...])


def gram_four(a, b, c, d, after):
    return local(gram_four_kernel, f32(RANK, RANK), [a, b, c, d], after, nbytes=400000, name="gram_four")


def hold_kernel(a_ref, out_ref):
    out_ref[...] = a_ref[...]


def add(a, b, after, name):
    return local(add_kernel, f32(*a.shape), [a, b], after, nbytes=12 * a.size, name=name)


def reciprocal(x):
    r = pl.reciprocal(x, approx=True)
    r = r * (2.0 - x * r)
    return r * (2.0 - x * r)


def unit_scale(rows, lane, sub):
    diagonal = jnp.zeros((8, RANK), jnp.float32)
    for k, row in enumerate(rows):
        diagonal = diagonal + jnp.where(lane == sub + 8 * k, row, 0.0)
    return lax.rsqrt(jnp.sum(diagonal, axis=0, keepdims=True))


def eliminate_kernel(start, stop, in_ref, gram_ref, out_ref, terms_ref=None):
    groups = RANK // 8
    lane = lax.broadcasted_iota(jnp.int32, (8, RANK), 1)
    sub = lax.broadcasted_iota(jnp.int32, (8, RANK), 0)

    def across(x):
        return jnp.broadcast_to(x, (8, RANK))

    t = [in_ref[8 * r:8 * r + 8, :] for r in range(groups)]
    if start == 0 or stop == RANK:
        gram = [gram_ref[8 * r:8 * r + 8, :] for r in range(groups)]
        scale = unit_scale(gram, lane, sub)
    if start == 0:
        for r in range(groups):
            own = jnp.sum(jnp.where(lane == sub + 8 * r, t[r], 0.0), axis=1, keepdims=True)
            t[r] = t[r] * lax.rsqrt(own) * scale
    for r in range(start // 8, stop // 8):
        cols = {
            k: [across(t[k][:, 8 * r + i:8 * r + i + 1]) for i in range(8)]
            for k in range(r, groups)
        }
        for i in range(0, 8, 2):
            j = 8 * r + i
            p, q = across(cols[r][i][i:i + 1, :]), across(cols[r][i][i + 1:i + 2, :])
            d = across(cols[r][i + 1][i + 1:i + 2, :])
            inv_p = reciprocal(p)
            inv_d = p * reciprocal(p * d - q * q)
            ratio = q * inv_p
            above = {n: across(cols[r][n][i:i + 1, :]) for n in range(i + 2, 8)}
            below = {n: across(cols[r][n][i + 1:i + 2, :]) - ratio * above[n] for n in above}
            at_j, at_next = lane == j, lane == j + 1
            unit_a = jnp.where(at_j, 1.0, across(t[r][i:i + 1, :]))
            new_b = jnp.where(at_j, 0.0, across(t[r][i + 1:i + 2, :])) - ratio * unit_a
            row_a = jnp.where(at_next, 0.0, unit_a)
            row_b = jnp.where(at_next, 1.0, new_b)
            either = at_j | at_next
            for k in range(r, groups):
                first = cols[k][i] * inv_p
                second = (cols[k][i + 1] - first * q) * inv_d
                if k == r:
                    first = jnp.where(sub > i, first, 0.0)
                    second = jnp.where(sub > i + 1, second, 0.0)
                for n in above:
                    cols[k][n] = cols[k][n] - first * above[n] - second * below[n]
                new = jnp.where(either, 0.0, t[k]) - first * row_a - second * row_b
                if k == r:
                    new = jnp.where(sub > i + 1, new, jnp.where(sub == i + 1, new_b, t[k]))
                t[k] = new
    for k in range(groups):
        if stop == RANK:
            row_of = sub + 8 * k
            pivot = jnp.sum(jnp.where(lane == row_of, t[k], 0.0), axis=1, keepdims=True)
            unit = jnp.where(lane < row_of, t[k], jnp.where(lane == row_of, 1.0, 0.0))
            out_ref[8 * k:8 * k + 8, :] = unit * lax.rsqrt(pivot) * scale
        else:
            out_ref[8 * k:8 * k + 8, :] = t[k]
    if stop == RANK:
        w = out_ref[...].T
        w_high = w.astype(jnp.bfloat16)
        w_low = (w - w_high.astype(jnp.float32)).astype(jnp.bfloat16)
        terms_ref[:RANK, :] = jnp.concatenate([w_high, w_low], axis=1)
        terms_ref[RANK:, :] = jnp.concatenate([w_high, jnp.zeros_like(w_low)], axis=1)


def eliminate(start, stop, state, gram, after=()):
    shape = f32(RANK, RANK)
    return local(
        functools.partial(eliminate_kernel, start, stop),
        [shape, bf16(2 * RANK, 2 * RANK)] if stop == RANK else shape, [state, gram], after,
        flops=4000000, nbytes=(stop - start) * 150000, name=f"eliminate{start}",
    )


def block_kernel(keep_ref, recv_ref, terms_ref, out_ref):
    d = keep_ref[...] + recv_ref[...]
    high = d.astype(jnp.bfloat16)
    low = (d - high.astype(jnp.float32)).astype(jnp.bfloat16)
    out = jnp.dot(
        jnp.concatenate([high, low], axis=1), terms_ref[...], preferred_element_type=jnp.float32
    )
    out_ref[...] = (out[:, :RANK] + out[:, RANK:]).astype(jnp.bfloat16)


def ortho_kernel(top_ref, low_ref, w_ref, out_ref):
    p = jnp.concatenate([top_ref[...], low_ref[...]], axis=0)
    out_ref[...] = lax.dot_general(
        p, w_ref[...], NT, precision=lax.Precision.HIGHEST, preferred_element_type=jnp.float32
    ).astype(jnp.bfloat16)


def join_kernel(k, n, mine_ref, recv_ref, out_ref):
    bit = step_bit(k)
    out_ref[pl.ds(pl.multiple_of(bit * n, 16), n), :] = mine_ref[...]
    out_ref[pl.ds(pl.multiple_of((1 - bit) * n, 16), n), :] = recv_ref[...]


def chunk_squares(ref, start):
    rows = ref[start:start + CHUNK, :].astype(jnp.float32)
    return jnp.sum((rows * rows).reshape(CHUNK // 8, 8, RANK), axis=0)


def squares_kernel(ref, out_ref):
    out_ref[...] = chunk_squares(ref, 0) + chunk_squares(ref, CHUNK)


def last_join_kernel(mine_ref, recv_ref, sq_ref, pair_ref, cross_ref, out_ref, sum_ref):
    join_kernel(0, 2 * CHUNK, mine_ref, recv_ref, out_ref)
    other = chunk_squares(recv_ref, 0) + chunk_squares(recv_ref, CHUNK)
    sum_ref[...] = (sq_ref[...] + other) + (pair_ref[...] + cross_ref[...])


def unpack_kernel(own_ref, other_ref, coef_ref):
    c = team(lax.axis_index("fsdp"))
    for source, half in ((own_ref, c), (other_ref, 1 - c)):
        for i in range(0, HALF, PIECE):
            rows = source[i:i + PIECE, :].astype(jnp.float32)
            coef_ref[pl.ds(pl.multiple_of(half * HALF + i, 8), PIECE), :] = rows


def stack_kernel(opposite_ref, next_ref, out_ref):
    out_ref[:8, :] = opposite_ref[...]
    out_ref[8:, :] = next_ref[...]


def momentum_kernel(coef_ref, ortho_ref, b_ref, mom_hbm, done_ref, buf, sems):
    ortho = ortho_ref[...]
    copies = []
    for i in range(TILES):
        cols = slice(i * WIDE, (i + 1) * WIDE)
        feedback = lax.dot_general(
            ortho, coef_ref[cols, :].astype(jnp.bfloat16), NT, preferred_element_type=jnp.float32
        )
        buf[:, cols] = (
            b_ref[:, cols].astype(jnp.float32) - (1.0 - inertia) * feedback
        ).astype(jnp.bfloat16)
        at = pl.ds(i * WIDE, WIDE)
        copies.append(pltpu.make_async_copy(buf.at[:, at], mom_hbm.at[:, at], sems.at[i]))
        copies[-1].start()
    for copy in copies:
        copy.wait()
    done_ref[...] = jnp.zeros_like(done_ref)


def finish_momentum(coef, ortho, blended):
    return pl.pallas_call(
        momentum_kernel,
        in_specs=[VMEM_SPEC] * 3,
        out_specs=[HBM_SPEC, VMEM_SPEC],
        out_shape=[bf16(LOCAL_ROWS, LOCAL_COLS), f32(8, RANK)],
        scratch_shapes=[
            VMEM((LOCAL_ROWS, LOCAL_COLS), jnp.bfloat16),
            pltpu.SemaphoreType.DMA((TILES,)),
        ],
        compiler_params=PARAMS,
        cost_estimate=cost(2 * 256 * 3328 * 128, 5000000),
        name="finish_momentum",
    )(coef, ortho, blended)


def weights_kernel(sq_ref, moved_ref, other_ref, coef_ref, ortho_ref, weights_ref, new_hbm, sub_hbm, buf, sub_buf, sems):
    scaling = math.sqrt(ROWS * COLS / RANK)
    moved = moved_ref[...] + other_ref[...]
    squares = (sq_ref[...] + moved[:8, :]) + moved[8:, :]
    norm = 1.0 / jnp.sqrt(jnp.sum(squares, axis=0, keepdims=True) + epsilon_sq)
    ortho = ortho_ref[...]
    copies = []
    for i in range(4):
        at = pl.ds(i * 2 * CHUNK, 2 * CHUNK)
        sub_buf[at, :] = coef_ref[at, :] * norm
        copies.append(pltpu.make_async_copy(sub_buf.at[at, :], sub_hbm.at[at, :], sems.at[0, i]))
        copies[-1].start()
    for i, (start, size) in enumerate(STRIPS):
        for first in range(start, start + size, WIDE):
            cols = slice(first, first + WIDE)
            update = lax.dot_general(
                ortho, sub_buf[cols, :].astype(jnp.bfloat16), NT, preferred_element_type=jnp.float32
            )
            buf[:, cols] = (
                weights_ref[:, cols].astype(jnp.float32) * (1.0 - step_size * shrinkage)
                - step_size * scaling * update
            ).astype(jnp.bfloat16)
        at = pl.ds(start, size)
        copies.append(pltpu.make_async_copy(buf.at[:, at], new_hbm.at[:, at], sems.at[1, i]))
        copies[-1].start()
    for copy in copies:
        copy.wait()


def finish_weights(squares, coef, ortho, weights):
    return pl.pallas_call(
        weights_kernel,
        in_specs=[VMEM_SPEC] * 6,
        out_specs=[HBM_SPEC] * 2,
        out_shape=[bf16(LOCAL_ROWS, LOCAL_COLS), f32(LOCAL_COLS, RANK)],
        scratch_shapes=[
            VMEM((LOCAL_ROWS, LOCAL_COLS), jnp.bfloat16),
            VMEM((LOCAL_COLS, RANK), jnp.float32),
            pltpu.SemaphoreType.DMA((2, len(STRIPS))),
        ],
        compiler_params=PARAMS,
        cost_estimate=cost(2 * 256 * 3328 * 128, 7000000),
        name="finish_weights",
    )(*squares, coef, ortho, weights)


def on_device(momentum, gradient, weights, subspace):
    blended, *projected = project(momentum, gradient, subspace)
    for step in range(3):
        projected = [rows + swap_z(rows, step) for rows in projected]

    send = local(
        lift_send_kernel, f32(HALF + RANK, RANK), [*projected, blended],
        flops=2 * 256 * 3328 * 128, nbytes=2000000, name="lift_send",
    )
    recv = xor_fsdp(send, CORE)
    keep = local(
        lift_keep_kernel, f32(HALF, RANK), [*projected, blended], [send],
        flops=2 * 256 * 3328 * 128, nbytes=2000000, name="lift_keep",
    )
    n = HALF // 2
    moving, keep = split_step(0, n, keep, recv)
    gram = local(gram_pair_kernel, f32(RANK, RANK), [send, recv], [moving], nbytes=200000, name="gram_pair")
    recv = xor_step(moving, 0)
    split = split_cores(gram, X_THREE, X_THREE ^ Y_THREE ^ CORE)
    gram = gram_four(gram, xor_fsdp(gram, Y_THREE), split, xor_fsdp(split, CORE), [])
    n //= 2
    moving, keep = split_step(1, n, keep, recv, [gram])
    recv = xor_step(moving, 1)
    gram = local(hold_kernel, f32(RANK, RANK), [gram], [moving], nbytes=130000, name="hold")
    split, both = split_cores(gram, X_ONE, Y_ONE), xor_fsdp(gram, X_ONE ^ Y_ONE)
    d = add(keep, recv, [split, both], "first_sum")
    recv = xor_step(d, 2)
    split = local(hold_kernel, f32(RANK, RANK), [split], [d], nbytes=130000, name="hold_split")
    gram = gram_four(gram, both, split, xor_fsdp(split, CORE), [d])
    state = eliminate(0, CUT, gram, gram)
    d = add(d, recv, [state], "second_sum")
    recv = xor_step(d, 3)
    inverse, terms = eliminate(CUT, RANK, state, gram, [d])

    coef = local(
        block_kernel, bf16(CHUNK, RANK), [d, recv, terms],
        flops=2 * CHUNK * 256 * 256, nbytes=700000, name="block",
    )
    ortho = local(
        ortho_kernel, bf16(LOCAL_ROWS, RANK), [*projected, inverse], [coef],
        flops=6 * 256 * 256 * 128, nbytes=300000, name="ortho",
    )
    coef = local(
        functools.partial(join_kernel, 1, CHUNK), bf16(2 * CHUNK, RANK), [coef, xor_step(coef, 1)],
        [ortho], nbytes=CHUNK * 1024, name="join1",
    )

    recv = xor_step(coef, 0)
    squares = local(squares_kernel, f32(8, RANK), [coef], flops=CHUNK * 512, nbytes=400000, name="squares")
    coef, squares = local(
        last_join_kernel, [bf16(HALF, RANK), f32(8, RANK)],
        [coef, recv, squares, pair_z(squares, False), pair_z(squares, True)],
        nbytes=CHUNK * 4096, name="join0",
    )
    opposite = turn_z(squares, (3, 3))
    other = xor_fsdp(coef, CORE)
    squares = add(squares, xor_fsdp(squares, CORE), [], "add_core")
    coef = local(
        unpack_kernel, f32(LOCAL_COLS, RANK), [coef, other], [squares],
        flops=3328 * 128, nbytes=2600000, name="unpack",
    )
    new_momentum, done = finish_momentum(coef, ortho, blended)
    moved = local(
        stack_kernel, f32(16, RANK), [opposite, turn_z(squares, (1, -2))], [done],
        nbytes=30000, name="stack",
    )
    squares = [squares, moved, xor_fsdp(moved, CORE)]
    new_weights, new_subspace = finish_weights(squares, coef, ortho, weights)
    return (new_momentum, new_weights, new_subspace)


def solution(mesh):
    placed = (P("fsdp", "tp"), P("fsdp", "tp"), P("fsdp", "tp"), P("tp", None))
    return jax.shard_map(
        on_device,
        mesh=mesh,
        in_specs=placed,
        out_specs=(P("fsdp", "tp"), P("fsdp", "tp"), P("tp", None)),
        check_vma=False,
    )
```
